128 devices in a mesh: rep: 32 (over y, z_hi, x), shard: 4 (over z_lo, core).
Axes of the slice: x: 4, y: 4, z: 4 (z_hi: 2, z_lo: 2; z = z_hi * 2 + z_lo), core: 2. Of those that a mesh axis runs over, the one named last changes fastest.
Arguments:
- block_input: bfloat16 [16384, 768], P(('rep', 'shard')), may hold values from -6 to 6
- cotangent: float32 [16384, 768], P(('rep', 'shard')), may hold values from -6 to 6
- lengths: int32 [32], P('rep'), may hold values from 257 to 512, as said below
- block_order: int32 [32, 4], P('rep'), may hold values from 0 to 3, as said below
- w_qkv: float32 [768, 3, 768], P(None, None, 'shard'), may hold values from -0.21875 to 0.21875
- w_out: float32 [768, 768], P('shard'), may hold values from -2.5 to 2.5
- w_fc: float32 [768, 3072], P(None, 'shard'), may hold values from -0.21875 to 0.21875
- w_proj: float32 [3072, 768], P('shard'), may hold values from -0.109375 to 0.109375
- mom_qkv: float32 [768, 3, 768], P(None, None, 'shard')
- mom_out: float32 [768, 768], P('shard')
- mom_fc: float32 [768, 3072], P(None, 'shard')
- mom_proj: float32 [3072, 768], P('shard')
- small_params: float32 [12, 768], replicated, as said below
- small_first: float32 [12, 768], replicated, may hold values from -80 to 80
- small_second: float32 [12, 768], replicated, may hold values from 8.192 to 65.536
Outputs:
- block_output: bfloat16 [16384, 768], P(('rep', 'shard'))
- input_grad: float32 [16384, 768], P(('rep', 'shard'))
- grad_qkv: float32 [768, 3, 768], P(None, None, 'shard')
- grad_out: float32 [768, 768], P('shard')
- grad_fc: float32 [768, 3072], P(None, 'shard')
- grad_proj: float32 [3072, 768], P('shard')
- grad_small: float32 [12, 768], replicated
- new_qkv: float32 [768, 3, 768], P(None, None, 'shard')
- new_out: float32 [768, 768], P('shard')
- new_fc: float32 [768, 3072], P(None, 'shard')
- new_proj: float32 [3072, 768], P('shard')
- next_mom_qkv: float32 [768, 3, 768], P(None, None, 'shard')
- next_mom_out: float32 [768, 768], P('shard')
- next_mom_fc: float32 [768, 3072], P(None, 'shard')
- next_mom_proj: float32 [3072, 768], P('shard')
- next_first: float32 [12, 768], replicated
- next_second: float32 [12, 768], replicated
- next_small: float32 [12, 768], replicated
- grad_last_bias: float32 [768], replicated
The draws below stay inside these ranges and needn't reach their ends.
Inputs may be any that keep to these rules, and one draw needn't show every extreme that they name: `lengths`: each group's sequence length; in every draw one group's is 512 and another's is 257. `block_order`: each row names every block number once; slot 0 holds block 0 and the last slot holds block 1. `small_params`: rows 0 and 2 are positive.
All inputs are finite; a program needn't handle non-finite values.
Results may differ from the reference program's by a relative error of at most 0.023.
Values may be sent and summed in bfloat16 or wider, within the bound.
A program may use at most 256 MiB of HBM per device.

```python
import math
import jax
import jax.numpy as jnp
from jax import lax

D = 768
H = 12
HD = 64
FF = 3072
BLOCK = 128
NS_STEPS = 4
STEP = 10
SLOTS = 4
GROUP = 512
GROUPS = 32
TOKENS = 16384


def draw_lengths(key, part):
    key = jax.random.fold_in(key, 1)
    length_key, pick_key = jax.random.split(key)
    drawn = jax.random.randint(length_key, (GROUPS,), GROUP // 2 + 1, GROUP + 1)
    chosen = jax.random.permutation(pick_key, GROUPS)
    drawn = drawn.at[chosen[0]].set(GROUP)
    drawn = drawn.at[chosen[1]].set(GROUP // 2 + 1)
    return drawn.astype(jnp.int32)


def draw_block_order(key, part):
    key = jax.random.fold_in(key, 2)
    row_keys = jax.random.split(key, GROUPS)

    def one_row(row_key):
        middle = (jax.random.permutation(row_key, SLOTS - 2) + 2).astype(jnp.int32)
        return jnp.concatenate([jnp.zeros((1,), jnp.int32), middle, jnp.ones((1,), jnp.int32)])
    return jax.vmap(one_row)(row_keys)


def textured(key, rows, cols, scale):
    base_key = jax.random.fold_in(key, 0)
    row_key = jax.random.fold_in(key, 2)
    col_key = jax.random.fold_in(key, 3)
    base = jax.random.normal(base_key, (rows, cols), jnp.float32)
    row_scale = jnp.exp(jax.random.uniform(row_key, (rows, 1), jnp.float32, -1.2, 1.2))
    col_scale = jnp.exp(jax.random.uniform(col_key, (1, cols), jnp.float32, -1.2, 1.2))
    return scale * base * row_scale * col_scale


def draw_mom_qkv(key, part):
    key = jax.random.fold_in(key, 3)
    return textured(key, D, 3 * D, 2.0 * TOKENS ** 0.5).reshape(D, 3, D)


def draw_mom_out(key, part):
    key = jax.random.fold_in(key, 4)
    return textured(key, D, D, 0.1 * TOKENS ** 0.5)


def draw_mom_fc(key, part):
    key = jax.random.fold_in(key, 5)
    return textured(key, D, FF, 0.25 * TOKENS ** 0.5)


def draw_mom_proj(key, part):
    key = jax.random.fold_in(key, 6)
    return textured(key, FF, D, 0.5 * TOKENS ** 0.5)


def draw_small_params(key, part):
    key = jax.random.fold_in(key, 7)
    gain_key, shift_key = jax.random.split(key)
    gains = jnp.exp(jax.random.uniform(gain_key, (12, D), jnp.float32, -0.5, 0.5))
    shifts = 0.3 * jnp.clip(jax.random.normal(shift_key, (12, D), jnp.float32), -3.0, 3.0)
    row_index = jnp.arange(12)[:, None]
    return jnp.where((row_index == 0) | (row_index == 2), gains, shifts)


def block_scale(stream_key, extent, pieces, smallest, top_value):
    loudness, own = 1.0, jax.random.fold_in(stream_key, 6)
    for position, parts in pieces:
        steps = jnp.exp(jax.random.uniform(jax.random.fold_in(own, position), (parts,), jnp.float32, smallest / len(pieces), top_value / len(pieces)))
        loudness = loudness * jnp.repeat(steps, extent[position] // parts).reshape([-1 if axis == position else 1 for axis in range(len(extent))])
    return loudness


def scatter_about(stream_key, extent, deviation, bound, cuts=(), kind=jnp.bfloat16):
    array = jax.random.normal(stream_key, extent, jnp.float32) * deviation
    if len(cuts) > 0:
        array = block_scale(stream_key, extent, cuts, -0.22, 0.18) * array
    return jnp.clip(array, min=-bound, max=bound).astype(kind)


def setup_inputs(seed: int = 0) -> dict:
    key_list = jax.random.split(jax.random.key(seed), 16)
    block_input = scatter_about(key_list[0], (TOKENS, D), 1.0, 6.0, ((0, 128),))
    cotangent = scatter_about(key_list[1], (TOKENS, D), 1.0, 6.0, ((0, 128),), jnp.float32)
    lengths = draw_lengths(jax.random.fold_in(key_list[15], 71), 0)
    block_order = draw_block_order(jax.random.fold_in(key_list[15], 71), 0)
    w_qkv = scatter_about(key_list[4], (D, 3, D), D ** -0.5, 0.21875, ((2, 4),), jnp.float32)
    w_out = scatter_about(key_list[5], (D, D), (max(D * 4 // GROUP, 2)) ** -0.5, 2.5, ((0, 4),), jnp.float32)
    w_fc = scatter_about(key_list[6], (D, FF), D ** -0.5, 0.21875, ((1, 4),), jnp.float32)
    w_proj = scatter_about(key_list[7], (FF, D), FF ** -0.5, 0.109375, ((0, 4),), jnp.float32)
    mom_qkv = draw_mom_qkv(jax.random.fold_in(key_list[15], 71), 0)
    mom_out = draw_mom_out(jax.random.fold_in(key_list[15], 71), 0)
    mom_fc = draw_mom_fc(jax.random.fold_in(key_list[15], 71), 0)
    mom_proj = draw_mom_proj(jax.random.fold_in(key_list[15], 71), 0)
    small_params = draw_small_params(jax.random.fold_in(key_list[15], 71), 0)
    small_first = scatter_about(key_list[13], (12, D), (0.1 * TOKENS ** 0.5), 80.0, (), jnp.float32)
    small_second = jnp.clip(jnp.exp(jax.random.uniform(key_list[14], (12, D), jnp.float32, math.log(8.192), math.log(65.536))), 8.192, 65.536)
    return {"block_input": block_input, "cotangent": cotangent, "lengths": lengths, "block_order": block_order, "w_qkv": w_qkv, "w_out": w_out, "w_fc": w_fc, "w_proj": w_proj, "mom_qkv": mom_qkv, "mom_out": mom_out, "mom_fc": mom_fc, "mom_proj": mom_proj, "small_params": small_params, "small_first": small_first, "small_second": small_second}


@jax.custom_vjp
def low(v):
    return lax.optimization_barrier(v.astype(jnp.bfloat16)).astype(jnp.float32)

@jax.custom_vjp
def low_back(v):
    return v

def low_keep(v):
    return (low(v), None)

def low_pass(kept, grad):
    return (grad,)

def back_keep(v):
    return (v, None)

def back_low(kept, grad):
    return (low(grad),)
low.defvjp(low_keep, low_pass)
low_back.defvjp(back_keep, back_low)
momentum_decay = 0.95
muon_rate = 0.15
out_rate = 0.75
muon_decay = 0.01
adam_rate = 0.4
beta_one = 0.9
beta_two = 0.999
adam_eps = 1e-08
norm_eps = 1e-05
poly_a = 3.4445
poly_b = -4.775
poly_c = 2.0315
masked_score = -1e+30

def product(left, right):
    return jnp.dot(left, right, precision=lax.Precision.HIGHEST)

def layer_norm(values_in, gain_row, shift_row):
    centred = values_in - lax.optimization_barrier(jnp.mean(values_in, axis=-1, keepdims=True))
    spread = lax.optimization_barrier(jnp.mean(centred * centred, axis=-1, keepdims=True))
    return centred * lax.rsqrt(spread + norm_eps) * gain_row + shift_row

def gelu_tanh(argument):
    return 0.5 * argument * (1.0 + jnp.tanh(0.7978845608028654 * (argument + 0.044715 * argument * argument * argument)))

def group_block(inputs, params):
    tokens_in, length, order_row = inputs
    qkv_weight, out_weight, fc_weight, proj_weight, small = params
    offsets = jnp.arange(BLOCK, dtype=jnp.int32)
    places = (order_row[:, None].astype(jnp.int32) * BLOCK + offsets[None, :]).reshape(-1)
    live_rows = (places < length).astype(jnp.float32)[:, None]
    normed = low(layer_norm(tokens_in, small[0], small[1]))
    qkv_bias = jnp.concatenate([small[4], jnp.zeros((D,), jnp.float32), small[5]])
    mixed_qkv = low_back(low(product(normed, qkv_weight) + qkv_bias))
    queries = mixed_qkv[:, :D].reshape(-1, H, HD)
    key_heads = mixed_qkv[:, D:2 * D].reshape(-1, H, HD)
    value_heads = mixed_qkv[:, 2 * D:].reshape(-1, H, HD)
    scores = low_back(jnp.einsum('qhd,khd->hqk', queries, key_heads, precision=lax.Precision.HIGHEST) * HD ** (-0.5))
    allowed = (places[None, :] <= places[:, None]) & (places[None, :] < length)
    scores = jnp.where(allowed[None], scores, masked_score)
    probability = low(jax.nn.softmax(scores, axis=-1))
    head_out = low_back(low(jnp.einsum('hqk,khd->qhd', probability, value_heads, precision=lax.Precision.HIGHEST).reshape(-1, D)))
    branch = low_back(product(head_out, out_weight) + small[6])
    residual = tokens_in + branch
    normed_two = low(layer_norm(residual, small[2], small[3]))
    hidden_pre = low_back(product(normed_two, fc_weight) + small[7:11].reshape(-1))
    activated = low(gelu_tanh(hidden_pre))
    feed_out = low_back(product(activated, proj_weight) + small[11])
    return (residual + feed_out) * live_rows

def orthogonalize(matrix):
    current = matrix / (jnp.sqrt(jnp.sum(matrix * matrix)) + 1e-07)
    for iteration in range(NS_STEPS):
        rounded = low(current)
        gram_matrix = product(rounded, rounded.T)
        gram_low = low(gram_matrix)
        square = product(gram_low, gram_low)
        polynomial = low(poly_b * gram_matrix + poly_c * square)
        current = poly_a * current + product(polynomial, rounded)
    return current

def muon(weight, momentum, gradient, transposed, rate):
    renewed = momentum_decay * momentum + gradient
    update = gradient + momentum_decay * renewed
    oriented = update.T if transposed else update
    orthogonal = orthogonalize(oriented)
    orthogonal = orthogonal.T if transposed else orthogonal
    stretch = 0.2 * math.sqrt(max(weight.shape))
    return (weight * (1.0 - rate * muon_decay) - rate * stretch * orthogonal, renewed)

def reference(block_input, cotangent, lengths, block_order, w_qkv, w_out, w_fc, w_proj, mom_qkv, mom_out, mom_fc, mom_proj, small_params, small_first, small_second):
    inputs_f = block_input.astype(jnp.float32)

    def forward(tokens_all, qkv_weight, out_weight, fc_weight, proj_weight, small):
        params = (low(qkv_weight).reshape(D, 3 * D), low(out_weight), low(fc_weight), low(proj_weight), low(small))
        blocks = tokens_all.reshape(GROUPS, GROUP, D)
        step_block = jax.checkpoint(lambda inputs: group_block(inputs, params))
        return lax.map(step_block, (blocks, lengths, block_order)).reshape(GROUPS * GROUP, D)
    outputs, pullback = jax.vjp(forward, inputs_f, w_qkv, w_out, w_fc, w_proj, small_params)
    input_grad, grad_qkv, grad_out, grad_fc, grad_proj, grad_small = pullback(cotangent)
    new_qkv, next_mom_qkv = muon(w_qkv.reshape(D, 3 * D), mom_qkv.reshape(D, 3 * D), grad_qkv.reshape(D, 3 * D), False, muon_rate)
    new_out, next_mom_out = muon(w_out, mom_out, grad_out, False, out_rate)
    new_fc, next_mom_fc = muon(w_fc, mom_fc, grad_fc, False, muon_rate)
    new_proj, next_mom_proj = muon(w_proj, mom_proj, grad_proj, True, muon_rate)
    next_first = beta_one * small_first + (1.0 - beta_one) * grad_small
    next_second = beta_two * small_second + (1.0 - beta_two) * grad_small * grad_small
    first_hat = next_first / (1.0 - beta_one ** STEP)
    second_hat = next_second / (1.0 - beta_two ** STEP)
    next_small = small_params - adam_rate * first_hat / (jnp.sqrt(second_hat) + adam_eps)
    return (outputs.astype(jnp.bfloat16), input_grad, grad_qkv, grad_out, grad_fc, grad_proj, grad_small, new_qkv.reshape(D, 3, D), new_out, new_fc, new_proj, next_mom_qkv.reshape(D, 3, D), next_mom_out, next_mom_fc, next_mom_proj, next_first, next_second, next_small, grad_small[11])
```

```python
import math

import jax
import jax.numpy as jnp
from jax import lax
from jax.sharding import PartitionSpec as P

D = 768
HD = 64
FF = 3072
BLOCK = 128
STEP = 10
momentum_decay = 0.95
muon_rate = 0.15
out_rate = 0.75
muon_decay = 0.01
adam_rate = 0.4
beta_one = 0.9
beta_two = 0.999
adam_eps = 1e-08
norm_eps = 1e-05
poly_a = 3.4445
poly_b = -4.775
poly_c = 2.0315
masked_score = -1e30
bf16 = jnp.bfloat16
f32 = jnp.float32


def dot(left, right, dims=((1,), (0,))):
    return lax.dot_general(left, right, (dims, ((), ())), preferred_element_type=f32)


def norm_parts(v):
    mean = jnp.mean(v, axis=-1, keepdims=True)
    centred = v - mean
    r = lax.rsqrt(jnp.mean(centred * centred, axis=-1, keepdims=True) + norm_eps)
    return centred * r, r


def norm_back(xhat, r, gain, c):
    cg = c * gain
    return r * (cg - jnp.mean(cg, -1, keepdims=True) - xhat * jnp.mean(cg * xhat, -1, keepdims=True))


def gelu_both(v):
    k = 0.7978845608028654
    t = jnp.tanh(k * (v + 0.044715 * v * v * v))
    value = 0.5 * v * (1.0 + t)
    slope = 0.5 * (1.0 + t) + 0.5 * v * (1.0 - t * t) * k * (1.0 + 3 * 0.044715 * v * v)
    return value, slope


def gather(v):
    return lax.all_gather(v, "shard", axis=0, tiled=True)


def scatter_sum(v):
    return lax.psum_scatter(v.astype(bf16), "shard", scatter_dimension=0, tiled=True).astype(f32)


def chain(g):
    q = None
    for k in range(4):
        gl = g.astype(bf16)
        p = (poly_b * g + poly_c * dot(gl, gl)).astype(bf16)
        if q is None:
            eye = (lax.broadcasted_iota(jnp.int32, g.shape, 0) == lax.broadcasted_iota(jnp.int32, g.shape, 1))
            q = p.astype(f32) + poly_a * eye.astype(f32)
        else:
            q = poly_a * q + dot(p, q.astype(bf16))
        if k < 3:
            t = poly_a * g + dot(p, gl)
            g = poly_a * t + dot(t.astype(bf16), p)
    return q


def shards(block_input, cotangent, lengths, block_order, w_qkv, w_out, w_fc, w_proj, mom_qkv, mom_out, mom_fc, mom_proj, small_params, small_first, small_second):
    member = lax.axis_index("shard")
    rows = block_input.shape[0]
    heads = w_out.shape[0] // HD
    offsets = jnp.arange(BLOCK, dtype=jnp.int32)
    places = (block_order[0][:, None] * BLOCK + offsets[None, :]).reshape(-1)
    own_places = lax.dynamic_slice_in_dim(places, member * rows, rows)
    length = lengths[0]
    live = (own_places < length).astype(f32)[:, None]
    small = lax.optimization_barrier(small_params.astype(bf16)).astype(f32)
    x_own = block_input.astype(f32)
    masked = cotangent * live
    x_all = gather(block_input).astype(f32)
    masked_low = gather(masked.astype(bf16))
    wq = w_qkv.astype(bf16).reshape(D, -1)
    wo, wf, wp = w_out.astype(bf16), w_fc.astype(bf16), w_proj.astype(bf16)
    hc = w_out.shape[0]

    def cols(row):
        return lax.dynamic_slice_in_dim(row, member * hc, hc)

    xhat_one, r_one = norm_parts(x_all)
    normed = (xhat_one * small[0] + small[1]).astype(bf16)
    qkv_bias = jnp.concatenate([cols(small[4]), jnp.zeros((hc,), f32), cols(small[5])])
    mixed = (dot(normed, wq) + qkv_bias).astype(bf16)
    allowed = (places[None, :] <= places[:, None]) & (places[None, :] < length)
    outs, probs = [], []
    scale = HD ** -0.5
    for h in range(heads):
        q = mixed[:, h * HD : (h + 1) * HD]
        k = mixed[:, hc + h * HD : hc + (h + 1) * HD]
        v = mixed[:, 2 * hc + h * HD : 2 * hc + (h + 1) * HD]
        sc = jnp.where(allowed, dot(q, k, ((1,), (1,))) * scale, masked_score)
        e = jnp.exp(sc - jnp.max(sc, -1, keepdims=True))
        p = e / jnp.sum(e, -1, keepdims=True)
        probs.append(p)
        outs.append(dot(p.astype(bf16), v).astype(bf16))
    head_out = jnp.concatenate(outs, 1)
    residual = x_own + scatter_sum(dot(head_out, wo)) + small[6]
    xhat_two, r_two = norm_parts(residual)
    normed_two = gather((xhat_two * small[2] + small[3]).astype(bf16))
    fc_bias = lax.dynamic_slice_in_dim(small[7:11], member, 1)
    hidden = dot(normed_two, wf) + fc_bias
    act, slope = gelu_both(hidden)
    act = act.astype(bf16)
    block_output = ((residual + scatter_sum(dot(act, wp)) + small[11]) * live).astype(bf16)
    g_proj = dot(act, masked_low, ((0,), (0,)))
    grad_pre = (slope * dot(masked_low, wp, ((1,), (1,)))).astype(bf16)
    g_fc = dot(normed_two, grad_pre, ((0,), (0,)))
    c_two = scatter_sum(dot(grad_pre, wf, ((1,), (1,))))
    grad_residual = masked + norm_back(xhat_two, r_two, small[2], c_two)
    branch_low = gather(grad_residual.astype(bf16))
    g_out = dot(head_out, branch_low, ((0,), (0,)))
    grad_heads = dot(branch_low, wo, ((1,), (1,))).astype(bf16)
    dq, dk, dv = [], [], []
    for h in range(heads):
        q = mixed[:, h * HD : (h + 1) * HD]
        k = mixed[:, hc + h * HD : hc + (h + 1) * HD]
        v = mixed[:, 2 * hc + h * HD : 2 * hc + (h + 1) * HD]
        gh = grad_heads[:, h * HD : (h + 1) * HD]
        p = probs[h]
        dv.append(dot(p.astype(bf16), gh, ((0,), (0,))))
        gp = dot(gh, v, ((1,), (1,)))
        gs = (p * (gp - jnp.sum(p * gp, -1, keepdims=True))).astype(bf16)
        dq.append(dot(gs, k) * scale)
        dk.append(dot(gs, q, ((0,), (0,))) * scale)
    grad_mixed = jnp.concatenate(dq + dk + dv, 1).astype(bf16)
    g_qkv = dot(normed, grad_mixed, ((0,), (0,)))
    c_one = scatter_sum(dot(grad_mixed, wq, ((1,), (1,))))
    own_hat, own_r = norm_parts(x_own)
    input_grad = grad_residual + norm_back(own_hat, own_r, small[0], c_one)

    def place_cols(row):
        return lax.dynamic_update_slice_in_dim(jnp.zeros((1, D), f32), row[None], member * hc, 1)

    mixed_sums = jnp.sum(grad_mixed.astype(f32), 0)
    pre_sums = jnp.sum(grad_pre.astype(f32), 0)[None]
    small_term = jnp.concatenate([
        jnp.sum(c_one * own_hat, 0)[None],
        jnp.sum(c_one, 0)[None],
        jnp.sum(c_two * xhat_two, 0)[None],
        jnp.sum(c_two, 0)[None],
        place_cols(mixed_sums[:hc]),
        place_cols(mixed_sums[2 * hc :]),
        jnp.sum(grad_residual.astype(bf16).astype(f32), 0)[None],
        lax.dynamic_update_slice_in_dim(jnp.zeros((4, D), f32), pre_sums, member, 0),
        jnp.sum(masked.astype(bf16).astype(f32), 0)[None],
    ], axis=0)
    grad_small = lax.psum(small_term, ("rep", "shard"))
    grads = lax.psum(tuple(g.astype(bf16) for g in (g_qkv, g_out, g_fc, g_proj)), "rep")
    grads = [g.astype(f32) for g in grads]
    moms = [mom_qkv.reshape(D, -1), mom_out, mom_fc, mom_proj]
    new_moms = [momentum_decay * m + g for m, g in zip(moms, grads)]
    updates = [(g + momentum_decay * m).astype(bf16) for g, m in zip(grads, new_moms)]
    over_rows = ((0,), (0,))
    over_cols = ((1,), (1,))
    dims = [over_cols, over_rows, over_cols, over_rows]
    grams = jnp.stack([dot(u, u, d) for u, d in zip(updates, dims)])
    gram = lax.psum_scatter(grams, "shard", scatter_dimension=0, tiled=True)[0]
    eye = (lax.broadcasted_iota(jnp.int32, gram.shape, 0) == lax.broadcasted_iota(jnp.int32, gram.shape, 1))
    inv = 1.0 / (jnp.sqrt(jnp.sum(jnp.where(eye, gram, 0.0))) + 1e-07)
    factor = (chain(gram * inv * inv) * inv).astype(bf16)
    factors = gather(factor[None])
    left = ((1,), (0,))
    orth = [dot(factors[0], updates[0]), dot(updates[1], factors[1]), dot(factors[2], updates[2]), dot(updates[3], factors[3])]
    news = []
    for w, o, longest, rate in zip([w_qkv.reshape(D, -1), w_out, w_fc, w_proj], orth, [3 * D, D, FF, FF], [muon_rate, out_rate, muon_rate, muon_rate]):
        news.append(w * (1.0 - rate * muon_decay) - rate * 0.2 * math.sqrt(longest) * o)
    next_first = beta_one * small_first + (1.0 - beta_one) * grad_small
    next_second = beta_two * small_second + (1.0 - beta_two) * grad_small * grad_small
    first_hat = next_first / (1.0 - beta_one**STEP)
    second_hat = next_second / (1.0 - beta_two**STEP)
    next_small = small_params - adam_rate * first_hat / (jnp.sqrt(second_hat) + adam_eps)
    cube = w_qkv.shape
    return (block_output, input_grad, grads[0].reshape(cube), *grads[1:], grad_small, news[0].reshape(cube), *news[1:], new_moms[0].reshape(cube), *new_moms[1:], next_first, next_second, next_small, grad_small[11])


def solution(mesh):
    rows = P(("rep", "shard"), None)
    mats = (P(None, None, "shard"), P("shard", None), P(None, "shard"), P("shard", None))
    in_specs = (rows, rows, P("rep"), P("rep", None), *mats, *mats, P(), P(), P())
    out_specs = (rows, rows, *mats, P(), *mats, *mats, P(), P(), P(), P())
    return jax.shard_map(shards, mesh=mesh, in_specs=in_specs, out_specs=out_specs, check_vma=False)
```

```python
import math

import jax
import jax.numpy as jnp
from jax import lax
from jax.experimental import pallas as pl
from jax.experimental.pallas import tpu as pltpu
from jax.sharding import PartitionSpec as P

D = 768
HD = 64
FF = 3072
BLOCK = 128
STEP = 10
momentum_decay = 0.95
muon_rate = 0.15
out_rate = 0.75
muon_decay = 0.01
adam_rate = 0.4
beta_one = 0.9
beta_two = 0.999
adam_eps = 1e-08
norm_eps = 1e-05
poly_a = 3.4445
poly_b = -4.775
poly_c = 2.0315
masked_score = -1e30
bf16 = jnp.bfloat16
f32 = jnp.float32


def dot(left, right, dims=((1,), (0,))):
    return lax.dot_general(left, right, (dims, ((), ())), preferred_element_type=f32)


MESH = pl.DeviceIdType.MESH
ROWS = 2304
HALF = 384


def place():
    rep = lax.axis_index("rep")
    return rep % 4, rep // 8, (rep // 4) % 2, lax.axis_index("shard")


def device(x, y, z, shard):
    return ((y * 2 + z) * 4 + x, shard)


def sum_kernel(parts_ref, small_ref, out_ref, small_out, got_one, got_two, got_z, pass_one, pass_two, mid, small_got, send, recv, small_send, small_recv):
    x, y, z, shard = place()
    xl, xr, yl, yr = (x + 3) % 4, (x + 1) % 4, (y + 3) % 4, (y + 1) % 4
    sides = {
        "x": (x, device(xl, y, z, shard), device(xr, y, z, shard)),
        "y": (y, device(x, yl, z, shard), device(x, yr, z, shard)),
    }
    across = device(x, y, 1 - z, shard)
    steps = [
        device(x, y, z, shard + 1 - 2 * (shard % 2)),
        device(x, y, z, (shard + 2) % 4),
        device(x + 1 - 2 * (x % 2), y, z, shard),
        device(3 - x, y, z, shard),
        device(x, y + 1 - 2 * (y % 2), z, shard),
        device(x, 3 - y, z, shard),
        across,
    ]
    barrier = pltpu.get_barrier_semaphore()
    partners = [sides["x"][1], sides["x"][2], sides["y"][1], sides["y"][2], across, steps[0], steps[1]]
    for partner in partners:
        pl.semaphore_signal(barrier, inc=1, device_id=partner, device_id_type=MESH)
    pl.semaphore_wait(barrier, len(partners))

    used = [0]

    def copy(src, dst, target):
        k = used[0]
        used[0] += 1
        c = pltpu.make_async_remote_copy(src_ref=src, dst_ref=dst, send_sem=send.at[k], recv_sem=recv.at[k], device_id=target, device_id_type=MESH)
        c.start()
        return c

    small_out[...] = small_ref[...]
    small_copies = []

    def small_start(k):
        c = pltpu.make_async_remote_copy(src_ref=small_out, dst_ref=small_got.at[k], send_sem=small_send.at[k], recv_sem=small_recv.at[k], device_id=steps[k], device_id_type=MESH)
        c.start()
        small_copies.append(c)

    def small_end(k):
        small_copies[k].wait()
        small_out[...] += small_got[k]

    def rows(start, size):
        return pl.ds(pl.multiple_of(start, 16), size)

    def reduce_start(axis, ref, base, n, cut, got):
        p, left, right = sides[axis]
        opp, nxt, prv = (p + 2) % 4, (p + 1) % 4, (p + 3) % 4
        first = (
            copy(ref.at[rows(base + opp * n, cut), :], got.at[0, 0:cut, :], right),
            copy(ref.at[rows(base + opp * n + cut, n - cut), :], got.at[1, cut:n, :], left),
            copy(ref.at[rows(base + nxt * n + cut, n - cut), :], got.at[2, cut:n, :], right),
            copy(ref.at[rows(base + prv * n, cut), :], got.at[3, 0:cut, :], left),
        )
        return first, (p, left, right, nxt, prv, ref, base, n, cut, got)

    def reduce_pass(state, passing):
        first, (p, left, right, nxt, prv, ref, base, n, cut, got) = state
        first[0].wait_recv()
        passing[0:cut, :] = (ref[rows(base + nxt * n, cut), :].astype(f32) + got[0, 0:cut, :].astype(f32)).astype(bf16)
        second = [copy(passing.at[0:cut, :], got.at[4, 0:cut, :], right)]
        first[1].wait_recv()
        passing[cut:n, :] = (ref[rows(base + prv * n + cut, n - cut), :].astype(f32) + got[1, cut:n, :].astype(f32)).astype(bf16)
        second.append(copy(passing.at[cut:n, :], got.at[4, cut:n, :], left))
        return second

    def reduce_end(state, second, dst, at):
        first, (p, left, right, nxt, prv, ref, base, n, cut, got) = state
        first[3].wait_recv()
        second[0].wait_recv()
        dst[rows(at, cut), :] = (ref[rows(base + p * n, cut), :].astype(f32) + got[3, 0:cut, :].astype(f32) + got[4, 0:cut, :].astype(f32)).astype(bf16)
        first[2].wait_recv()
        second[1].wait_recv()
        dst[rows(at + cut, n - cut), :] = (ref[rows(base + p * n + cut, n - cut), :].astype(f32) + got[2, cut:n, :].astype(f32) + got[4, cut:n, :].astype(f32)).astype(bf16)
        for c in (*first, *second):
            c.wait_send()

    def gather_start(axis, ref, base, n, cut):
        p, left, right = sides[axis]
        own_a, own_b = rows(base + p * n, cut), rows(base + p * n + cut, n - cut)
        first = (
            copy(ref.at[own_a, :], ref.at[own_a, :], right),
            copy(ref.at[own_b, :], ref.at[own_b, :], left),
            copy(ref.at[own_b, :], ref.at[own_b, :], right),
            copy(ref.at[own_a, :], ref.at[own_a, :], left),
        )
        return first, (p, left, right, ref, base, n, cut)

    def gather_pass(state):
        first, (p, left, right, ref, base, n, cut) = state
        prv, nxt = (p + 3) % 4, (p + 1) % 4
        first[0].wait_recv()
        spot = rows(base + prv * n, cut)
        second = [copy(ref.at[spot, :], ref.at[spot, :], right)]
        first[1].wait_recv()
        spot = rows(base + nxt * n + cut, n - cut)
        second.append(copy(ref.at[spot, :], ref.at[spot, :], left))
        return second

    def gather_end(state, second):
        for c in (*state[0][2:], *second):
            c.wait_recv()
        for c in (*state[0], *second):
            c.wait_send()

    part_a, part_b = parts_ref.at[0], parts_ref.at[1]
    out_a, out_b = out_ref.at[0], out_ref.at[1]
    big, small_n = ROWS // 4, ROWS // 16
    state_a = reduce_start("x", part_a, 0, big, big // 2, got_one.at[0])
    state_b = reduce_start("y", part_b, 0, big, big // 2, got_one.at[1])
    small_start(0)
    second_a = reduce_pass(state_a, pass_one.at[0])
    second_b = reduce_pass(state_b, pass_one.at[1])
    small_end(0)
    small_start(1)
    base_a, base_b = x * big, y * big
    reduce_end(state_a, second_a, mid.at[0], 0)
    reduce_end(state_b, second_b, mid.at[1], 0)
    small_end(1)
    small_start(2)
    cut = 80
    state_a = reduce_start("y", mid.at[0], 0, small_n, cut, got_two.at[0])
    state_b = reduce_start("x", mid.at[1], 0, small_n, cut, got_two.at[1])
    second_a = reduce_pass(state_a, pass_two.at[0])
    second_b = reduce_pass(state_b, pass_two.at[1])
    small_end(2)
    small_start(3)
    reduce_end(state_a, second_a, pass_two.at[2], 0)
    reduce_end(state_b, second_b, pass_two.at[3], 0)
    over = [copy(pass_two.at[2 + k], got_z.at[k], across) for k in range(2)]
    small_end(3)
    small_start(4)
    at_a, at_b = base_a + y * small_n, base_b + x * small_n
    over[0].wait()
    out_a[rows(at_a, small_n), :] = (pass_two[2].astype(f32) + got_z[0].astype(f32)).astype(bf16)
    state_a = gather_start("y", out_a, base_a, small_n, cut)
    over[1].wait()
    out_b[rows(at_b, small_n), :] = (pass_two[3].astype(f32) + got_z[1].astype(f32)).astype(bf16)
    state_b = gather_start("x", out_b, base_b, small_n, cut)
    second_a = gather_pass(state_a)
    second_b = gather_pass(state_b)
    small_end(4)
    small_start(5)
    gather_end(state_a, second_a)
    gather_end(state_b, second_b)
    state_a = gather_start("x", out_a, 0, big, big // 2)
    state_b = gather_start("y", out_b, 0, big, big // 2)
    small_end(5)
    small_start(6)
    second_a = gather_pass(state_a)
    second_b = gather_pass(state_b)
    small_end(6)
    gather_end(state_a, second_a)
    gather_end(state_b, second_b)


def sum_over_groups(parts, small_term):
    vm = pl.BlockSpec(memory_space=pltpu.VMEM)
    big, little = ROWS // 4, ROWS // 16
    return pl.pallas_call(
        sum_kernel,
        out_shape=(jax.ShapeDtypeStruct((2, ROWS, HALF), bf16), jax.ShapeDtypeStruct((12, D), f32)),
        in_specs=[vm, vm],
        out_specs=(vm, vm),
        scratch_shapes=[
            pltpu.VMEM((2, 5, big, HALF), bf16),
            pltpu.VMEM((2, 5, little, HALF), bf16),
            pltpu.VMEM((2, little, HALF), bf16),
            pltpu.VMEM((2, big, HALF), bf16),
            pltpu.VMEM((4, little, HALF), bf16),
            pltpu.VMEM((2, big, HALF), bf16),
            pltpu.VMEM((7, 12, D), f32),
            pltpu.SemaphoreType.DMA((50,)),
            pltpu.SemaphoreType.DMA((50,)),
            pltpu.SemaphoreType.DMA((7,)),
            pltpu.SemaphoreType.DMA((7,)),
        ],
        compiler_params=pltpu.CompilerParams(collective_id=1, has_side_effects=True, vmem_limit_bytes=40 * 1024 * 1024),
    )(parts, small_term)


def make_gather(sides, copy):
    def start(axis, ref, base, n, cut, unit):
        p, left, right = sides[axis]

        def rows(chunk, first):
            at = base + chunk * n + (0 if first else cut)
            return pl.ds(pl.multiple_of(at, unit), cut if first else n - cut)

        def send(chunk, first, target):
            spot = rows(chunk, first)
            return copy(ref.at[spot, :], ref.at[spot, :], target)

        first = (send(p, True, right), send(p, False, left), send(p, False, right), send(p, True, left))
        return first, (p, left, right, send)

    def onward(state):
        first, (p, left, right, send) = state
        first[0].wait_recv()
        second = [send((p + 3) % 4, True, right)]
        first[1].wait_recv()
        second.append(send((p + 1) % 4, False, left))
        return second

    def end(state, second):
        for c in (*state[0][2:], *second):
            c.wait_recv()
        for c in (*state[0], *second):
            c.wait_send()

    def both(refs, orders, base, sizes, unit):
        for step in range(2):
            states = []
            for k in range(2):
                n, cut = sizes[step]
                states.append(start(orders[k][step], refs[k], base[k] if step == 0 else 0, n, cut, unit))
            seconds = [onward(state) for state in states]
            for state, second in zip(states, seconds):
                end(state, second)

    return both


def muon_kernel(u_qkv, u_out, u_fc, u_proj, q_all, piece, got, halves, gram, gram_low, poly, factor, factor_low, send, recv):
    x, y, z, shard = place()
    sides = {
        "x": (x, device((x + 3) % 4, y, z, shard), device((x + 1) % 4, y, z, shard)),
        "y": (y, device(x, (y + 3) % 4, z, shard), device(x, (y + 1) % 4, z, shard)),
    }
    others = [device(x, y, z, (shard + d) % 4) for d in (1, 2, 3)]
    sibling = device(x, y, z, shard + 1 - 2 * (shard % 2))
    barrier = pltpu.get_barrier_semaphore()
    partners = [*sides["x"][1:], *sides["y"][1:], *others]
    for partner in partners:
        pl.semaphore_signal(barrier, inc=1, device_id=partner, device_id_type=MESH)

    used = [0]

    def copy(src, dst, target):
        k = used[0]
        used[0] += 1
        c = pltpu.make_async_remote_copy(src_ref=src, dst_ref=dst, send_sem=send.at[k], recv_sem=recv.at[k], device_id=target, device_id_type=MESH)
        c.start()
        return c

    gather = make_gather(sides, copy)
    n = D // 16
    at = (pl.multiple_of((x * 4 + y) * n, 16), pl.multiple_of((y * 4 + x) * n, 16))
    over_cols, over_rows = ((1,), (1,)), ((0,), (0,))
    for k in range(2):
        cols = slice(k * HALF, k * HALF + HALF)
        pick = (lax.broadcasted_iota(jnp.int32, (D, n), 0) == lax.broadcasted_iota(jnp.int32, (D, n), 1) + at[k]).astype(f32).astype(bf16)
        for m, u in enumerate((u_qkv, u_out, u_fc, u_proj)):
            if m % 2 == 0:
                piece[m, k] = dot(u[pl.ds(at[k], n), :], u[cols, :], over_cols)
            else:
                own = dot(u[...], pick).astype(bf16)
                piece[m, k] = dot(own, u[:, cols], over_rows)
    pl.semaphore_wait(barrier, len(partners))
    sums = [copy(piece.at[(shard + d) % 4], got.at[d - 1], others[d - 1]) for d in (1, 2, 3)]
    for c in sums:
        c.wait_recv()
    for k in range(2):
        halves[k, pl.ds(at[k], n), :] = piece[shard, k] + got[0, k] + got[1, k] + got[2, k]
    orders = (("y", "x"), ("x", "y"))
    base = (x * 4 * n, y * 4 * n)
    gather([halves.at[0], halves.at[1]], orders, base, ((n, 24), (4 * n, 2 * n)), 8)
    for c in sums:
        c.wait_send()

    tile = 256
    blocks = D // tile

    def eye(r, width, first):
        return (lax.broadcasted_iota(jnp.int32, (tile, width), 0) + r * tile == lax.broadcasted_iota(jnp.int32, (tile, width), 1) + first).astype(f32)

    trace = jnp.zeros((1, 1), f32)
    for r in range(blocks):
        for k in range(2):
            part = halves[k, r * tile : (r + 1) * tile, :] * eye(r, HALF, k * HALF)
            trace = trace + jnp.sum(jnp.sum(part, axis=1, keepdims=True), axis=0, keepdims=True)
    inv = 1.0 / (jnp.sqrt(trace) + 1e-07)
    for r in range(blocks):
        spot = slice(r * tile, (r + 1) * tile)
        for k in range(2):
            cols = slice(k * HALF, k * HALF + HALF)
            g = halves[k, spot, :] * (inv * inv)
            gram[spot, cols] = g
            gram_low[0, spot, cols] = g.astype(bf16)

    for k in range(4):
        now, later = k % 2, (k + 1) % 2

        def poly_rows(r, carry):
            spot = pl.ds(pl.multiple_of(r * tile, tile), tile)
            poly[spot, :] = (poly_b * gram[spot, :] + poly_c * dot(gram_low[now, spot, :], gram_low[now])).astype(bf16)
            return carry

        def update_rows(r, carry):
            spot = pl.ds(pl.multiple_of(r * tile, tile), tile)
            p = poly[spot, :]
            if k == 0:
                q = p.astype(f32) + poly_a * eye(r, D, 0)
            else:
                q = poly_a * factor[spot, :] + dot(p, factor_low[now])
            factor[spot, :] = q
            if k < 3:
                factor_low[later, spot, :] = q.astype(bf16)
                t = poly_a * gram[spot, :] + dot(p, gram_low[now])
                g = poly_a * t + dot(t.astype(bf16), poly[...])
                gram[spot, :] = g
                gram_low[later, spot, :] = g.astype(bf16)
            return carry

        lax.fori_loop(0, blocks, poly_rows, 0)
        lax.fori_loop(0, blocks, update_rows, 0)
    for r in range(blocks):
        spot = slice(r * tile, (r + 1) * tile)
        for k in range(2):
            q_all[shard, k, spot, :] = (factor[spot, k * HALF : (k + 1) * HALF] * inv).astype(bf16)

    away = (shard + 2) % 4
    pieces = [copy(q_all.at[shard, k, pl.ds(at[k], n), :], q_all.at[shard, k, pl.ds(at[k], n), :], others[1]) for k in range(2)]
    near = copy(q_all.at[shard], q_all.at[shard], sibling)
    for c in pieces:
        c.wait_recv()
    gather([q_all.at[away, 0], q_all.at[away, 1]], orders, base, ((n, 32), (4 * n, 2 * n)), 16)
    far = copy(q_all.at[away], q_all.at[away], sibling)
    for c in (*pieces, near):
        c.wait_send()
    near.wait_recv()
    far.wait()


def muon_factors(updates):
    vm = pl.BlockSpec(memory_space=pltpu.VMEM)
    n = D // 16
    return pl.pallas_call(
        muon_kernel,
        out_shape=jax.ShapeDtypeStruct((4, 2, D, HALF), bf16),
        in_specs=[vm] * 4,
        out_specs=vm,
        scratch_shapes=[
            pltpu.VMEM((4, 2, n, HALF), f32),
            pltpu.VMEM((3, 2, n, HALF), f32),
            pltpu.VMEM((2, D, HALF), f32),
            pltpu.VMEM((D, D), f32),
            pltpu.VMEM((2, D, D), bf16),
            pltpu.VMEM((D, D), bf16),
            pltpu.VMEM((D, D), f32),
            pltpu.VMEM((2, D, D), bf16),
            pltpu.SemaphoreType.DMA((60,)),
            pltpu.SemaphoreType.DMA((60,)),
        ],
        compiler_params=pltpu.CompilerParams(collective_id=2, has_side_effects=True, vmem_limit_bytes=44 * 1024 * 1024),
    )(*updates)


def block_kernel(
    x_ref, cot_ref, live_ref, col_ref, row_ref, len_ref, wq, wo_hbm, wf_hbm, wp_hbm, small, qkv_bias, fc_bias,
    out_ref, dx_ref, parts, small_out,
    nrm, mlow, nrm2, branch, mixed, probs, bias, head_out, part, got, passing, wo32, wf32, wp32, wo, wf, wp,
    gact, act, gpre, gheads, gmixed, xhat1, xhat2, resid, gres, send, recv, local,
):
    x, y, z, shard = place()
    sib = shard + 1 - 2 * (shard % 2)
    par = (shard + 2) % 4
    sibling, partner = device(x, y, z, sib), device(x, y, z, par)
    barrier = pltpu.get_barrier_semaphore()
    for other in (sibling, partner):
        pl.semaphore_signal(barrier, inc=1, device_id=other, device_id_type=MESH)
    loads = [pltpu.make_async_copy(src, dst, local.at[k]) for k, (src, dst) in enumerate(((wo_hbm, wo32), (wf_hbm, wf32), (wp_hbm, wp32)))]
    for load in loads:
        load.start()

    rows = BLOCK

    def chunk(index, size=rows, at=0):
        return pl.ds(pl.multiple_of(index * rows + at, 16), size)

    own, own_sib, own_par, own_ps = chunk(shard), chunk(sib), chunk(par), chunk((sib + 2) % 4)
    near = pl.multiple_of((shard // 2) * 256, 256)
    far = pl.multiple_of(256 - near, 256)
    used = [0]

    def copy(src, dst, target):
        k = used[0]
        used[0] += 1
        c = pltpu.make_async_remote_copy(src_ref=src, dst_ref=dst, send_sem=send.at[k], recv_sem=recv.at[k], device_id=target, device_id_type=MESH)
        c.start()
        return c

    class Spread:
        def __init__(self, ref):
            self.ref = ref
            self.cross = [self.to(shard, 64 * i, partner) for i in range(2)]
            self.direct = copy(ref.at[own, :], ref.at[own, :], sibling)

        def to(self, index, at, target):
            spot = chunk(index, 64, at)
            return copy(self.ref.at[spot, :], self.ref.at[spot, :], target)

        def near(self):
            self.direct.wait_recv()

        def far(self):
            onward = []
            for i in range(2):
                self.cross[i].wait_recv()
                onward.append(self.to(par, 64 * i, sibling))
            for c in onward:
                c.wait_recv()
            for c in (*self.cross, self.direct, *onward):
                c.wait_send()

    class Fold:
        def __init__(self, k):
            self.k = k

        def start_far(self):
            self.a = copy(part.at[self.k, own_ps, :], got.at[self.k, 0], sibling)

        def start_near(self):
            self.b = copy(part.at[self.k, own_sib, :], got.at[self.k, 1], sibling)

        def cross(self):
            self.a.wait_recv()
            passing[self.k] = (part[self.k, own_par, :].astype(f32) + got[self.k, 0].astype(f32)).astype(bf16)
            self.c = copy(passing.at[self.k], got.at[self.k, 2], partner)

        def end(self):
            self.b.wait_recv()
            self.c.wait_recv()
            for c in (self.a, self.b, self.c):
                c.wait_send()
            return part[self.k, own, :].astype(f32) + got[self.k, 1].astype(f32) + got[self.k, 2].astype(f32)

    def norm(v):
        centred = v - jnp.mean(v, axis=-1, keepdims=True)
        r = lax.rsqrt(jnp.mean(centred * centred, axis=-1, keepdims=True) + norm_eps)
        return centred * r, r

    def norm_grad(xhat, r, gain, c):
        cg = c * gain
        return r * (cg - jnp.mean(cg, -1, keepdims=True) - xhat * jnp.mean(cg * xhat, -1, keepdims=True))

    def total(v):
        return jnp.sum(v, axis=0, keepdims=True)

    nt, tn = ((1,), (1,)), ((0,), (0,))
    hc = wq.shape[1] // 3
    heads = hc // HD
    scale = HD ** -0.5

    xf = x_ref[...].astype(f32)
    hat, r_one = norm(xf)
    xhat1[...] = hat
    nrm[own, :] = (hat * small[0:1, :] + small[1:2, :]).astype(bf16)
    mlow[own, :] = (cot_ref[...] * live_ref[...]).astype(bf16)
    pl.semaphore_wait(barrier, 2)
    go_nrm = Spread(nrm)
    go_mlow = Spread(mlow)
    bias[...] = jnp.where((row_ref[...] <= col_ref[...]) & (row_ref[...] < len_ref[...]), 0.0, masked_score)
    loads[0].wait()
    wo[...] = wo32[...].astype(bf16)

    def mix(at):
        spot = pl.ds(at, 256)
        mixed[spot, :] = (dot(nrm[spot, :], wq[...]) + qkv_bias[...]).astype(bf16)

    go_nrm.near()
    mix(near)
    go_nrm.far()
    mix(far)

    def head(h, part_of):
        lo = part_of * hc + h * HD
        return slice(lo, lo + HD)

    for h in range(heads):

        def attend(i, carry):
            spot = pl.ds(pl.multiple_of(i * 256, 256), 256)
            s = dot(mixed[spot, head(h, 0)], mixed[:, head(h, 1)], nt) * scale + bias[spot, :]
            e = jnp.exp(s - jnp.max(s, axis=-1, keepdims=True))
            p = (e * (1.0 / jnp.sum(e, axis=-1, keepdims=True))).astype(bf16)
            probs[h, spot, :] = p
            head_out[spot, head(h, 0)] = dot(p, mixed[:, head(h, 2)]).astype(bf16)
            return carry

        lax.fori_loop(0, 2, attend, 0)

    fold = Fold(0)
    part[0, pl.ds(far, 256), :] = dot(head_out[pl.ds(far, 256), :], wo[...]).astype(bf16)
    fold.start_far()
    part[0, pl.ds(near, 256), :] = dot(head_out[pl.ds(near, 256), :], wo[...]).astype(bf16)
    fold.start_near()
    fold.cross()
    go_mlow.near()
    go_mlow.far()
    loads[1].wait()
    wf[...] = wf32[...].astype(bf16)
    loads[2].wait()
    wp[...] = wp32[...].astype(bf16)

    def activation_grad(i, carry):
        spot = pl.ds(pl.multiple_of(i * 256, 256), 256)
        gact[spot, :] = dot(mlow[spot, :], wp[...], nt)
        return carry

    lax.fori_loop(0, 2, activation_grad, 0)
    res = x_ref[...].astype(f32) + fold.end() + small[6:7, :]
    resid[...] = res
    hat, r_two = norm(res)
    xhat2[...] = hat
    nrm2[own, :] = (hat * small[2:3, :] + small[3:4, :]).astype(bf16)
    go_nrm2 = Spread(nrm2)

    def feed(at):
        spot = pl.ds(at, 256)
        hidden = dot(nrm2[spot, :], wf[...]) + fc_bias[...]
        k = 0.7978845608028654
        square = hidden * hidden
        t = jnp.tanh(k * (hidden + 0.044715 * hidden * square))
        half = 0.5 * (1.0 + t)
        act[spot, :] = (hidden * half).astype(bf16)
        slope = half + 0.5 * hidden * (1.0 - t * t) * (k + (3 * 0.044715 * k) * square)
        gpre[spot, :] = (slope * gact[spot, :]).astype(bf16)

    go_nrm2.near()
    feed(near)
    go_nrm2.far()
    feed(far)
    fold = Fold(1)
    part[1, pl.ds(far, 256), :] = dot(gpre[pl.ds(far, 256), :], wf[...], nt).astype(bf16)
    fold.start_far()
    part[1, pl.ds(near, 256), :] = dot(gpre[pl.ds(near, 256), :], wf[...], nt).astype(bf16)
    fold.start_near()
    fold.cross()

    def keep(at, size, value):
        low_value = value.astype(bf16)
        parts[0, pl.ds(at, size), :] = low_value[:, :HALF]
        parts[1, pl.ds(at, size), :] = low_value[:, HALF:]

    def grad_columns(base, left, right, width):
        for c in range(left.shape[1] // width):
            keep(base + c * width, width, dot(left[:, c * width : (c + 1) * width], right[...], tn))

    grad_columns(D, act, mlow, 256)
    small_out[11:12, :] = total(mlow[own, :].astype(f32))
    c_two = fold.end()
    hat = xhat2[...]
    small_out[2:3, :] = total(c_two * hat)
    small_out[3:4, :] = total(c_two)
    g = cot_ref[...] * live_ref[...] + norm_grad(hat, r_two, small[2:3, :], c_two)
    gres[...] = g
    branch[own, :] = g.astype(bf16)
    go_branch = Spread(branch)
    small_out[6:7, :] = total(branch[own, :].astype(f32))
    grad_columns(0, nrm2, gpre, 256)
    pre_sum = total(gpre[...].astype(f32))
    small_out[7:11, :] = jnp.where(lax.broadcasted_iota(jnp.int32, (4, D), 0) == shard, pre_sum, 0.0)

    def head_grads(at):
        spot = pl.ds(at, 256)
        gheads[spot, :] = dot(branch[spot, :], wo[...], nt).astype(bf16)

    go_branch.near()
    head_grads(near)
    go_branch.far()
    head_grads(far)
    fold_out = Fold(2)
    part[2, pl.ds(far, 256), :] = dot(act[pl.ds(far, 256), :], wp[...]).astype(bf16)
    fold_out.start_far()
    part[2, pl.ds(near, 256), :] = dot(act[pl.ds(near, 256), :], wp[...]).astype(bf16)
    fold_out.start_near()
    fold_out.cross()
    for h in range(heads):
        q, k, v = (mixed[:, head(h, i)] for i in range(3))
        gh = gheads[:, head(h, 0)]
        gmixed[:, head(h, 2)] = dot(gh, probs[h], tn).T.astype(bf16)

        def scores_grad(i, carry):
            spot = pl.ds(pl.multiple_of(i * 256, 256), 256)
            p = probs[h, spot, :].astype(f32)
            gp = dot(gheads[spot, head(h, 0)], mixed[:, head(h, 2)], nt)
            gs = (p * (gp - jnp.sum(p * gp, axis=-1, keepdims=True))).astype(bf16)
            probs[h, spot, :] = gs
            gmixed[spot, head(h, 0)] = (dot(gs, mixed[:, head(h, 1)]) * scale).astype(bf16)
            return carry

        lax.fori_loop(0, 2, scores_grad, 0)
        gmixed[:, head(h, 1)] = (dot(q, probs[h], tn).T * scale).astype(bf16)

    fold = Fold(3)
    part[3, pl.ds(far, 256), :] = dot(gmixed[pl.ds(far, 256), :], wq[...], nt).astype(bf16)
    fold.start_far()
    part[3, pl.ds(near, 256), :] = dot(gmixed[pl.ds(near, 256), :], wq[...], nt).astype(bf16)
    fold.start_near()
    fold.cross()
    grad_columns(2 * D, head_out, branch, hc)
    grad_columns(2 * D + hc, gmixed, nrm, hc)
    mixed_sum = total(gmixed[...].astype(f32))
    spread_out = (lax.broadcasted_iota(jnp.int32, (hc, D), 0) + shard * hc == lax.broadcasted_iota(jnp.int32, (hc, D), 1)).astype(f32)
    for row, lo in ((4, 0), (5, 2 * hc)):
        small_out[row : row + 1, :] = jnp.dot(mixed_sum[:, lo : lo + hc], spread_out, precision=lax.Precision.HIGHEST, preferred_element_type=f32)
    out_ref[...] = ((resid[...] + fold_out.end() + small[11:12, :]) * live_ref[...]).astype(bf16)
    c_one = fold.end()
    hat = xhat1[...]
    small_out[0:1, :] = total(c_one * hat)
    small_out[1:2, :] = total(c_one)
    dx_ref[...] = gres[...] + norm_grad(hat, r_one, small[0:1, :], c_one)


def run_block(x_own, cot, live, col, row, length, wq, wo, wf, wp, small, qkv_bias, fc_bias):
    vm = pl.BlockSpec(memory_space=pltpu.VMEM)
    hbm = pl.BlockSpec(memory_space=pl.ANY)
    rows, wide = x_own.shape[0], wq.shape[1]
    hc = wide // 3
    group = 4 * rows
    vmem = pltpu.VMEM
    return pl.pallas_call(
        block_kernel,
        out_shape=(
            jax.ShapeDtypeStruct((rows, D), bf16),
            jax.ShapeDtypeStruct((rows, D), f32),
            jax.ShapeDtypeStruct((2, ROWS, HALF), bf16),
            jax.ShapeDtypeStruct((12, D), f32),
        ),
        in_specs=[vm] * 7 + [hbm] * 3 + [vm] * 3,
        out_specs=(vm,) * 4,
        scratch_shapes=[
            vmem((group, D), bf16),
            vmem((group, D), bf16),
            vmem((group, D), bf16),
            vmem((group, D), bf16),
            vmem((group, wide), bf16),
            vmem((hc // HD, group, group), bf16),
            vmem((group, group), f32),
            vmem((group, hc), bf16),
            vmem((4, group, D), bf16),
            vmem((4, 3, rows, D), bf16),
            vmem((4, rows, D), bf16),
            vmem(wo.shape, f32),
            vmem(wf.shape, f32),
            vmem(wp.shape, f32),
            vmem(wo.shape, bf16),
            vmem(wf.shape, bf16),
            vmem(wp.shape, bf16),
            vmem((group, D), f32),
            vmem((group, D), bf16),
            vmem((group, D), bf16),
            vmem((group, hc), bf16),
            vmem((group, wide), bf16),
            vmem((rows, D), f32),
            vmem((rows, D), f32),
            vmem((rows, D), f32),
            vmem((rows, D), f32),
            pltpu.SemaphoreType.DMA((32,)),
            pltpu.SemaphoreType.DMA((32,)),
            pltpu.SemaphoreType.DMA((3,)),
        ],
        compiler_params=pltpu.CompilerParams(collective_id=3, has_side_effects=True, vmem_limit_bytes=50 * 1024 * 1024),
    )(x_own, cot, live, col, row, length, wq, wo, wf, wp, small, qkv_bias, fc_bias)


def shards(block_input, cotangent, lengths, block_order, w_qkv, w_out, w_fc, w_proj, mom_qkv, mom_out, mom_fc, mom_proj, small_params, small_first, small_second):
    member = lax.axis_index("shard")
    rows = block_input.shape[0]
    hc = w_out.shape[0]
    offsets = jnp.arange(BLOCK, dtype=jnp.int32)
    places = (block_order[0][:, None] * BLOCK + offsets[None, :]).reshape(-1)
    own_places = lax.dynamic_slice_in_dim(places, member * rows, rows)
    live = (own_places < lengths[0]).astype(f32)[:, None]
    places = places.astype(f32)
    small = lax.optimization_barrier(small_params.astype(bf16)).astype(f32)

    def cols(row):
        return lax.dynamic_slice_in_dim(row, member * hc, hc)

    qkv_bias = jnp.concatenate([cols(small[4]), jnp.zeros((hc,), f32), cols(small[5])])[None]
    fc_bias = lax.dynamic_slice_in_dim(small[7:11], member, 1)
    wq = w_qkv.astype(bf16).reshape(D, -1)
    block_output, input_grad, parts, small_term = run_block(
        block_input, cotangent, live, places[:, None], places[None, :], lengths.astype(f32)[None], wq, w_out, w_fc, w_proj, small, qkv_bias, fc_bias
    )
    sums, grad_small = sum_over_groups(parts, small_term)
    sums = jnp.concatenate([sums[0], sums[1]], 1).astype(f32)
    grads = [sums[2 * D + hc :].T, sums[2 * D : 2 * D + hc], sums[:D], sums[D : 2 * D]]
    moms = [mom_qkv.reshape(D, -1), mom_out, mom_fc, mom_proj]
    new_moms = [momentum_decay * m + g for m, g in zip(moms, grads)]
    updates = [(g + momentum_decay * m).astype(bf16) for g, m in zip(grads, new_moms)]
    factors = muon_factors(updates)
    factors = jnp.concatenate([factors[:, 0], factors[:, 1]], 2)
    orth = [dot(factors[0], updates[0]), dot(updates[1], factors[1]), dot(factors[2], updates[2]), dot(updates[3], factors[3])]
    news = []
    for w, o, longest, rate in zip([w_qkv.reshape(D, -1), w_out, w_fc, w_proj], orth, [3 * D, D, FF, FF], [muon_rate, out_rate, muon_rate, muon_rate]):
        news.append(w * (1.0 - rate * muon_decay) - rate * 0.2 * math.sqrt(longest) * o)
    next_first = beta_one * small_first + (1.0 - beta_one) * grad_small
    next_second = beta_two * small_second + (1.0 - beta_two) * grad_small * grad_small
    first_hat = next_first / (1.0 - beta_one**STEP)
    second_hat = next_second / (1.0 - beta_two**STEP)
    next_small = small_params - adam_rate * first_hat / (jnp.sqrt(second_hat) + adam_eps)
    cube = w_qkv.shape
    return (block_output, input_grad, grads[0].reshape(cube), *grads[1:], grad_small, news[0].reshape(cube), *news[1:], new_moms[0].reshape(cube), *new_moms[1:], next_first, next_second, next_small, grad_small[11])


def solution(mesh):
    rows = P(("rep", "shard"), None)
    mats = (P(None, None, "shard"), P("shard", None), P(None, "shard"), P("shard", None))
    in_specs = (rows, rows, P("rep"), P("rep", None), *mats, *mats, P(), P(), P())
    out_specs = (rows, rows, *mats, P(), *mats, *mats, P(), P(), P(), P())
    return jax.shard_map(shards, mesh=mesh, in_specs=in_specs, out_specs=out_specs, check_vma=False)
```

```python
import math

import jax
import jax.numpy as jnp
from jax import lax
from jax.experimental import pallas as pl
from jax.experimental.pallas import tpu as pltpu
from jax.sharding import PartitionSpec as P

D = 768
HD = 64
FF = 3072
BLOCK = 128
STEP = 10
momentum_decay = 0.95
muon_rate = 0.15
out_rate = 0.75
muon_decay = 0.01
adam_rate = 0.4
beta_one = 0.9
beta_two = 0.999
adam_eps = 1e-08
norm_eps = 1e-05
poly_a = 3.4445
poly_b = -4.775
poly_c = 2.0315
masked_score = -1e30
bf16 = jnp.bfloat16
f32 = jnp.float32


def dot(left, right, dims=((1,), (0,))):
    return lax.dot_general(left, right, (dims, ((), ())), preferred_element_type=f32)


MESH = pl.DeviceIdType.MESH
HALF = 384


def place():
    rep = lax.axis_index("rep")
    return rep % 4, rep // 8, (rep // 4) % 2, lax.axis_index("shard")


def device(x, y, z, shard):
    return ((y * 2 + z) * 4 + x, shard)


class GroupSum:
    def __init__(self, sides, across, copy, here, total_rows, parts, out, got_one, got_two, got_z, pass_one, pass_two, mid):
        self.sides, self.across, self.copy, self.here = sides, across, copy, here
        self.parts, self.out, self.got, self.got_z = parts, out, (got_one, got_two), got_z
        self.passing, self.mid, self.ends = (pass_one, pass_two), mid, pass_two
        self.big, self.little = total_rows // 4, total_rows // 16
        self.cuts = (self.big // 2, (self.little // 2 + 15) // 16 * 16)

    @staticmethod
    def rows(start, size):
        return pl.ds(pl.multiple_of(start, 16), size)

    def reduce_start(self, step, ref, axis, k):
        p, left, right = self.sides[axis]
        n, cut, got = (self.big, self.little)[step], self.cuts[step], self.got[step].at[k]
        opp, nxt, prv = (p + 2) % 4, (p + 1) % 4, (p + 3) % 4
        rows, copy = self.rows, self.copy
        first = (
            copy(ref.at[rows(opp * n, cut), :], got.at[0, 0:cut, :], right),
            copy(ref.at[rows(opp * n + cut, n - cut), :], got.at[0, cut:n, :], left),
            copy(ref.at[rows(nxt * n + cut, n - cut), :], got.at[1, cut:n, :], right),
            copy(ref.at[rows(prv * n, cut), :], got.at[1, 0:cut, :], left),
        )
        return first, (p, left, right, nxt, prv, ref, n, cut, got, self.passing[step].at[k])

    def reduce_pass(self, state):
        first, (p, left, right, nxt, prv, ref, n, cut, got, passing) = state
        rows = self.rows
        first[0].wait_recv()
        passing[0:cut, :] = (ref[rows(nxt * n, cut), :].astype(f32) + got[0, 0:cut, :].astype(f32)).astype(bf16)
        second = [self.copy(passing.at[0:cut, :], got.at[2, 0:cut, :], right)]
        first[1].wait_recv()
        passing[cut:n, :] = (ref[rows(prv * n + cut, n - cut), :].astype(f32) + got[0, cut:n, :].astype(f32)).astype(bf16)
        second.append(self.copy(passing.at[cut:n, :], got.at[2, cut:n, :], left))
        return second

    def reduce_end(self, state, second, dst):
        first, (p, left, right, nxt, prv, ref, n, cut, got, passing) = state
        for c in (first[2], first[3], *second):
            c.wait_recv()
        dst[...] = (ref[self.rows(p * n, n), :].astype(f32) + got[1].astype(f32) + got[2].astype(f32)).astype(bf16)
        for c in (*first, *second):
            c.wait_send()

    def gather_start(self, step, ref, axis, base):
        p, left, right = self.sides[axis]
        n, cut = (self.big, self.little)[step], self.cuts[step]

        def send(chunk, head, target):
            spot = self.rows(base + chunk * n + (0 if head else cut), cut if head else n - cut)
            return self.copy(ref.at[spot, :], ref.at[spot, :], target)

        return (send(p, True, right), send(p, False, left), send(p, False, right), send(p, True, left)), (p, left, right, send)

    def gather_pass(self, state):
        first, (p, left, right, send) = state
        first[0].wait_recv()
        second = [send((p + 3) % 4, True, right)]
        first[1].wait_recv()
        second.append(send((p + 1) % 4, False, left))
        return second

    def gather_end(self, state, second):
        for c in (*state[0][2:], *second):
            c.wait_recv()
        for c in (*state[0], *second):
            c.wait_send()

    def one_start(self):
        self.state = [self.reduce_start(0, self.parts.at[k], "xy"[k], k) for k in range(2)]

    def one_pass(self):
        self.second = [self.reduce_pass(state) for state in self.state]

    def two_start(self):
        for k in range(2):
            self.reduce_end(self.state[k], self.second[k], self.mid.at[k])
        self.state = [self.reduce_start(1, self.mid.at[k], "yx"[k], k) for k in range(2)]

    two_pass = one_pass

    def z_start(self):
        for k in range(2):
            self.reduce_end(self.state[k], self.second[k], self.ends.at[2 + k])
        self.over = [self.copy(self.ends.at[2 + k], self.got_z.at[k], self.across) for k in range(2)]

    def back_start(self):
        x, y = self.here
        self.state = []
        for k in range(2):
            base = (x, y)[k] * self.big
            at = base + (y, x)[k] * self.little
            self.over[k].wait()
            self.out[k, self.rows(at, self.little), :] = (self.ends[2 + k].astype(f32) + self.got_z[k].astype(f32)).astype(bf16)
            self.state.append(self.gather_start(1, self.out.at[k], "yx"[k], base))

    def back_pass(self):
        self.second = [self.gather_pass(state) for state in self.state]

    def last_start(self):
        for k in range(2):
            self.gather_end(self.state[k], self.second[k])
        self.state = [self.gather_start(0, self.out.at[k], "xy"[k], 0) for k in range(2)]

    last_pass = back_pass

    def last_end(self):
        for k in range(2):
            self.gather_end(self.state[k], self.second[k])


def sum_scratch(total_rows):
    big, little = total_rows // 4, total_rows // 16
    return [
        pltpu.VMEM((2, 3, big, HALF), bf16),
        pltpu.VMEM((2, 3, little, HALF), bf16),
        pltpu.VMEM((2, little, HALF), bf16),
        pltpu.VMEM((2, big, HALF), bf16),
        pltpu.VMEM((4, little, HALF), bf16),
        pltpu.VMEM((2, big, HALF), bf16),
    ]


def make_gather(sides, copy):
    def start(axis, ref, base, n, cut, unit):
        p, left, right = sides[axis]

        def rows(chunk, first):
            at = base + chunk * n + (0 if first else cut)
            return pl.ds(pl.multiple_of(at, unit), cut if first else n - cut)

        def send(chunk, first, target):
            spot = rows(chunk, first)
            return copy(ref.at[spot, :], ref.at[spot, :], target)

        first = (send(p, True, right), send(p, False, left), send(p, False, right), send(p, True, left))
        return first, (p, left, right, send)

    def onward(state):
        first, (p, left, right, send) = state
        first[0].wait_recv()
        second = [send((p + 3) % 4, True, right)]
        first[1].wait_recv()
        second.append(send((p + 1) % 4, False, left))
        return second

    def end(state, second):
        for c in (*state[0][2:], *second):
            c.wait_recv()
        for c in (*state[0], *second):
            c.wait_send()

    def both(refs, orders, base, sizes, unit):
        for step in range(2):
            states = []
            for k in range(2):
                n, cut = sizes[step]
                states.append(start(orders[k][step], refs[k], base[k] if step == 0 else 0, n, cut, unit))
            seconds = [onward(state) for state in states]
            for state, second in zip(states, seconds):
                end(state, second)

    return both


def muon_kernel(u_qkv, u_out, u_fc, u_proj, q_all, piece, got, halves, gram, gram_low, poly, factor, factor_low, send, recv):
    x, y, z, shard = place()
    sides = {
        "x": (x, device((x + 3) % 4, y, z, shard), device((x + 1) % 4, y, z, shard)),
        "y": (y, device(x, (y + 3) % 4, z, shard), device(x, (y + 1) % 4, z, shard)),
    }
    others = [device(x, y, z, (shard + d) % 4) for d in (1, 2, 3)]
    sibling = device(x, y, z, shard + 1 - 2 * (shard % 2))
    barrier = pltpu.get_barrier_semaphore()
    partners = [*sides["x"][1:], *sides["y"][1:], *others]
    for partner in partners:
        pl.semaphore_signal(barrier, inc=1, device_id=partner, device_id_type=MESH)

    used = [0]

    def copy(src, dst, target):
        k = used[0]
        used[0] += 1
        c = pltpu.make_async_remote_copy(src_ref=src, dst_ref=dst, send_sem=send.at[k], recv_sem=recv.at[k], device_id=target, device_id_type=MESH)
        c.start()
        return c

    gather = make_gather(sides, copy)
    n = D // 16
    at = (pl.multiple_of((x * 4 + y) * n, 16), pl.multiple_of((y * 4 + x) * n, 16))
    over_cols, over_rows = ((1,), (1,)), ((0,), (0,))
    for k in range(2):
        cols = slice(k * HALF, k * HALF + HALF)
        pick = (lax.broadcasted_iota(jnp.int32, (D, n), 0) == lax.broadcasted_iota(jnp.int32, (D, n), 1) + at[k]).astype(f32).astype(bf16)
        for m, u in enumerate((u_qkv, u_out, u_fc, u_proj)):
            if m % 2 == 0:
                piece[m, k] = dot(u[pl.ds(at[k], n), :], u[cols, :], over_cols)
            else:
                own = dot(u[...], pick).astype(bf16)
                piece[m, k] = dot(own, u[:, cols], over_rows)
    pl.semaphore_wait(barrier, len(partners))
    sums = [copy(piece.at[(shard + d) % 4], got.at[d - 1], others[d - 1]) for d in (1, 2, 3)]
    for c in sums:
        c.wait_recv()
    for k in range(2):
        halves[k, pl.ds(at[k], n), :] = piece[shard, k] + got[0, k] + got[1, k] + got[2, k]
    orders = (("y", "x"), ("x", "y"))
    base = (x * 4 * n, y * 4 * n)
    gather([halves.at[0], halves.at[1]], orders, base, ((n, 24), (4 * n, 2 * n)), 8)
    for c in sums:
        c.wait_send()

    tile = 256
    blocks = D // tile

    def eye(r, width, first):
        return (lax.broadcasted_iota(jnp.int32, (tile, width), 0) + r * tile == lax.broadcasted_iota(jnp.int32, (tile, width), 1) + first).astype(f32)

    trace = jnp.zeros((1, 1), f32)
    for r in range(blocks):
        for k in range(2):
            part = halves[k, r * tile : (r + 1) * tile, :] * eye(r, HALF, k * HALF)
            trace = trace + jnp.sum(jnp.sum(part, axis=1, keepdims=True), axis=0, keepdims=True)
    inv = 1.0 / (jnp.sqrt(trace) + 1e-07)
    for r in range(blocks):
        spot = slice(r * tile, (r + 1) * tile)
        for k in range(2):
            cols = slice(k * HALF, k * HALF + HALF)
            g = halves[k, spot, :] * (inv * inv)
            gram[spot, cols] = g
            gram_low[0, spot, cols] = g.astype(bf16)

    for k in range(4):
        now, later = k % 2, (k + 1) % 2

        def poly_rows(r):
            spot = slice(r * tile, (r + 1) * tile)
            poly[spot, :] = (poly_b * gram[spot, :] + poly_c * dot(gram_low[now, spot, :], gram_low[now])).astype(bf16)

        def update_rows(r):
            spot = slice(r * tile, (r + 1) * tile)
            p = poly[spot, :]
            if k == 0:
                q = p.astype(f32) + poly_a * eye(r, D, 0)
            else:
                q = poly_a * factor[spot, :] + dot(p, factor_low[now])
            factor[spot, :] = q
            if k < 3:
                factor_low[later, spot, :] = q.astype(bf16)
                t = poly_a * gram[spot, :] + dot(p, gram_low[now])
                g = poly_a * t + dot(t.astype(bf16), poly[...])
                gram[spot, :] = g
                gram_low[later, spot, :] = g.astype(bf16)

        for r in range(blocks):
            poly_rows(r)
        for r in range(blocks):
            update_rows(r)
    for r in range(blocks):
        spot = slice(r * tile, (r + 1) * tile)
        for k in range(2):
            q_all[shard, k, spot, :] = (factor[spot, k * HALF : (k + 1) * HALF] * inv).astype(bf16)

    away = (shard + 2) % 4
    pieces = [copy(q_all.at[shard, k, pl.ds(at[k], n), :], q_all.at[shard, k, pl.ds(at[k], n), :], others[1]) for k in range(2)]
    near = copy(q_all.at[shard], q_all.at[shard], sibling)
    for c in pieces:
        c.wait_recv()
    gather([q_all.at[away, 0], q_all.at[away, 1]], orders, base, ((n, 32), (4 * n, 2 * n)), 16)
    far = copy(q_all.at[away], q_all.at[away], sibling)
    for c in (*pieces, near):
        c.wait_send()
    near.wait_recv()
    far.wait()


def muon_factors(updates):
    vm = pl.BlockSpec(memory_space=pltpu.VMEM)
    n = D // 16
    return pl.pallas_call(
        muon_kernel,
        out_shape=jax.ShapeDtypeStruct((4, 2, D, HALF), bf16),
        in_specs=[vm] * 4,
        out_specs=vm,
        scratch_shapes=[
            pltpu.VMEM((4, 2, n, HALF), f32),
            pltpu.VMEM((3, 2, n, HALF), f32),
            pltpu.VMEM((2, D, HALF), f32),
            pltpu.VMEM((D, D), f32),
            pltpu.VMEM((2, D, D), bf16),
            pltpu.VMEM((D, D), bf16),
            pltpu.VMEM((D, D), f32),
            pltpu.VMEM((2, D, D), bf16),
            pltpu.SemaphoreType.DMA((60,)),
            pltpu.SemaphoreType.DMA((60,)),
        ],
        compiler_params=pltpu.CompilerParams(collective_id=2, has_side_effects=True, vmem_limit_bytes=44 * 1024 * 1024),
    )(*updates)


def block_kernel(
    x_ref, cot_ref, live_ref, col_ref, row_ref, len_ref, wq, wo_hbm, wf_hbm, wp_hbm, small, qkv_bias, fc_bias,
    out_ref, dx_ref, sums_one, sums_two, small_out,
    nrm, mlow, nrm2, branch, mixed, probs, bias, head_out, part, got, passing, wo32, wf32, wp32, wo, wf, wp,
    gact, act, gpre, gheads, gmixed, xhat1, xhat2, resid, gres, parts_one, parts_two, *rest,
):
    one_refs, two_refs = rest[:6], rest[6:12]
    small_got, send, recv, small_send, small_recv, local = rest[12:]
    x, y, z, shard = place()
    sib = shard + 1 - 2 * (shard % 2)
    par = (shard + 2) % 4
    sibling, partner = device(x, y, z, sib), device(x, y, z, par)
    sides = {
        "x": (x, device((x + 3) % 4, y, z, shard), device((x + 1) % 4, y, z, shard)),
        "y": (y, device(x, (y + 3) % 4, z, shard), device(x, (y + 1) % 4, z, shard)),
    }
    across = device(x, y, 1 - z, shard)
    partners = (sibling, partner, *sides["x"][1:], *sides["y"][1:], across)
    barrier = pltpu.get_barrier_semaphore()
    for other in partners:
        pl.semaphore_signal(barrier, inc=1, device_id=other, device_id_type=MESH)
    loads = [pltpu.make_async_copy(src, dst, local.at[k]) for k, (src, dst) in enumerate(((wo_hbm, wo32), (wf_hbm, wf32), (wp_hbm, wp32)))]
    for load in loads:
        load.start()

    rows = BLOCK

    def chunk(index, size=rows, at=0):
        return pl.ds(pl.multiple_of(index * rows + at, 16), size)

    own, own_sib, own_par, own_ps = chunk(shard), chunk(sib), chunk(par), chunk((sib + 2) % 4)
    near = pl.multiple_of((shard // 2) * 256, 256)
    far = pl.multiple_of(256 - near, 256)
    used = [0]

    def copy(src, dst, target):
        k = used[0]
        used[0] += 1
        c = pltpu.make_async_remote_copy(src_ref=src, dst_ref=dst, send_sem=send.at[k], recv_sem=recv.at[k], device_id=target, device_id_type=MESH)
        c.start()
        return c

    sum_one = GroupSum(sides, across, copy, (x, y), 2 * D, parts_one, sums_one, *one_refs)
    sum_two = GroupSum(sides, across, copy, (x, y), D, parts_two, sums_two, *two_refs)
    steps = [
        sibling,
        partner,
        device(x + 1 - 2 * (x % 2), y, z, shard),
        device(3 - x, y, z, shard),
        device(x, y + 1 - 2 * (y % 2), z, shard),
        device(x, 3 - y, z, shard),
        across,
    ]
    small_copies = []

    def small_step():
        k = len(small_copies)
        if k > 0:
            small_copies[-1].wait()
            small_out[...] += small_got[k - 1]
        if k < len(steps):
            c = pltpu.make_async_remote_copy(src_ref=small_out, dst_ref=small_got.at[k], send_sem=small_send.at[k], recv_sem=small_recv.at[k], device_id=steps[k], device_id_type=MESH)
            c.start()
            small_copies.append(c)

    class Spread:
        def __init__(self, ref):
            self.ref = ref
            self.cross = [self.to(shard, 64 * i, partner) for i in range(2)]
            self.direct = copy(ref.at[own, :], ref.at[own, :], sibling)

        def to(self, index, at, target):
            spot = chunk(index, 64, at)
            return copy(self.ref.at[spot, :], self.ref.at[spot, :], target)

        def near(self):
            self.direct.wait_recv()

        def far(self):
            onward = []
            for i in range(2):
                self.cross[i].wait_recv()
                onward.append(self.to(par, 64 * i, sibling))
            for c in onward:
                c.wait_recv()
            for c in (*self.cross, self.direct, *onward):
                c.wait_send()

    class Fold:
        def __init__(self, k):
            self.k = k

        def start_far(self):
            self.a = copy(part.at[self.k, own_ps, :], got.at[self.k, 0], sibling)

        def start_near(self):
            self.b = copy(part.at[self.k, own_sib, :], got.at[self.k, 1], sibling)

        def cross(self):
            self.a.wait_recv()
            passing[self.k] = (part[self.k, own_par, :].astype(f32) + got[self.k, 0].astype(f32)).astype(bf16)
            self.c = copy(passing.at[self.k], got.at[self.k, 2], partner)

        def end(self):
            self.b.wait_recv()
            self.c.wait_recv()
            for c in (self.a, self.b, self.c):
                c.wait_send()
            return part[self.k, own, :].astype(f32) + got[self.k, 1].astype(f32) + got[self.k, 2].astype(f32)

    def norm(v):
        centred = v - jnp.mean(v, axis=-1, keepdims=True)
        r = lax.rsqrt(jnp.mean(centred * centred, axis=-1, keepdims=True) + norm_eps)
        return centred * r, r

    def norm_grad(xhat, r, gain, c):
        cg = c * gain
        return r * (cg - jnp.mean(cg, -1, keepdims=True) - xhat * jnp.mean(cg * xhat, -1, keepdims=True))

    def total(v):
        return jnp.sum(v, axis=0, keepdims=True)

    nt, tn = ((1,), (1,)), ((0,), (0,))
    hc = wq.shape[1] // 3
    heads = hc // HD
    scale = HD ** -0.5

    xf = x_ref[...].astype(f32)
    hat, r_one = norm(xf)
    xhat1[...] = hat
    nrm[own, :] = (hat * small[0:1, :] + small[1:2, :]).astype(bf16)
    mlow[own, :] = (cot_ref[...] * live_ref[...]).astype(bf16)
    pl.semaphore_wait(barrier, len(partners))
    go_nrm = Spread(nrm)
    go_mlow = Spread(mlow)
    bias[...] = jnp.where((row_ref[...] <= col_ref[...]) & (row_ref[...] < len_ref[...]), 0.0, masked_score)
    loads[0].wait()
    wo[...] = wo32[...].astype(bf16)

    def mix(at):
        spot = pl.ds(at, 256)
        mixed[spot, :] = (dot(nrm[spot, :], wq[...]) + qkv_bias[...]).astype(bf16)

    go_nrm.near()
    mix(near)
    go_nrm.far()
    mix(far)

    def head(h, part_of):
        lo = part_of * hc + h * HD
        return slice(lo, lo + HD)

    for h in range(heads):

        def attend(i, carry):
            spot = pl.ds(pl.multiple_of(i * 256, 256), 256)
            s = dot(mixed[spot, head(h, 0)], mixed[:, head(h, 1)], nt) * scale + bias[spot, :]
            e = jnp.exp(s - jnp.max(s, axis=-1, keepdims=True))
            p = (e * (1.0 / jnp.sum(e, axis=-1, keepdims=True))).astype(bf16)
            probs[h, spot, :] = p
            head_out[spot, head(h, 0)] = dot(p, mixed[:, head(h, 2)]).astype(bf16)
            return carry

        lax.fori_loop(0, 2, attend, 0)

    fold = Fold(0)
    part[0, pl.ds(far, 256), :] = dot(head_out[pl.ds(far, 256), :], wo[...]).astype(bf16)
    fold.start_far()
    part[0, pl.ds(near, 256), :] = dot(head_out[pl.ds(near, 256), :], wo[...]).astype(bf16)
    fold.start_near()
    fold.cross()
    go_mlow.near()
    go_mlow.far()
    loads[1].wait()
    wf[...] = wf32[...].astype(bf16)
    loads[2].wait()
    wp[...] = wp32[...].astype(bf16)

    def activation_grad(i, carry):
        spot = pl.ds(pl.multiple_of(i * 256, 256), 256)
        gact[spot, :] = dot(mlow[spot, :], wp[...], nt)
        return carry

    lax.fori_loop(0, 2, activation_grad, 0)
    res = x_ref[...].astype(f32) + fold.end() + small[6:7, :]
    resid[...] = res
    hat, r_two = norm(res)
    xhat2[...] = hat
    nrm2[own, :] = (hat * small[2:3, :] + small[3:4, :]).astype(bf16)
    go_nrm2 = Spread(nrm2)

    def feed(at):
        spot = pl.ds(at, 256)
        hidden = dot(nrm2[spot, :], wf[...]) + fc_bias[...]
        k = 0.7978845608028654
        square = hidden * hidden
        t = jnp.tanh(k * (hidden + 0.044715 * hidden * square))
        half = 0.5 * (1.0 + t)
        act[spot, :] = (hidden * half).astype(bf16)
        slope = half + 0.5 * hidden * (1.0 - t * t) * (k + (3 * 0.044715 * k) * square)
        gpre[spot, :] = (slope * gact[spot, :]).astype(bf16)

    go_nrm2.near()
    feed(near)
    go_nrm2.far()
    feed(far)
    fold = Fold(1)
    part[1, pl.ds(far, 256), :] = dot(gpre[pl.ds(far, 256), :], wf[...], nt).astype(bf16)
    fold.start_far()
    part[1, pl.ds(near, 256), :] = dot(gpre[pl.ds(near, 256), :], wf[...], nt).astype(bf16)
    fold.start_near()
    fold.cross()

    def grad_columns(parts, base, left, right, width):
        for c in range(left.shape[1] // width):
            value = dot(left[:, c * width : (c + 1) * width], right[...], tn).astype(bf16)
            spot = pl.ds(base + c * width, width)
            parts[0, spot, :] = value[:, :HALF]
            parts[1, spot, :] = value[:, HALF:]

    grad_columns(parts_one, 0, nrm2, gpre, 256)
    grad_columns(parts_one, D, act, mlow, 256)
    sum_one.one_start()
    small_out[11:12, :] = total(mlow[own, :].astype(f32))
    c_two = fold.end()
    hat = xhat2[...]
    small_out[2:3, :] = total(c_two * hat)
    small_out[3:4, :] = total(c_two)
    g = cot_ref[...] * live_ref[...] + norm_grad(hat, r_two, small[2:3, :], c_two)
    gres[...] = g
    branch[own, :] = g.astype(bf16)
    go_branch = Spread(branch)
    small_out[6:7, :] = total(branch[own, :].astype(f32))
    pre_sum = total(gpre[...].astype(f32))
    small_out[7:11, :] = jnp.where(lax.broadcasted_iota(jnp.int32, (4, D), 0) == shard, pre_sum, 0.0)

    def head_grads(at):
        spot = pl.ds(at, 256)
        gheads[spot, :] = dot(branch[spot, :], wo[...], nt).astype(bf16)

    fold_out = Fold(2)
    part[2, pl.ds(far, 256), :] = dot(act[pl.ds(far, 256), :], wp[...]).astype(bf16)
    fold_out.start_far()
    part[2, pl.ds(near, 256), :] = dot(act[pl.ds(near, 256), :], wp[...]).astype(bf16)
    fold_out.start_near()
    go_branch.near()
    head_grads(near)
    fold_out.cross()
    sum_one.one_pass()
    go_branch.far()
    head_grads(far)
    for h in range(heads):
        q, k, v = (mixed[:, head(h, i)] for i in range(3))
        gh = gheads[:, head(h, 0)]
        gmixed[:, head(h, 2)] = dot(gh, probs[h], tn).T.astype(bf16)

        def scores_grad(i, carry):
            spot = pl.ds(pl.multiple_of(i * 256, 256), 256)
            p = probs[h, spot, :].astype(f32)
            gp = dot(gheads[spot, head(h, 0)], mixed[:, head(h, 2)], nt)
            gs = (p * (gp - jnp.sum(p * gp, axis=-1, keepdims=True))).astype(bf16)
            probs[h, spot, :] = gs
            gmixed[spot, head(h, 0)] = (dot(gs, mixed[:, head(h, 1)]) * scale).astype(bf16)
            return carry

        lax.fori_loop(0, 2, scores_grad, 0)
        gmixed[:, head(h, 1)] = (dot(q, probs[h], tn).T * scale).astype(bf16)
        if h == heads - 1:
            sum_one.two_start()

    fold = Fold(3)
    part[3, pl.ds(far, 256), :] = dot(gmixed[pl.ds(far, 256), :], wq[...], nt).astype(bf16)
    fold.start_far()
    part[3, pl.ds(near, 256), :] = dot(gmixed[pl.ds(near, 256), :], wq[...], nt).astype(bf16)
    fold.start_near()
    grad_columns(parts_two, 0, head_out, branch, hc)
    grad_columns(parts_two, hc, gmixed, nrm, hc)
    sum_two.one_start()
    sum_one.two_pass()
    fold.cross()
    mixed_sum = total(gmixed[...].astype(f32))
    spread_out = (lax.broadcasted_iota(jnp.int32, (hc, D), 0) + shard * hc == lax.broadcasted_iota(jnp.int32, (hc, D), 1)).astype(f32)
    for row, lo in ((4, 0), (5, 2 * hc)):
        small_out[row : row + 1, :] = jnp.dot(mixed_sum[:, lo : lo + hc], spread_out, precision=lax.Precision.HIGHEST, preferred_element_type=f32)
    out_ref[...] = ((resid[...] + fold_out.end() + small[11:12, :]) * live_ref[...]).astype(bf16)
    sum_one.z_start()
    sum_two.one_pass()
    c_one = fold.end()
    hat = xhat1[...]
    small_out[0:1, :] = total(c_one * hat)
    small_out[1:2, :] = total(c_one)
    small_step()
    dx_ref[...] = gres[...] + norm_grad(hat, r_one, small[0:1, :], c_one)
    sum_one.back_start()
    sum_two.two_start()
    small_step()
    sum_one.back_pass()
    sum_two.two_pass()
    sum_one.last_start()
    small_step()
    sum_two.z_start()
    small_step()
    sum_one.last_pass()
    sum_two.back_start()
    small_step()
    sum_two.back_pass()
    sum_two.last_start()
    small_step()
    sum_one.last_end()
    sum_two.last_pass()
    small_step()
    sum_two.last_end()
    small_step()


def run_block(x_own, cot, live, col, row, length, wq, wo, wf, wp, small, qkv_bias, fc_bias):
    vm = pl.BlockSpec(memory_space=pltpu.VMEM)
    hbm = pl.BlockSpec(memory_space=pl.ANY)
    rows, wide = x_own.shape[0], wq.shape[1]
    hc = wide // 3
    group = 4 * rows
    vmem = pltpu.VMEM
    return pl.pallas_call(
        block_kernel,
        out_shape=(
            jax.ShapeDtypeStruct((rows, D), bf16),
            jax.ShapeDtypeStruct((rows, D), f32),
            jax.ShapeDtypeStruct((2, 2 * D, HALF), bf16),
            jax.ShapeDtypeStruct((2, D, HALF), bf16),
            jax.ShapeDtypeStruct((12, D), f32),
        ),
        in_specs=[vm] * 7 + [hbm] * 3 + [vm] * 3,
        out_specs=(vm,) * 5,
        scratch_shapes=[
            vmem((group, D), bf16),
            vmem((group, D), bf16),
            vmem((group, D), bf16),
            vmem((group, D), bf16),
            vmem((group, wide), bf16),
            vmem((hc // HD, group, group), bf16),
            vmem((group, group), f32),
            vmem((group, hc), bf16),
            vmem((4, group, D), bf16),
            vmem((4, 3, rows, D), bf16),
            vmem((4, rows, D), bf16),
            vmem(wo.shape, f32),
            vmem(wf.shape, f32),
            vmem(wp.shape, f32),
            vmem(wo.shape, bf16),
            vmem(wf.shape, bf16),
            vmem(wp.shape, bf16),
            vmem((group, D), f32),
            vmem((group, D), bf16),
            vmem((group, D), bf16),
            vmem((group, hc), bf16),
            vmem((group, wide), bf16),
            vmem((rows, D), f32),
            vmem((rows, D), f32),
            vmem((rows, D), f32),
            vmem((rows, D), f32),
            vmem((2, 2 * D, HALF), bf16),
            vmem((2, D, HALF), bf16),
            *sum_scratch(2 * D),
            *sum_scratch(D),
            vmem((7, 12, D), f32),
            pltpu.SemaphoreType.DMA((140,)),
            pltpu.SemaphoreType.DMA((140,)),
            pltpu.SemaphoreType.DMA((7,)),
            pltpu.SemaphoreType.DMA((7,)),
            pltpu.SemaphoreType.DMA((3,)),
        ],
        compiler_params=pltpu.CompilerParams(collective_id=3, has_side_effects=True, vmem_limit_bytes=50 * 1024 * 1024),
    )(x_own, cot, live, col, row, length, wq, wo, wf, wp, small, qkv_bias, fc_bias)


def shards(block_input, cotangent, lengths, block_order, w_qkv, w_out, w_fc, w_proj, mom_qkv, mom_out, mom_fc, mom_proj, small_params, small_first, small_second):
    member = lax.axis_index("shard")
    rows = block_input.shape[0]
    hc = w_out.shape[0]
    offsets = jnp.arange(BLOCK, dtype=jnp.int32)
    places = (block_order[0][:, None] * BLOCK + offsets[None, :]).reshape(-1)
    own_places = lax.dynamic_slice_in_dim(places, member * rows, rows)
    live = (own_places < lengths[0]).astype(f32)[:, None]
    places = places.astype(f32)
    small = lax.optimization_barrier(small_params.astype(bf16)).astype(f32)

    def cols(row):
        return lax.dynamic_slice_in_dim(row, member * hc, hc)

    qkv_bias = jnp.concatenate([cols(small[4]), jnp.zeros((hc,), f32), cols(small[5])])[None]
    fc_bias = lax.dynamic_slice_in_dim(small[7:11], member, 1)
    wq = w_qkv.astype(bf16).reshape(D, -1)
    block_output, input_grad, sums_one, sums_two, grad_small = run_block(
        block_input, cotangent, live, places[:, None], places[None, :], lengths.astype(f32)[None], wq, w_out, w_fc, w_proj, small, qkv_bias, fc_bias
    )
    one = jnp.concatenate([sums_one[0], sums_one[1]], 1).astype(f32)
    two = jnp.concatenate([sums_two[0], sums_two[1]], 1).astype(f32)
    grads = [two[hc:].T, two[:hc], one[:D], one[D:]]
    moms = [mom_qkv.reshape(D, -1), mom_out, mom_fc, mom_proj]
    new_moms = [momentum_decay * m + g for m, g in zip(moms, grads)]
    updates = [(g + momentum_decay * m).astype(bf16) for g, m in zip(grads, new_moms)]
    factors = muon_factors(updates)
    factors = jnp.concatenate([factors[:, 0], factors[:, 1]], 2)
    orth = [dot(factors[0], updates[0]), dot(updates[1], factors[1]), dot(factors[2], updates[2]), dot(updates[3], factors[3])]
    news = []
    for w, o, longest, rate in zip([w_qkv.reshape(D, -1), w_out, w_fc, w_proj], orth, [3 * D, D, FF, FF], [muon_rate, out_rate, muon_rate, muon_rate]):
        news.append(w * (1.0 - rate * muon_decay) - rate * 0.2 * math.sqrt(longest) * o)
    next_first = beta_one * small_first + (1.0 - beta_one) * grad_small
    next_second = beta_two * small_second + (1.0 - beta_two) * grad_small * grad_small
    first_hat = next_first / (1.0 - beta_one**STEP)
    second_hat = next_second / (1.0 - beta_two**STEP)
    next_small = small_params - adam_rate * first_hat / (jnp.sqrt(second_hat) + adam_eps)
    cube = w_qkv.shape
    return (block_output, input_grad, grads[0].reshape(cube), *grads[1:], grad_small, news[0].reshape(cube), *news[1:], new_moms[0].reshape(cube), *new_moms[1:], next_first, next_second, next_small, grad_small[11])


def solution(mesh):
    rows = P(("rep", "shard"), None)
    mats = (P(None, None, "shard"), P("shard", None), P(None, "shard"), P("shard", None))
    in_specs = (rows, rows, P("rep"), P("rep", None), *mats, *mats, P(), P(), P())
    out_specs = (rows, rows, *mats, P(), *mats, *mats, P(), P(), P(), P())
    return jax.shard_map(shards, mesh=mesh, in_specs=in_specs, out_specs=out_specs, check_vma=False)
```

```python
import math

import jax
import jax.numpy as jnp
from jax import lax
from jax.experimental import pallas as pl
from jax.experimental.pallas import tpu as pltpu
from jax.sharding import PartitionSpec as P

D = 768
HD = 64
FF = 3072
BLOCK = 128
STEP = 10
momentum_decay = 0.95
muon_rate = 0.15
out_rate = 0.75
muon_decay = 0.01
adam_rate = 0.4
beta_one = 0.9
beta_two = 0.999
adam_eps = 1e-08
norm_eps = 1e-05
poly_a = 3.4445
poly_b = -4.775
poly_c = 2.0315
masked_score = -1e30
bf16 = jnp.bfloat16
f32 = jnp.float32


def dot(left, right, dims=((1,), (0,))):
    return lax.dot_general(left, right, (dims, ((), ())), preferred_element_type=f32)


MESH = pl.DeviceIdType.MESH
HALF = 384


def place():
    rep = lax.axis_index("rep")
    return rep % 4, rep // 8, (rep // 4) % 2, lax.axis_index("shard")


def device(x, y, z, shard):
    return ((y * 2 + z) * 4 + x, shard)


class GroupSum:
    def __init__(self, sides, across, copy, here, total_rows, parts, out, got_one, got_two, got_z, pass_one, pass_two, mid):
        self.sides, self.across, self.copy, self.here = sides, across, copy, here
        self.parts, self.out, self.got, self.got_z = parts, out, (got_one, got_two), got_z
        self.passing, self.mid, self.ends = (pass_one, pass_two), mid, pass_two
        self.big, self.little = total_rows // 4, total_rows // 16
        self.cuts = (self.big // 2, (self.little // 2 + 15) // 16 * 16)

    @staticmethod
    def rows(start, size):
        return pl.ds(pl.multiple_of(start, 16), size)

    def reduce_start(self, step, ref, axis, k):
        p, left, right = self.sides[axis]
        n, cut, got = (self.big, self.little)[step], self.cuts[step], self.got[step].at[k]
        opp, nxt, prv = (p + 2) % 4, (p + 1) % 4, (p + 3) % 4
        rows, copy = self.rows, self.copy
        first = (
            copy(ref.at[rows(opp * n, cut), :], got.at[0, 0:cut, :], right),
            copy(ref.at[rows(opp * n + cut, n - cut), :], got.at[0, cut:n, :], left),
            copy(ref.at[rows(nxt * n + cut, n - cut), :], got.at[1, cut:n, :], right),
            copy(ref.at[rows(prv * n, cut), :], got.at[1, 0:cut, :], left),
        )
        return first, (p, left, right, nxt, prv, ref, n, cut, got, self.passing[step].at[k])

    def reduce_pass(self, state):
        first, (p, left, right, nxt, prv, ref, n, cut, got, passing) = state
        rows = self.rows
        first[0].wait_recv()
        passing[0:cut, :] = (ref[rows(nxt * n, cut), :].astype(f32) + got[0, 0:cut, :].astype(f32)).astype(bf16)
        second = [self.copy(passing.at[0:cut, :], got.at[2, 0:cut, :], right)]
        first[1].wait_recv()
        passing[cut:n, :] = (ref[rows(prv * n + cut, n - cut), :].astype(f32) + got[0, cut:n, :].astype(f32)).astype(bf16)
        second.append(self.copy(passing.at[cut:n, :], got.at[2, cut:n, :], left))
        return second

    def reduce_end(self, state, second, dst):
        first, (p, left, right, nxt, prv, ref, n, cut, got, passing) = state
        for c in (first[2], first[3], *second):
            c.wait_recv()
        dst[...] = (ref[self.rows(p * n, n), :].astype(f32) + got[1].astype(f32) + got[2].astype(f32)).astype(bf16)
        for c in (*first, *second):
            c.wait_send()

    def gather_start(self, step, ref, axis, base):
        p, left, right = self.sides[axis]
        n, cut = (self.big, self.little)[step], self.cuts[step]

        def send(chunk, head, target):
            spot = self.rows(base + chunk * n + (0 if head else cut), cut if head else n - cut)
            return self.copy(ref.at[spot, :], ref.at[spot, :], target)

        return (send(p, True, right), send(p, False, left), send(p, False, right), send(p, True, left)), (p, left, right, send)

    def gather_pass(self, state):
        first, (p, left, right, send) = state
        first[0].wait_recv()
        second = [send((p + 3) % 4, True, right)]
        first[1].wait_recv()
        second.append(send((p + 1) % 4, False, left))
        return second

    def gather_end(self, state, second):
        for c in (*state[0][2:], *second):
            c.wait_recv()
        for c in (*state[0], *second):
            c.wait_send()

    def one_start(self):
        self.state = [self.reduce_start(0, self.parts.at[k], "xy"[k], k) for k in range(2)]

    def one_pass(self):
        self.second = [self.reduce_pass(state) for state in self.state]

    def two_start(self):
        for k in range(2):
            self.reduce_end(self.state[k], self.second[k], self.mid.at[k])
        self.state = [self.reduce_start(1, self.mid.at[k], "yx"[k], k) for k in range(2)]

    two_pass = one_pass

    def z_start(self):
        for k in range(2):
            self.reduce_end(self.state[k], self.second[k], self.ends.at[2 + k])
        self.over = [self.copy(self.ends.at[2 + k], self.got_z.at[k], self.across) for k in range(2)]

    def back_start(self):
        x, y = self.here
        self.state = []
        for k in range(2):
            base = (x, y)[k] * self.big
            at = base + (y, x)[k] * self.little
            self.over[k].wait()
            self.out[k, self.rows(at, self.little), :] = (self.ends[2 + k].astype(f32) + self.got_z[k].astype(f32)).astype(bf16)
            self.state.append(self.gather_start(1, self.out.at[k], "yx"[k], base))

    def back_pass(self):
        self.second = [self.gather_pass(state) for state in self.state]

    def last_start(self):
        for k in range(2):
            self.gather_end(self.state[k], self.second[k])
        self.state = [self.gather_start(0, self.out.at[k], "xy"[k], 0) for k in range(2)]

    last_pass = back_pass

    def last_end(self):
        for k in range(2):
            self.gather_end(self.state[k], self.second[k])


def sum_scratch(total_rows):
    big, little = total_rows // 4, total_rows // 16
    return [
        pltpu.VMEM((2, 3, big, HALF), bf16),
        pltpu.VMEM((2, 3, little, HALF), bf16),
        pltpu.VMEM((2, little, HALF), bf16),
        pltpu.VMEM((2, big, HALF), bf16),
        pltpu.VMEM((4, little, HALF), bf16),
        pltpu.VMEM((2, big, HALF), bf16),
    ]


def make_gather(sides, copy):
    def start(axis, ref, base, n, cut, unit):
        p, left, right = sides[axis]

        def rows(chunk, first):
            at = base + chunk * n + (0 if first else cut)
            return pl.ds(pl.multiple_of(at, unit), cut if first else n - cut)

        def send(chunk, first, target):
            spot = rows(chunk, first)
            return copy(ref.at[spot, :], ref.at[spot, :], target)

        first = (send(p, True, right), send(p, False, left), send(p, False, right), send(p, True, left))
        return first, (p, left, right, send)

    def onward(state):
        first, (p, left, right, send) = state
        first[0].wait_recv()
        second = [send((p + 3) % 4, True, right)]
        first[1].wait_recv()
        second.append(send((p + 1) % 4, False, left))
        return second

    def end(state, second):
        for c in (*state[0][2:], *second):
            c.wait_recv()
        for c in (*state[0], *second):
            c.wait_send()

    def both(refs, orders, base, sizes, unit):
        for step in range(2):
            states = []
            for k in range(2):
                n, cut = sizes[step]
                states.append(start(orders[k][step], refs[k], base[k] if step == 0 else 0, n, cut, unit))
            seconds = [onward(state) for state in states]
            for state, second in zip(states, seconds):
                end(state, second)

    return both


def orth_factors(here, sides, sibling, others, copy, at, piece, got, halves, gram, gram_low, poly, factor, factor_low, q_all):
    x, y, z, shard = here
    gather = make_gather(sides, copy)
    n = D // 16
    sums = [copy(piece.at[(shard + d) % 4], got.at[d - 1], others[d - 1]) for d in (1, 2, 3)]
    for c in sums:
        c.wait_recv()
    for k in range(2):
        halves[k, pl.ds(at[k], n), :] = piece[shard, k] + got[0, k] + got[1, k] + got[2, k]
    orders = (("y", "x"), ("x", "y"))
    base = (x * 4 * n, y * 4 * n)
    gather([halves.at[0], halves.at[1]], orders, base, ((n, 24), (4 * n, 2 * n)), 8)
    for c in sums:
        c.wait_send()

    tile = 256
    blocks = D // tile

    def eye(r, width, first):
        return (lax.broadcasted_iota(jnp.int32, (tile, width), 0) + r * tile == lax.broadcasted_iota(jnp.int32, (tile, width), 1) + first).astype(f32)

    trace = jnp.zeros((1, 1), f32)
    for r in range(blocks):
        for k in range(2):
            part = halves[k, r * tile : (r + 1) * tile, :] * eye(r, HALF, k * HALF)
            trace = trace + jnp.sum(jnp.sum(part, axis=1, keepdims=True), axis=0, keepdims=True)
    inv = 1.0 / (jnp.sqrt(trace) + 1e-07)
    for r in range(blocks):
        spot = slice(r * tile, (r + 1) * tile)
        for k in range(2):
            cols = slice(k * HALF, k * HALF + HALF)
            g = halves[k, spot, :] * (inv * inv)
            gram[spot, cols] = g
            gram_low[0, spot, cols] = g.astype(bf16)

    for k in range(4):
        now, later = k % 2, (k + 1) % 2

        def poly_rows(r):
            spot = slice(r * tile, (r + 1) * tile)
            poly[spot, :] = (poly_b * gram[spot, :] + poly_c * dot(gram_low[now, spot, :], gram_low[now])).astype(bf16)

        def update_rows(r):
            spot = slice(r * tile, (r + 1) * tile)
            p = poly[spot, :]
            if k == 0:
                q = p.astype(f32) + poly_a * eye(r, D, 0)
            else:
                q = poly_a * factor[spot, :] + dot(p, factor_low[now])
            factor[spot, :] = q
            if k < 3:
                factor_low[later, spot, :] = q.astype(bf16)
                t = poly_a * gram[spot, :] + dot(p, gram_low[now])
                g = poly_a * t + dot(t.astype(bf16), poly[...])
                gram[spot, :] = g
                gram_low[later, spot, :] = g.astype(bf16)

        for r in range(blocks):
            poly_rows(r)
        for r in range(blocks):
            update_rows(r)
    for r in range(blocks):
        spot = slice(r * tile, (r + 1) * tile)
        for k in range(2):
            q_all[shard, k, spot, :] = (factor[spot, k * HALF : (k + 1) * HALF] * inv).astype(bf16)

    away = (shard + 2) % 4
    pieces = [copy(q_all.at[shard, k, pl.ds(at[k], n), :], q_all.at[shard, k, pl.ds(at[k], n), :], others[1]) for k in range(2)]
    near = copy(q_all.at[shard], q_all.at[shard], sibling)
    for c in pieces:
        c.wait_recv()
    gather([q_all.at[away, 0], q_all.at[away, 1]], orders, base, ((n, 32), (4 * n, 2 * n)), 16)
    far = copy(q_all.at[away], q_all.at[away], sibling)
    for c in (*pieces, near):
        c.wait_send()
    near.wait_recv()
    far.wait()


def block_kernel(
    x_ref, cot_ref, live_ref, col_ref, row_ref, len_ref, wq, wo_hbm, wf_hbm, wp_hbm, mq_hbm, mo_hbm, mf_hbm, mp_hbm, small, qkv_bias, fc_bias,
    out_ref, dx_ref, sums_one, sums_two, small_out, q_all,
    nrm, mlow, nrm2, branch, mixed, probs, bias, head_out, part, got, passing, wo32, wf32, wp32, wo, wf, wp,
    gact, act, gpre, gheads, gmixed, xhat1, xhat2, resid, gres, parts_one, parts_two, *rest,
):
    one_refs, two_refs = rest[:6], rest[6:12]
    momq, uq, piece, gram_got, halves, gram_low, poly, factor_low = rest[12:20]
    small_got, send, recv, small_send, small_recv, local = rest[20:]
    x, y, z, shard = place()
    sib = shard + 1 - 2 * (shard % 2)
    par = (shard + 2) % 4
    sibling, partner = device(x, y, z, sib), device(x, y, z, par)
    sides = {
        "x": (x, device((x + 3) % 4, y, z, shard), device((x + 1) % 4, y, z, shard)),
        "y": (y, device(x, (y + 3) % 4, z, shard), device(x, (y + 1) % 4, z, shard)),
    }
    across = device(x, y, 1 - z, shard)
    partners = (sibling, partner, *sides["x"][1:], *sides["y"][1:], across)
    barrier = pltpu.get_barrier_semaphore()
    for other in partners:
        pl.semaphore_signal(barrier, inc=1, device_id=other, device_id_type=MESH)
    loads = [pltpu.make_async_copy(src, dst, local.at[k]) for k, (src, dst) in enumerate(((wo_hbm, wo32), (wf_hbm, wf32), (wp_hbm, wp32)))]
    for load in loads:
        load.start()

    rows = BLOCK

    def chunk(index, size=rows, at=0):
        return pl.ds(pl.multiple_of(index * rows + at, 16), size)

    own, own_sib, own_par, own_ps = chunk(shard), chunk(sib), chunk(par), chunk((sib + 2) % 4)
    near = pl.multiple_of((shard // 2) * 256, 256)
    far = pl.multiple_of(256 - near, 256)
    used = [0]

    def copy(src, dst, target):
        k = used[0]
        used[0] += 1
        c = pltpu.make_async_remote_copy(src_ref=src, dst_ref=dst, send_sem=send.at[k], recv_sem=recv.at[k], device_id=target, device_id_type=MESH)
        c.start()
        return c

    sum_one = GroupSum(sides, across, copy, (x, y), 2 * D, parts_one, sums_one, *one_refs)
    sum_two = GroupSum(sides, across, copy, (x, y), D, parts_two, sums_two, *two_refs)
    steps = [
        sibling,
        partner,
        device(x + 1 - 2 * (x % 2), y, z, shard),
        device(3 - x, y, z, shard),
        device(x, y + 1 - 2 * (y % 2), z, shard),
        device(x, 3 - y, z, shard),
        across,
    ]
    small_copies = []

    def small_step():
        k = len(small_copies)
        if k > 0:
            small_copies[-1].wait()
            small_out[...] += small_got[k - 1]
        if k < len(steps):
            c = pltpu.make_async_remote_copy(src_ref=small_out, dst_ref=small_got.at[k], send_sem=small_send.at[k], recv_sem=small_recv.at[k], device_id=steps[k], device_id_type=MESH)
            c.start()
            small_copies.append(c)

    class Spread:
        def __init__(self, ref):
            self.ref = ref
            self.cross = [self.to(shard, 64 * i, partner) for i in range(2)]
            self.direct = copy(ref.at[own, :], ref.at[own, :], sibling)

        def to(self, index, at, target):
            spot = chunk(index, 64, at)
            return copy(self.ref.at[spot, :], self.ref.at[spot, :], target)

        def near(self):
            self.direct.wait_recv()

        def far(self):
            onward = []
            for i in range(2):
                self.cross[i].wait_recv()
                onward.append(self.to(par, 64 * i, sibling))
            for c in onward:
                c.wait_recv()
            for c in (*self.cross, self.direct, *onward):
                c.wait_send()

    class Fold:
        def __init__(self, k):
            self.k = k

        def start_far(self):
            self.a = copy(part.at[self.k, own_ps, :], got.at[self.k, 0], sibling)

        def start_near(self):
            self.b = copy(part.at[self.k, own_sib, :], got.at[self.k, 1], sibling)

        def cross(self):
            self.a.wait_recv()
            passing[self.k] = (part[self.k, own_par, :].astype(f32) + got[self.k, 0].astype(f32)).astype(bf16)
            self.c = copy(passing.at[self.k], got.at[self.k, 2], partner)

        def end(self):
            self.b.wait_recv()
            self.c.wait_recv()
            for c in (self.a, self.b, self.c):
                c.wait_send()
            return part[self.k, own, :].astype(f32) + got[self.k, 1].astype(f32) + got[self.k, 2].astype(f32)

    def norm(v):
        centred = v - jnp.mean(v, axis=-1, keepdims=True)
        r = lax.rsqrt(jnp.mean(centred * centred, axis=-1, keepdims=True) + norm_eps)
        return centred * r, r

    def norm_grad(xhat, r, gain, c):
        cg = c * gain
        return r * (cg - jnp.mean(cg, -1, keepdims=True) - xhat * jnp.mean(cg * xhat, -1, keepdims=True))

    def total(v):
        return jnp.sum(v, axis=0, keepdims=True)

    nt, tn = ((1,), (1,)), ((0,), (0,))
    hc = wq.shape[1] // 3
    heads = hc // HD
    scale = HD ** -0.5

    xf = x_ref[...].astype(f32)
    hat, r_one = norm(xf)
    xhat1[...] = hat
    nrm[own, :] = (hat * small[0:1, :] + small[1:2, :]).astype(bf16)
    mlow[own, :] = (cot_ref[...] * live_ref[...]).astype(bf16)
    pl.semaphore_wait(barrier, len(partners))
    go_nrm = Spread(nrm)
    go_mlow = Spread(mlow)
    bias[...] = jnp.where((row_ref[...] <= col_ref[...]) & (row_ref[...] < len_ref[...]), 0.0, masked_score)
    loads[0].wait()
    wo[...] = wo32[...].astype(bf16)

    def mix(at):
        spot = pl.ds(at, 256)
        mixed[spot, :] = (dot(nrm[spot, :], wq[...]) + qkv_bias[...]).astype(bf16)

    go_nrm.near()
    mix(near)
    go_nrm.far()
    mix(far)

    def head(h, part_of):
        lo = part_of * hc + h * HD
        return slice(lo, lo + HD)

    for h in range(heads):

        def attend(i, carry):
            spot = pl.ds(pl.multiple_of(i * 256, 256), 256)
            s = dot(mixed[spot, head(h, 0)], mixed[:, head(h, 1)], nt) * scale + bias[spot, :]
            e = jnp.exp(s - jnp.max(s, axis=-1, keepdims=True))
            p = (e * (1.0 / jnp.sum(e, axis=-1, keepdims=True))).astype(bf16)
            probs[h, spot, :] = p
            head_out[spot, head(h, 0)] = dot(p, mixed[:, head(h, 2)]).astype(bf16)
            return carry

        lax.fori_loop(0, 2, attend, 0)

    fold = Fold(0)
    part[0, pl.ds(far, 256), :] = dot(head_out[pl.ds(far, 256), :], wo[...]).astype(bf16)
    fold.start_far()
    part[0, pl.ds(near, 256), :] = dot(head_out[pl.ds(near, 256), :], wo[...]).astype(bf16)
    fold.start_near()
    fold.cross()
    go_mlow.near()
    go_mlow.far()
    loads[1].wait()
    wf[...] = wf32[...].astype(bf16)
    loads[2].wait()
    wp[...] = wp32[...].astype(bf16)

    mom_loads = [pltpu.make_async_copy(src, dst, local.at[3 + k]) for k, (src, dst) in enumerate(((mo_hbm, wo32), (mf_hbm, wf32), (mp_hbm, wp32), (mq_hbm, momq)))]
    for load in mom_loads:
        load.start()

    def activation_grad(i, carry):
        spot = pl.ds(pl.multiple_of(i * 256, 256), 256)
        gact[spot, :] = dot(mlow[spot, :], wp[...], nt)
        return carry

    lax.fori_loop(0, 2, activation_grad, 0)
    res = x_ref[...].astype(f32) + fold.end() + small[6:7, :]
    resid[...] = res
    hat, r_two = norm(res)
    xhat2[...] = hat
    nrm2[own, :] = (hat * small[2:3, :] + small[3:4, :]).astype(bf16)
    go_nrm2 = Spread(nrm2)

    def feed(at):
        spot = pl.ds(at, 256)
        hidden = dot(nrm2[spot, :], wf[...]) + fc_bias[...]
        k = 0.7978845608028654
        square = hidden * hidden
        t = jnp.tanh(k * (hidden + 0.044715 * hidden * square))
        half = 0.5 * (1.0 + t)
        act[spot, :] = (hidden * half).astype(bf16)
        slope = half + 0.5 * hidden * (1.0 - t * t) * (k + (3 * 0.044715 * k) * square)
        gpre[spot, :] = (slope * gact[spot, :]).astype(bf16)

    go_nrm2.near()
    feed(near)
    go_nrm2.far()
    feed(far)
    fold = Fold(1)
    part[1, pl.ds(far, 256), :] = dot(gpre[pl.ds(far, 256), :], wf[...], nt).astype(bf16)
    fold.start_far()
    part[1, pl.ds(near, 256), :] = dot(gpre[pl.ds(near, 256), :], wf[...], nt).astype(bf16)
    fold.start_near()
    fold.cross()

    def grad_columns(parts, base, left, right, width):
        for c in range(left.shape[1] // width):
            value = dot(left[:, c * width : (c + 1) * width], right[...], tn).astype(bf16)
            spot = pl.ds(base + c * width, width)
            parts[0, spot, :] = value[:, :HALF]
            parts[1, spot, :] = value[:, HALF:]

    grad_columns(parts_one, 0, nrm2, gpre, 256)
    grad_columns(parts_one, D, act, mlow, 256)
    sum_one.one_start()
    small_out[11:12, :] = total(mlow[own, :].astype(f32))
    c_two = fold.end()
    hat = xhat2[...]
    small_out[2:3, :] = total(c_two * hat)
    small_out[3:4, :] = total(c_two)
    g = cot_ref[...] * live_ref[...] + norm_grad(hat, r_two, small[2:3, :], c_two)
    gres[...] = g
    branch[own, :] = g.astype(bf16)
    go_branch = Spread(branch)
    sum_one.one_pass()
    small_out[6:7, :] = total(branch[own, :].astype(f32))
    pre_sum = total(gpre[...].astype(f32))
    small_out[7:11, :] = jnp.where(lax.broadcasted_iota(jnp.int32, (4, D), 0) == shard, pre_sum, 0.0)

    def head_grads(at):
        spot = pl.ds(at, 256)
        gheads[spot, :] = dot(branch[spot, :], wo[...], nt).astype(bf16)

    fold_out = Fold(2)
    part[2, pl.ds(far, 256), :] = dot(act[pl.ds(far, 256), :], wp[...]).astype(bf16)
    fold_out.start_far()
    part[2, pl.ds(near, 256), :] = dot(act[pl.ds(near, 256), :], wp[...]).astype(bf16)
    fold_out.start_near()
    go_branch.near()
    head_grads(near)
    go_branch.far()
    head_grads(far)
    fold_out.cross()
    sum_one.two_start()
    for h in range(heads):
        q, k, v = (mixed[:, head(h, i)] for i in range(3))
        gh = gheads[:, head(h, 0)]
        gmixed[:, head(h, 2)] = dot(gh, probs[h], tn).T.astype(bf16)

        def scores_grad(i, carry):
            spot = pl.ds(pl.multiple_of(i * 256, 256), 256)
            p = probs[h, spot, :].astype(f32)
            gp = dot(gheads[spot, head(h, 0)], mixed[:, head(h, 2)], nt)
            gs = (p * (gp - jnp.sum(p * gp, axis=-1, keepdims=True))).astype(bf16)
            probs[h, spot, :] = gs
            gmixed[spot, head(h, 0)] = (dot(gs, mixed[:, head(h, 1)]) * scale).astype(bf16)
            return carry

        lax.fori_loop(0, 2, scores_grad, 0)
        gmixed[:, head(h, 1)] = (dot(q, probs[h], tn).T * scale).astype(bf16)
        if h == 1:
            sum_one.two_pass()

    sum_one.z_start()
    fold = Fold(3)
    part[3, pl.ds(far, 256), :] = dot(gmixed[pl.ds(far, 256), :], wq[...], nt).astype(bf16)
    fold.start_far()
    part[3, pl.ds(near, 256), :] = dot(gmixed[pl.ds(near, 256), :], wq[...], nt).astype(bf16)
    fold.start_near()
    grad_columns(parts_two, 0, head_out, branch, hc)
    grad_columns(parts_two, hc, gmixed, nrm, hc)
    sum_two.one_start()
    fold.cross()
    mixed_sum = total(gmixed[...].astype(f32))
    spread_out = (lax.broadcasted_iota(jnp.int32, (hc, D), 0) + shard * hc == lax.broadcasted_iota(jnp.int32, (hc, D), 1)).astype(f32)
    for row, lo in ((4, 0), (5, 2 * hc)):
        small_out[row : row + 1, :] = jnp.dot(mixed_sum[:, lo : lo + hc], spread_out, precision=lax.Precision.HIGHEST, preferred_element_type=f32)
    out_ref[...] = ((resid[...] + fold_out.end() + small[11:12, :]) * live_ref[...]).astype(bf16)
    sum_two.one_pass()
    sum_one.back_start()
    c_one = fold.end()
    hat = xhat1[...]
    small_out[0:1, :] = total(c_one * hat)
    small_out[1:2, :] = total(c_one)
    small_step()
    dx_ref[...] = gres[...] + norm_grad(hat, r_one, small[0:1, :], c_one)
    sum_one.back_pass()
    sum_two.two_start()
    small_step()
    sum_two.two_pass()
    sum_one.last_start()
    small_step()
    sum_two.z_start()
    small_step()
    sum_one.last_pass()
    sum_two.back_start()
    small_step()
    sum_two.back_pass()
    sum_one.last_end()

    def update(u, base, mom, sums):
        count = u.shape[0]
        for k in range(2):
            cols = slice(k * HALF, k * HALF + HALF)
            g = sums[k, base : base + count, :].astype(f32)
            u[:, cols] = (g + momentum_decay * (momentum_decay * mom[:, cols] + g)).astype(bf16)

    n = D // 16
    at = (pl.multiple_of((x * 4 + y) * n, 16), pl.multiple_of((y * 4 + x) * n, 16))

    def gram_rows(m, u, whole):
        for k in range(2):
            cols = slice(k * HALF, k * HALF + HALF)
            if whole:
                piece[m, k] = dot(u[pl.ds(at[k], n), :], u[cols, :], nt)
            else:
                pick = (lax.broadcasted_iota(jnp.int32, (D, n), 0) == lax.broadcasted_iota(jnp.int32, (D, n), 1) + at[k]).astype(f32).astype(bf16)
                piece[m, k] = dot(dot(u[...], pick).astype(bf16), u[:, cols], tn)

    for load in mom_loads:
        load.wait()
    update(wf, 0, wf32, sums_one)
    update(wp, D, wp32, sums_one)
    gram_rows(2, wf, True)
    gram_rows(3, wp, False)
    sum_two.last_start()
    small_step()
    sum_two.last_pass()
    small_step()
    sum_two.last_end()
    small_step()
    update(wo, 0, wo32, sums_two)
    update(uq, hc, momq, sums_two)
    gram_rows(1, wo, False)
    gram_rows(0, uq, False)
    others = [device(x, y, z, (shard + d) % 4) for d in (1, 2, 3)]
    orth_factors(place(), sides, sibling, others, copy, at, piece, gram_got, halves, wf32, gram_low, poly, wp32, factor_low, q_all)


def run_block(x_own, cot, live, col, row, length, wq, wo, wf, wp, mq, mo, mf, mp, small, qkv_bias, fc_bias):
    vm = pl.BlockSpec(memory_space=pltpu.VMEM)
    hbm = pl.BlockSpec(memory_space=pl.ANY)
    rows, wide = x_own.shape[0], wq.shape[1]
    hc = wide // 3
    group = 4 * rows
    vmem = pltpu.VMEM
    return pl.pallas_call(
        block_kernel,
        out_shape=(
            jax.ShapeDtypeStruct((rows, D), bf16),
            jax.ShapeDtypeStruct((rows, D), f32),
            jax.ShapeDtypeStruct((2, 2 * D, HALF), bf16),
            jax.ShapeDtypeStruct((2, D, HALF), bf16),
            jax.ShapeDtypeStruct((12, D), f32),
            jax.ShapeDtypeStruct((4, 2, D, HALF), bf16),
        ),
        in_specs=[vm] * 7 + [hbm] * 7 + [vm] * 3,
        out_specs=(vm,) * 6,
        scratch_shapes=[
            vmem((group, D), bf16),
            vmem((group, D), bf16),
            vmem((group, D), bf16),
            vmem((group, D), bf16),
            vmem((group, wide), bf16),
            vmem((hc // HD, group, group), bf16),
            vmem((group, group), f32),
            vmem((group, hc), bf16),
            vmem((4, group, D), bf16),
            vmem((4, 3, rows, D), bf16),
            vmem((4, rows, D), bf16),
            vmem(wo.shape, f32),
            vmem(wf.shape, f32),
            vmem(wp.shape, f32),
            vmem(wo.shape, bf16),
            vmem(wf.shape, bf16),
            vmem(wp.shape, bf16),
            vmem((group, D), f32),
            vmem((group, D), bf16),
            vmem((group, D), bf16),
            vmem((group, hc), bf16),
            vmem((group, wide), bf16),
            vmem((rows, D), f32),
            vmem((rows, D), f32),
            vmem((rows, D), f32),
            vmem((rows, D), f32),
            vmem((2, 2 * D, HALF), bf16),
            vmem((2, D, HALF), bf16),
            *sum_scratch(2 * D),
            *sum_scratch(D),
            vmem((wide, D), f32),
            vmem((wide, D), bf16),
            vmem((4, 2, D // 16, HALF), f32),
            vmem((3, 2, D // 16, HALF), f32),
            vmem((2, D, HALF), f32),
            vmem((2, D, D), bf16),
            vmem((D, D), bf16),
            vmem((2, D, D), bf16),
            vmem((7, 12, D), f32),
            pltpu.SemaphoreType.DMA((200,)),
            pltpu.SemaphoreType.DMA((200,)),
            pltpu.SemaphoreType.DMA((7,)),
            pltpu.SemaphoreType.DMA((7,)),
            pltpu.SemaphoreType.DMA((7,)),
        ],
        compiler_params=pltpu.CompilerParams(collective_id=1, has_side_effects=True, vmem_limit_bytes=60 * 1024 * 1024),
    )(x_own, cot, live, col, row, length, wq, wo, wf, wp, mq, mo, mf, mp, small, qkv_bias, fc_bias)


def shards(block_input, cotangent, lengths, block_order, w_qkv, w_out, w_fc, w_proj, mom_qkv, mom_out, mom_fc, mom_proj, small_params, small_first, small_second):
    member = lax.axis_index("shard")
    rows = block_input.shape[0]
    hc = w_out.shape[0]
    offsets = jnp.arange(BLOCK, dtype=jnp.int32)
    places = (block_order[0][:, None] * BLOCK + offsets[None, :]).reshape(-1)
    own_places = lax.dynamic_slice_in_dim(places, member * rows, rows)
    live = (own_places < lengths[0]).astype(f32)[:, None]
    places = places.astype(f32)
    small = lax.optimization_barrier(small_params.astype(bf16)).astype(f32)

    def cols(row):
        return lax.dynamic_slice_in_dim(row, member * hc, hc)

    qkv_bias = jnp.concatenate([cols(small[4]), jnp.zeros((hc,), f32), cols(small[5])])[None]
    fc_bias = lax.dynamic_slice_in_dim(small[7:11], member, 1)
    wq = w_qkv.astype(bf16).reshape(D, -1)
    block_output, input_grad, sums_one, sums_two, grad_small, factors = run_block(
        block_input, cotangent, live, places[:, None], places[None, :], lengths.astype(f32)[None], wq, w_out, w_fc, w_proj, mom_qkv.reshape(D, -1).T, mom_out, mom_fc, mom_proj, small, qkv_bias, fc_bias
    )
    one = jnp.concatenate([sums_one[0], sums_one[1]], 1).astype(f32)
    two = jnp.concatenate([sums_two[0], sums_two[1]], 1).astype(f32)
    grads = [two[hc:].T, two[:hc], one[:D], one[D:]]
    moms = [mom_qkv.reshape(D, -1), mom_out, mom_fc, mom_proj]
    new_moms = [momentum_decay * m + g for m, g in zip(moms, grads)]
    updates = [(g + momentum_decay * m).astype(bf16) for g, m in zip(grads, new_moms)]
    factors = jnp.concatenate([factors[:, 0], factors[:, 1]], 2)
    orth = [dot(factors[0], updates[0]), dot(updates[1], factors[1]), dot(factors[2], updates[2]), dot(updates[3], factors[3])]
    news = []
    for w, o, longest, rate in zip([w_qkv.reshape(D, -1), w_out, w_fc, w_proj], orth, [3 * D, D, FF, FF], [muon_rate, out_rate, muon_rate, muon_rate]):
        news.append(w * (1.0 - rate * muon_decay) - rate * 0.2 * math.sqrt(longest) * o)
    next_first = beta_one * small_first + (1.0 - beta_one) * grad_small
    next_second = beta_two * small_second + (1.0 - beta_two) * grad_small * grad_small
    first_hat = next_first / (1.0 - beta_one**STEP)
    second_hat = next_second / (1.0 - beta_two**STEP)
    next_small = small_params - adam_rate * first_hat / (jnp.sqrt(second_hat) + adam_eps)
    cube = w_qkv.shape
    return (block_output, input_grad, grads[0].reshape(cube), *grads[1:], grad_small, news[0].reshape(cube), *news[1:], new_moms[0].reshape(cube), *new_moms[1:], next_first, next_second, next_small, grad_small[11])


def solution(mesh):
    rows = P(("rep", "shard"), None)
    mats = (P(None, None, "shard"), P("shard", None), P(None, "shard"), P("shard", None))
    in_specs = (rows, rows, P("rep"), P("rep", None), *mats, *mats, P(), P(), P())
    out_specs = (rows, rows, *mats, P(), *mats, *mats, P(), P(), P(), P())
    return jax.shard_map(shards, mesh=mesh, in_specs=in_specs, out_specs=out_specs, check_vma=False)
```

```python
import math

import jax
import jax.numpy as jnp
from jax import lax
from jax.experimental import pallas as pl
from jax.experimental.pallas import tpu as pltpu
from jax.sharding import PartitionSpec as P

D = 768
HD = 64
FF = 3072
BLOCK = 128
STEP = 10
momentum_decay = 0.95
muon_rate = 0.15
out_rate = 0.75
muon_decay = 0.01
adam_rate = 0.4
beta_one = 0.9
beta_two = 0.999
adam_eps = 1e-08
norm_eps = 1e-05
poly_a = 3.4445
poly_b = -4.775
poly_c = 2.0315
masked_score = -1e30
bf16 = jnp.bfloat16
f32 = jnp.float32


def dot(left, right, dims=((1,), (0,))):
    return lax.dot_general(left, right, (dims, ((), ())), preferred_element_type=f32)


MESH = pl.DeviceIdType.MESH
HALF = 384
SENDS = 48
RECVS = 177


def place():
    rep = lax.axis_index("rep")
    return rep % 4, rep // 8, (rep // 4) % 2, lax.axis_index("shard")


def device(x, y, z, shard):
    return ((y * 2 + z) * 4 + x, shard)


class GroupSum:
    def __init__(self, sides, across, copy, here, total_rows, parts, out, got_one, got_two, got_z, pass_one, pass_two, mid):
        self.sides, self.across, self.copy, self.here = sides, across, copy, here
        self.parts, self.out, self.got, self.got_z = parts, out, (got_one, got_two), got_z
        self.passing, self.mid, self.ends = (pass_one, pass_two), mid, pass_two
        self.big, self.little = total_rows // 4, total_rows // 16
        self.cuts = (self.big // 2, (self.little // 2 + 15) // 16 * 16)

    @staticmethod
    def rows(start, size):
        return pl.ds(pl.multiple_of(start, 16), size)

    def reduce_start(self, step, ref, axis, k):
        p, left, right = self.sides[axis]
        n, cut, got = (self.big, self.little)[step], self.cuts[step], self.got[step].at[k]
        opp, nxt, prv = (p + 2) % 4, (p + 1) % 4, (p + 3) % 4
        rows, copy = self.rows, self.copy
        first = (
            copy(ref.at[rows(opp * n, cut), :], got.at[0, 0:cut, :], right),
            copy(ref.at[rows(opp * n + cut, n - cut), :], got.at[0, cut:n, :], left),
            copy(ref.at[rows(nxt * n + cut, n - cut), :], got.at[1, cut:n, :], right),
            copy(ref.at[rows(prv * n, cut), :], got.at[1, 0:cut, :], left),
        )
        return first, (p, left, right, nxt, prv, ref, n, cut, got, self.passing[step].at[k])

    def reduce_pass(self, state):
        first, (p, left, right, nxt, prv, ref, n, cut, got, passing) = state
        rows = self.rows
        first[0].wait_recv()
        passing[0:cut, :] = (ref[rows(nxt * n, cut), :].astype(f32) + got[0, 0:cut, :].astype(f32)).astype(bf16)
        second = [self.copy(passing.at[0:cut, :], got.at[2, 0:cut, :], right)]
        first[1].wait_recv()
        passing[cut:n, :] = (ref[rows(prv * n + cut, n - cut), :].astype(f32) + got[0, cut:n, :].astype(f32)).astype(bf16)
        second.append(self.copy(passing.at[cut:n, :], got.at[2, cut:n, :], left))
        return second

    def reduce_end(self, state, second, dst):
        first, (p, left, right, nxt, prv, ref, n, cut, got, passing) = state
        for c in (first[2], first[3], *second):
            c.wait_recv()
        dst[...] = (ref[self.rows(p * n, n), :].astype(f32) + got[1].astype(f32) + got[2].astype(f32)).astype(bf16)
        for c in (*first, *second):
            c.wait_send()

    def gather_start(self, step, ref, axis, base):
        p, left, right = self.sides[axis]
        n, cut = (self.big, self.little)[step], self.cuts[step]

        def send(chunk, head, target):
            spot = self.rows(base + chunk * n + (0 if head else cut), cut if head else n - cut)
            return self.copy(ref.at[spot, :], ref.at[spot, :], target)

        return (send(p, True, right), send(p, False, left), send(p, False, right), send(p, True, left)), (p, left, right, send)

    def gather_pass(self, state):
        first, (p, left, right, send) = state
        first[0].wait_recv()
        second = [send((p + 3) % 4, True, right)]
        first[1].wait_recv()
        second.append(send((p + 1) % 4, False, left))
        return second

    def gather_end(self, state, second):
        for c in (*state[0][2:], *second):
            c.wait_recv()
        for c in (*state[0], *second):
            c.wait_send()

    def one_start(self):
        self.state = [self.reduce_start(0, self.parts.at[k], "xy"[k], k) for k in range(2)]

    def one_pass(self):
        self.second = [self.reduce_pass(state) for state in self.state]

    def two_start(self):
        for k in range(2):
            self.reduce_end(self.state[k], self.second[k], self.mid.at[k])
        self.state = [self.reduce_start(1, self.mid.at[k], "yx"[k], k) for k in range(2)]

    two_pass = one_pass

    def z_start(self):
        for k in range(2):
            self.reduce_end(self.state[k], self.second[k], self.ends.at[2 + k])
        self.over = [self.copy(self.ends.at[2 + k], self.got_z.at[k], self.across) for k in range(2)]

    def back_start(self):
        x, y = self.here
        self.state = []
        for k in range(2):
            base = (x, y)[k] * self.big
            at = base + (y, x)[k] * self.little
            self.over[k].wait()
            self.out[k, self.rows(at, self.little), :] = (self.ends[2 + k].astype(f32) + self.got_z[k].astype(f32)).astype(bf16)
            self.state.append(self.gather_start(1, self.out.at[k], "yx"[k], base))

    def back_pass(self):
        self.second = [self.gather_pass(state) for state in self.state]

    def last_start(self):
        for k in range(2):
            self.gather_end(self.state[k], self.second[k])
        self.state = [self.gather_start(0, self.out.at[k], "xy"[k], 0) for k in range(2)]

    last_pass = back_pass

    def last_end(self):
        for k in range(2):
            self.gather_end(self.state[k], self.second[k])


def sum_scratch(total_rows):
    big, little = total_rows // 4, total_rows // 16
    return [
        pltpu.VMEM((2, 3, big, HALF), bf16),
        pltpu.VMEM((2, 3, little, HALF), bf16),
        pltpu.VMEM((2, little, HALF), bf16),
        pltpu.VMEM((2, big, HALF), bf16),
        pltpu.VMEM((4, little, HALF), bf16),
        pltpu.VMEM((2, big, HALF), bf16),
    ]


def make_gather(sides, copy):
    def start(axis, ref, base, n, cut, unit):
        p, left, right = sides[axis]

        def rows(chunk, first):
            at = base + chunk * n + (0 if first else cut)
            return pl.ds(pl.multiple_of(at, unit), cut if first else n - cut)

        def send(chunk, first, target):
            spot = rows(chunk, first)
            return copy(ref.at[spot, :], ref.at[spot, :], target)

        first = (send(p, True, right), send(p, False, left), send(p, False, right), send(p, True, left))
        return first, (p, left, right, send)

    def onward(state):
        first, (p, left, right, send) = state
        first[0].wait_recv()
        second = [send((p + 3) % 4, True, right)]
        first[1].wait_recv()
        second.append(send((p + 1) % 4, False, left))
        return second

    def end(state, second):
        for c in (*state[0][2:], *second):
            c.wait_recv()
        for c in (*state[0], *second):
            c.wait_send()

    def both(refs, orders, base, sizes, unit):
        for step in range(2):
            states = []
            for k in range(2):
                n, cut = sizes[step]
                states.append(start(orders[k][step], refs[k], base[k] if step == 0 else 0, n, cut, unit))
            seconds = [onward(state) for state in states]
            for state, second in zip(states, seconds):
                end(state, second)

    return both


def orth_factors(here, sides, sibling, over_z, over_z_next, copy, at, piece, got, halves, gram, gram_low, poly, factor, factor_low, q_all):
    x, y, z, shard = here
    gather = make_gather(sides, copy)
    n = D // 16
    sib, par = shard + 1 - 2 * (shard % 2), (shard + 2) % 4
    ps = (sib + 2) % 4
    sums = [copy(piece.at[sib], got.at[0], sibling)]
    for k in range(2):
        sums.append(copy(piece.at[par, k], got.at[1, k], over_z[k]))
        sums.append(copy(piece.at[ps, k], got.at[2, k], over_z_next[k]))
    for c in sums:
        c.wait_recv()
    for k in range(2):
        halves[k, pl.ds(at[k], n), :] = piece[shard, k] + got[0, k] + got[1, k] + got[2, k]
    orders = (("y", "x"), ("x", "y"))
    base = (x * 4 * n, y * 4 * n)
    gather([halves.at[0], halves.at[1]], orders, base, ((n, 24), (4 * n, 2 * n)), 8)
    for c in sums:
        c.wait_send()

    tile = 256
    blocks = D // tile

    def eye(r, width, first):
        return (lax.broadcasted_iota(jnp.int32, (tile, width), 0) + r * tile == lax.broadcasted_iota(jnp.int32, (tile, width), 1) + first).astype(f32)

    trace = jnp.zeros((1, 1), f32)
    for r in range(blocks):
        for k in range(2):
            part = halves[k, r * tile : (r + 1) * tile, :] * eye(r, HALF, k * HALF)
            trace = trace + jnp.sum(jnp.sum(part, axis=1, keepdims=True), axis=0, keepdims=True)
    inv = 1.0 / (jnp.sqrt(trace) + 1e-07)
    for r in range(blocks):
        spot = slice(r * tile, (r + 1) * tile)
        for k in range(2):
            cols = slice(k * HALF, k * HALF + HALF)
            g = halves[k, spot, :] * (inv * inv)
            gram[spot, cols] = g
            gram_low[0, spot, cols] = g.astype(bf16)

    for k in range(4):
        now, later = k % 2, (k + 1) % 2

        def poly_rows(r):
            spot = slice(r * tile, (r + 1) * tile)
            poly[spot, :] = (poly_b * gram[spot, :] + poly_c * dot(gram_low[now, spot, :], gram_low[now])).astype(bf16)

        def update_rows(r):
            spot = slice(r * tile, (r + 1) * tile)
            p = poly[spot, :]
            if k == 0:
                q = p.astype(f32) + poly_a * eye(r, D, 0)
            else:
                q = poly_a * factor[spot, :] + dot(p, factor_low[now])
            factor[spot, :] = q
            if k < 3:
                factor_low[later, spot, :] = q.astype(bf16)
                t = poly_a * gram[spot, :] + dot(p, gram_low[now])
                g = poly_a * t + dot(t.astype(bf16), poly[...])
                gram[spot, :] = g
                gram_low[later, spot, :] = g.astype(bf16)

        for r in range(blocks):
            poly_rows(r)
        for r in range(blocks):
            update_rows(r)
    q_all[shard, 0] = (factor[0:HALF, 0:HALF] * inv).astype(bf16)
    q_all[shard, 1] = (factor[0:HALF, HALF:D] * inv).astype(bf16)
    q_all[shard, 2] = (factor[HALF:D, HALF:D] * inv).astype(bf16)
    top, low_part = pl.ds(0, HALF // 2), pl.ds(HALF // 2, HALF // 2)
    cross = []
    for k in range(2):
        for block, spot in ((1, (top, low_part)[k]), (2 * k, pl.ds(0, HALF))):
            view = q_all.at[shard, block, spot, :]
            cross.append((copy(view, view, over_z[k]), block, spot))
    near = copy(q_all.at[shard], q_all.at[shard], sibling)
    away = (shard + 2) % 4
    onward = []
    for c, block, spot in (cross[0], cross[2], cross[1], cross[3]):
        c.wait_recv()
        view = q_all.at[away, block, spot, :]
        onward.append(copy(view, view, sibling))
    near.wait_recv()
    for c in onward:
        c.wait_recv()
    for c in (*[c for c, block, spot in cross], near, *onward):
        c.wait_send()


def block_kernel(
    x_ref, cot_ref, length_ref, order_ref, wq_hbm, wo_hbm, wf_hbm, wp_hbm, mq_hbm, mo_hbm, mf_hbm, mp_hbm, small_ref,
    out_ref, dx_ref, sums_one, sums_two, small_out, q_all, u_fc,
    nrm, mlow, nrm2, branch, mixed, probs, bias, head_out, part, got, passing, wo32, wf32, wp32, wq, wo, wf, wp,
    gact, act, gpre, gheads, gmixed, xhat1, xhat2, resid, gres, parts_one, parts_two, *rest,
):
    one_refs, two_refs = rest[:6], rest[6:12]
    momq, small, qkv_bias, row_place, uq, piece, gram_got, halves, gram_low, poly, factor_low = rest[12:23]
    small_got, send, recv, local = rest[23:]
    x, y, z, shard = place()
    sib = shard + 1 - 2 * (shard % 2)
    par = (shard + 2) % 4
    sibling, partner = device(x, y, z, sib), device(x, y, z, par)
    sides = {
        "x": (x, device((x + 3) % 4, y, z, shard), device((x + 1) % 4, y, z, shard)),
        "y": (y, device(x, (y + 3) % 4, z, shard), device(x, (y + 1) % 4, z, shard)),
    }
    across = device(x, y, 1 - z, shard)
    far_sib = (sib + 2) % 4
    partners = (sibling, partner, device(x, y, z, far_sib), device(x, y, 1 - z, par), device(x, y, 1 - z, far_sib), *sides["x"][1:], *sides["y"][1:], across)
    barrier = pltpu.get_barrier_semaphore()
    for other in partners:
        pl.semaphore_signal(barrier, inc=1, device_id=other, device_id_type=MESH)
    loads = [pltpu.make_async_copy(src, dst, local.at[k]) for k, (src, dst) in enumerate(((wq_hbm, momq), (wo_hbm, wo32), (wf_hbm, wf32), (wp_hbm, wp32)))]
    for load in loads:
        load.start()

    rows = BLOCK

    def chunk(index, size=rows, at=0):
        return pl.ds(pl.multiple_of(index * rows + at, 16), size)

    own, own_sib, own_par, own_ps = chunk(shard), chunk(sib), chunk(par), chunk((sib + 2) % 4)
    near = pl.multiple_of((shard // 2) * 256, 256)
    far = pl.multiple_of(256 - near, 256)
    used = [0]

    free = list(range(SENDS))

    class Copy:
        def __init__(self, src, dst, target):
            self.slot = free.pop(0)
            self.copy = pltpu.make_async_remote_copy(
                src_ref=src, dst_ref=dst, send_sem=send.at[self.slot], recv_sem=recv.at[used[0]], device_id=target, device_id_type=MESH
            )
            used[0] += 1
            self.copy.start()

        def wait_recv(self):
            self.copy.wait_recv()

        def wait_send(self):
            self.copy.wait_send()
            free.append(self.slot)

        def wait(self):
            self.wait_recv()
            self.wait_send()

    copy = Copy
    sum_one = GroupSum(sides, across, copy, (x, y), 2 * D, parts_one, sums_one, *one_refs)
    sum_two = GroupSum(sides, across, copy, (x, y), D, parts_two, sums_two, *two_refs)
    steps = [
        sibling,
        partner,
        device(x + 1 - 2 * (x % 2), y, z, shard),
        device(3 - x, y, z, shard),
        device(x, y + 1 - 2 * (y % 2), z, shard),
        device(x, 3 - y, z, shard),
        across,
    ]
    small_copies = []

    def small_step():
        k = len(small_copies)
        if k > 0:
            small_copies[-1].wait()
            small_out[...] += small_got[k - 1]
        if k < len(steps):
            small_copies.append(copy(small_out, small_got.at[k], steps[k]))

    class Spread:
        def __init__(self, ref):
            self.ref = ref
            self.cross = [self.to(shard, 64 * i, partner) for i in range(2)]
            self.direct = copy(ref.at[own, :], ref.at[own, :], sibling)

        def to(self, index, at, target):
            spot = chunk(index, 64, at)
            return copy(self.ref.at[spot, :], self.ref.at[spot, :], target)

        def near(self):
            self.direct.wait_recv()

        def far(self):
            onward = []
            for i in range(2):
                self.cross[i].wait_recv()
                onward.append(self.to(par, 64 * i, sibling))
            for c in onward:
                c.wait_recv()
            for c in (*self.cross, self.direct, *onward):
                c.wait_send()

    class Fold:
        def __init__(self, k):
            self.k = k

        def start_far(self):
            self.a = copy(part.at[self.k, own_ps, :], got.at[self.k, 0], sibling)

        def start_near(self):
            self.b = copy(part.at[self.k, own_sib, :], got.at[self.k, 1], sibling)

        def cross(self):
            self.a.wait_recv()
            passing[self.k] = (part[self.k, own_par, :].astype(f32) + got[self.k, 0].astype(f32)).astype(bf16)
            self.c = copy(passing.at[self.k], got.at[self.k, 2], partner)

        def end(self):
            self.b.wait_recv()
            self.c.wait_recv()
            for c in (self.a, self.b, self.c):
                c.wait_send()
            return part[self.k, own, :].astype(f32) + got[self.k, 1].astype(f32) + got[self.k, 2].astype(f32)

    def norm(v):
        centred = v - jnp.mean(v, axis=-1, keepdims=True)
        r = lax.rsqrt(jnp.mean(centred * centred, axis=-1, keepdims=True) + norm_eps)
        return centred * r, r

    def norm_grad(xhat, r, gain, c):
        cg = c * gain
        return r * (cg - jnp.mean(cg, -1, keepdims=True) - xhat * jnp.mean(cg * xhat, -1, keepdims=True))

    def total(v):
        return jnp.sum(v, axis=0, keepdims=True)

    nt, tn = ((1,), (1,)), ((0,), (0,))
    hc = wq.shape[0] // 3
    heads = hc // HD
    scale = HD ** -0.5

    small[...] = small_ref[...].astype(bf16).astype(f32)
    length = length_ref[0]

    def places(slot, axis):
        return lax.broadcasted_iota(jnp.int32, (rows, 1) if axis == 0 else (1, rows), axis) + order_ref[0, slot] * rows

    live = (places(shard, 0) < length).astype(f32)
    xf = x_ref[...].astype(f32)
    hat, r_one = norm(xf)
    xhat1[...] = hat
    nrm[own, :] = (hat * small[0:1, :] + small[1:2, :]).astype(bf16)
    mlow[own, :] = (cot_ref[...] * live).astype(bf16)
    pl.semaphore_wait(barrier, len(partners))
    go_nrm = Spread(nrm)
    go_mlow = Spread(mlow)
    for slot in range(4):
        row_place[:, slot * rows : (slot + 1) * rows] = places(slot, 1)
    row = row_place[...]
    for slot in range(4):
        bias[slot * rows : (slot + 1) * rows, :] = jnp.where((row <= places(slot, 0)) & (row < length), 0.0, masked_score)
    for part_of, line in ((0, 4), (2, 5)):
        mine = jnp.zeros((1, hc), f32)
        for s in range(4):
            mine = jnp.where(shard == s, small[line : line + 1, s * hc : (s + 1) * hc], mine)
        qkv_bias[:, part_of * hc : (part_of + 1) * hc] = mine
    qkv_bias[:, hc : 2 * hc] = jnp.zeros((1, hc), f32)
    fc_bias = small[pl.ds(7 + shard, 1), :]
    loads[0].wait()
    wq[...] = momq[...].astype(bf16)
    loads[1].wait()
    wo[...] = wo32[...].astype(bf16)

    def mix(at):
        spot = pl.ds(at, 256)
        mixed[spot, :] = (dot(nrm[spot, :], wq[...], nt) + qkv_bias[...]).astype(bf16)

    go_nrm.near()
    mix(near)
    go_nrm.far()
    mix(far)

    def head(h, part_of):
        lo = part_of * hc + h * HD
        return slice(lo, lo + HD)

    for h in range(heads):

        def attend(i, carry):
            spot = pl.ds(pl.multiple_of(i * 256, 256), 256)
            s = dot(mixed[spot, head(h, 0)], mixed[:, head(h, 1)], nt) * scale + bias[spot, :]
            e = jnp.exp(s - jnp.max(s, axis=-1, keepdims=True))
            p = (e * (1.0 / jnp.sum(e, axis=-1, keepdims=True))).astype(bf16)
            probs[h, spot, :] = p
            head_out[spot, head(h, 0)] = dot(p, mixed[:, head(h, 2)]).astype(bf16)
            return carry

        lax.fori_loop(0, 2, attend, 0)

    fold = Fold(0)
    part[0, pl.ds(far, 256), :] = dot(head_out[pl.ds(far, 256), :], wo[...]).astype(bf16)
    fold.start_far()
    part[0, pl.ds(near, 256), :] = dot(head_out[pl.ds(near, 256), :], wo[...]).astype(bf16)
    fold.start_near()
    fold.cross()
    go_mlow.near()
    go_mlow.far()
    loads[2].wait()
    wf[...] = wf32[...].astype(bf16)
    loads[3].wait()
    wp[...] = wp32[...].astype(bf16)

    mom_loads = [pltpu.make_async_copy(src, dst, local.at[4 + k]) for k, (src, dst) in enumerate(((mo_hbm, wo32), (mf_hbm, wf32), (mp_hbm, wp32), (mq_hbm, momq)))]
    for load in mom_loads:
        load.start()

    def activation_grad(i, carry):
        spot = pl.ds(pl.multiple_of(i * 256, 256), 256)
        gact[spot, :] = dot(mlow[spot, :], wp[...], nt)
        return carry

    lax.fori_loop(0, 2, activation_grad, 0)
    res = x_ref[...].astype(f32) + fold.end() + small[6:7, :]
    resid[...] = res
    hat, r_two = norm(res)
    xhat2[...] = hat
    nrm2[own, :] = (hat * small[2:3, :] + small[3:4, :]).astype(bf16)
    go_nrm2 = Spread(nrm2)

    def feed(at):
        spot = pl.ds(at, 256)
        hidden = dot(nrm2[spot, :], wf[...]) + fc_bias
        k = 0.7978845608028654
        square = hidden * hidden
        t = jnp.tanh(k * (hidden + 0.044715 * hidden * square))
        half = 0.5 * (1.0 + t)
        act[spot, :] = (hidden * half).astype(bf16)
        slope = half + 0.5 * hidden * (1.0 - t * t) * (k + (3 * 0.044715 * k) * square)
        gpre[spot, :] = (slope * gact[spot, :]).astype(bf16)

    go_nrm2.near()
    feed(near)
    go_nrm2.far()
    feed(far)
    fold = Fold(1)
    part[1, pl.ds(far, 256), :] = dot(gpre[pl.ds(far, 256), :], wf[...], nt).astype(bf16)
    fold.start_far()
    part[1, pl.ds(near, 256), :] = dot(gpre[pl.ds(near, 256), :], wf[...], nt).astype(bf16)
    fold.start_near()
    fold.cross()

    def grad_columns(parts, base, left, right, width):
        for c in range(left.shape[1] // width):
            value = dot(left[:, c * width : (c + 1) * width], right[...], tn).astype(bf16)
            spot = pl.ds(base + c * width, width)
            parts[0, spot, :] = value[:, :HALF]
            parts[1, spot, :] = value[:, HALF:]

    grad_columns(parts_one, 0, nrm2, gpre, 256)
    grad_columns(parts_one, D, act, mlow, 256)
    sum_one.one_start()
    small_out[11:12, :] = total(mlow[own, :].astype(f32))
    c_two = fold.end()
    hat = xhat2[...]
    small_out[2:3, :] = total(c_two * hat)
    small_out[3:4, :] = total(c_two)
    g = cot_ref[...] * live + norm_grad(hat, r_two, small[2:3, :], c_two)
    gres[...] = g
    branch[own, :] = g.astype(bf16)
    go_branch = Spread(branch)
    sum_one.one_pass()
    small_out[6:7, :] = total(branch[own, :].astype(f32))
    pre_sum = total(gpre[...].astype(f32))
    small_out[7:11, :] = jnp.where(lax.broadcasted_iota(jnp.int32, (4, D), 0) == shard, pre_sum, 0.0)

    def head_grads(at):
        spot = pl.ds(at, 256)
        gheads[spot, :] = dot(branch[spot, :], wo[...], nt).astype(bf16)

    fold_out = Fold(2)
    part[2, pl.ds(far, 256), :] = dot(act[pl.ds(far, 256), :], wp[...]).astype(bf16)
    fold_out.start_far()
    part[2, pl.ds(near, 256), :] = dot(act[pl.ds(near, 256), :], wp[...]).astype(bf16)
    fold_out.start_near()
    go_branch.near()
    head_grads(near)
    go_branch.far()
    head_grads(far)
    fold_out.cross()
    sum_one.two_start()
    for h in range(heads):
        q, k, v = (mixed[:, head(h, i)] for i in range(3))
        gh = gheads[:, head(h, 0)]
        gmixed[:, head(h, 2)] = dot(gh, probs[h], tn).T.astype(bf16)

        def scores_grad(i, carry):
            spot = pl.ds(pl.multiple_of(i * 256, 256), 256)
            p = probs[h, spot, :].astype(f32)
            gp = dot(gheads[spot, head(h, 0)], mixed[:, head(h, 2)], nt)
            gs = (p * (gp - jnp.sum(p * gp, axis=-1, keepdims=True))).astype(bf16)
            probs[h, spot, :] = gs
            gmixed[spot, head(h, 0)] = (dot(gs, mixed[:, head(h, 1)]) * scale).astype(bf16)
            return carry

        lax.fori_loop(0, 2, scores_grad, 0)
        gmixed[:, head(h, 1)] = (dot(q, probs[h], tn).T * scale).astype(bf16)
        if h == 1:
            sum_one.two_pass()

    sum_one.z_start()
    fold = Fold(3)
    part[3, pl.ds(far, 256), :] = dot(gmixed[pl.ds(far, 256), :], wq[...]).astype(bf16)
    fold.start_far()
    part[3, pl.ds(near, 256), :] = dot(gmixed[pl.ds(near, 256), :], wq[...]).astype(bf16)
    fold.start_near()
    grad_columns(parts_two, 0, head_out, branch, hc)
    grad_columns(parts_two, hc, gmixed, nrm, hc)
    sum_two.one_start()
    fold.cross()
    mixed_sum = total(gmixed[...].astype(f32))
    spread_out = (lax.broadcasted_iota(jnp.int32, (hc, D), 0) + shard * hc == lax.broadcasted_iota(jnp.int32, (hc, D), 1)).astype(f32)
    for row, lo in ((4, 0), (5, 2 * hc)):
        small_out[row : row + 1, :] = jnp.dot(mixed_sum[:, lo : lo + hc], spread_out, precision=lax.Precision.HIGHEST, preferred_element_type=f32)
    out_ref[...] = ((resid[...] + fold_out.end() + small[11:12, :]) * live).astype(bf16)
    sum_two.one_pass()
    sum_one.back_start()
    c_one = fold.end()
    hat = xhat1[...]
    small_out[0:1, :] = total(c_one * hat)
    small_out[1:2, :] = total(c_one)
    small_step()
    dx_ref[...] = gres[...] + norm_grad(hat, r_one, small[0:1, :], c_one)
    sum_one.back_pass()
    sum_two.two_start()
    small_step()
    sum_two.two_pass()
    sum_one.last_start()
    small_step()
    sum_two.z_start()
    small_step()
    sum_one.last_pass()
    sum_two.back_start()
    small_step()
    sum_two.back_pass()
    sum_one.last_end()

    def update(u, base, mom, sums):
        count = u.shape[0]
        for k in range(2):
            cols = slice(k * HALF, k * HALF + HALF)
            g = sums[k, base : base + count, :].astype(f32)
            u[:, cols] = (g + momentum_decay * (momentum_decay * mom[:, cols] + g)).astype(bf16)

    n = D // 16
    at = (pl.multiple_of((x * 4 + y) * n, 16), pl.multiple_of((y * 4 + x) * n, 16))

    def gram_rows(m, u, whole):
        for k in range(2):
            cols = slice(k * HALF, k * HALF + HALF)
            if whole:
                piece[m, k] = dot(u[pl.ds(at[k], n), :], u[cols, :], nt)
            else:
                pick = (lax.broadcasted_iota(jnp.int32, (D, n), 0) == lax.broadcasted_iota(jnp.int32, (D, n), 1) + at[k]).astype(f32).astype(bf16)
                piece[m, k] = dot(dot(u[...], pick).astype(bf16), u[:, cols], tn)

    for load in mom_loads:
        load.wait()
    update(u_fc, 0, wf32, sums_one)
    update(wp, D, wp32, sums_one)
    gram_rows(2, u_fc, True)
    gram_rows(3, wp, False)
    sum_two.last_start()
    small_step()
    sum_two.last_pass()
    small_step()
    sum_two.last_end()
    small_step()
    update(wo, 0, wo32, sums_two)
    update(uq, hc, momq, sums_two)
    gram_rows(1, wo, False)
    gram_rows(0, uq, False)
    over_z = [partner, device(x, y, 1 - z, par)]
    over_z_next = [device(x, y, z, (sib + 2) % 4), device(x, y, 1 - z, (sib + 2) % 4)]
    orth_factors(place(), sides, sibling, over_z, over_z_next, copy, at, piece, gram_got, halves, wf32, gram_low, poly, wp32, factor_low, q_all)
    assert used[0] <= RECVS and len(free) == SENDS


def run_block(x_own, cot, lengths, order, wq, wo, wf, wp, mq, mo, mf, mp, small):
    vm = pl.BlockSpec(memory_space=pltpu.VMEM)
    sm = pl.BlockSpec(memory_space=pltpu.SMEM)
    hbm = pl.BlockSpec(memory_space=pl.ANY)
    rows, wide = x_own.shape[0], wq.shape[0]
    hc = wide // 3
    group = 4 * rows
    vmem = pltpu.VMEM
    return pl.pallas_call(
        block_kernel,
        out_shape=(
            pltpu.VMEM((rows, D), bf16),
            pltpu.VMEM((rows, D), f32),
            pltpu.VMEM((2, 2 * D, HALF), bf16),
            pltpu.VMEM((2, D, HALF), bf16),
            pltpu.VMEM((12, D), f32),
            pltpu.VMEM((4, 3, HALF, HALF), bf16),
            pltpu.VMEM((D, D), bf16),
        ),
        in_specs=[vm, vm, sm, sm] + [hbm] * 8 + [vm],
        out_specs=(vm,) * 7,
        scratch_shapes=[
            vmem((group, D), bf16),
            vmem((group, D), bf16),
            vmem((group, D), bf16),
            vmem((group, D), bf16),
            vmem((group, wide), bf16),
            vmem((hc // HD, group, group), bf16),
            vmem((group, group), f32),
            vmem((group, hc), bf16),
            vmem((4, group, D), bf16),
            vmem((4, 3, rows, D), bf16),
            vmem((4, rows, D), bf16),
            vmem(wo.shape, f32),
            vmem(wf.shape, f32),
            vmem(wp.shape, f32),
            vmem(wq.shape, bf16),
            vmem(wo.shape, bf16),
            vmem(wf.shape, bf16),
            vmem(wp.shape, bf16),
            vmem((group, D), f32),
            vmem((group, D), bf16),
            vmem((group, D), bf16),
            vmem((group, hc), bf16),
            vmem((group, wide), bf16),
            vmem((rows, D), f32),
            vmem((rows, D), f32),
            vmem((rows, D), f32),
            vmem((rows, D), f32),
            vmem((2, 2 * D, HALF), bf16),
            vmem((2, D, HALF), bf16),
            *sum_scratch(2 * D),
            *sum_scratch(D),
            vmem((wide, D), f32),
            vmem((12, D), f32),
            vmem((1, wide), f32),
            vmem((1, group), jnp.int32),
            vmem((wide, D), bf16),
            vmem((4, 2, D // 16, HALF), f32),
            vmem((3, 2, D // 16, HALF), f32),
            vmem((2, D, HALF), f32),
            vmem((2, D, D), bf16),
            vmem((D, D), bf16),
            vmem((2, D, D), bf16),
            vmem((7, 12, D), f32),
            pltpu.SemaphoreType.DMA((SENDS,)),
            pltpu.SemaphoreType.DMA((RECVS,)),
            pltpu.SemaphoreType.DMA((8,)),
        ],
        compiler_params=pltpu.CompilerParams(collective_id=1, has_side_effects=True, vmem_limit_bytes=50 * 1024 * 1024),
    )(x_own, cot, lengths, order, wq, wo, wf, wp, mq, mo, mf, mp, small)


def finish_kernel(
    sums_one, sums_two, q_all, u_fc, out_in, dx_in, small_sum, small_params, small_first, small_second,
    wq, wo, wf, wp, mq, mo, mf, mp,
    out_ref, dx_ref, gq, go, gf, gp, nq, no, nf, np_, rq, ro, rf, rp, small_grad, first_ref, second_ref, small_new, last_bias,
):
    i = pl.program_id(0)
    nt, tn = ((1,), (1,)), ((0,), (0,))

    @pl.when(i == 0)
    def _():
        out_ref[...] = out_in[...]
        dx_ref[...] = dx_in[...]
        g = small_sum[...]
        small_grad[...] = g
        last_bias[...] = g[11:12, :]
        first = beta_one * small_first[...] + (1.0 - beta_one) * g
        second = beta_two * small_second[...] + (1.0 - beta_two) * g * g
        first_ref[...] = first
        second_ref[...] = second
        first_hat = first / (1.0 - beta_one**STEP)
        second_hat = second / (1.0 - beta_two**STEP)
        small_new[...] = small_params[...] - adam_rate * first_hat / (jnp.sqrt(second_hat) + adam_eps)

    def renew(owner, sums, base, w, m, g_out, w_out, m_out, longest, rate, rows_of=None):
        count = w.shape[0]
        keep_rate, step_rate = 1.0 - rate * muon_decay, rate * 0.2 * math.sqrt(longest)
        spot = pl.ds(pl.multiple_of(base + i * count, 16), count)
        low = []
        for k in range(2):
            cols = slice(k * HALF, k * HALF + HALF)
            g = sums[k, spot, :].astype(f32)
            moved = momentum_decay * m[:, cols] + g
            g_out[:, cols] = g
            m_out[:, cols] = moved
            low.append((g + momentum_decay * moved).astype(bf16))
        q11, q12, q22 = q_all[owner, 0], q_all[owner, 1], q_all[owner, 2]
        w_out[:, :HALF] = keep_rate * w[:, :HALF] - step_rate * (dot(low[0], q11) + dot(low[1], q12, nt))
        w_out[:, HALF:] = keep_rate * w[:, HALF:] - step_rate * (dot(low[0], q12) + dot(low[1], q22))

    renew(0, sums_two, 192, wq, mq, gq, nq, rq, 3 * D, muon_rate)
    renew(1, sums_two, 0, wo, mo, go, no, ro, D, out_rate)
    renew(3, sums_one, D, wp, mp, gp, np_, rp, FF, muon_rate)
    count = wf.shape[0]
    keep_rate, step_rate = 1.0 - muon_rate * muon_decay, muon_rate * 0.2 * math.sqrt(FF)
    spot = pl.ds(pl.multiple_of(i * count, 16), count)
    for k in range(2):
        cols = slice(k * HALF, k * HALF + HALF)
        g = sums_one[k, spot, :].astype(f32)
        gf[:, cols] = g
        rf[:, cols] = momentum_decay * mf[:, cols] + g
    half_steps = HALF // count

    @pl.when(i < half_steps)
    def _():
        at = pl.ds(pl.multiple_of(i * count, count), count)
        nf[...] = keep_rate * wf[...] - step_rate * (dot(q_all[2, 0, at, :], u_fc[:HALF, :]) + dot(q_all[2, 1, at, :], u_fc[HALF:, :]))

    @pl.when(i >= half_steps)
    def _():
        at = pl.ds(pl.multiple_of((i - half_steps) * count, count), count)
        nf[...] = keep_rate * wf[...] - step_rate * (dot(q_all[2, 1, :, at], u_fc[:HALF, :], tn) + dot(q_all[2, 2, at, :], u_fc[HALF:, :]))


def finish(kept, small, weights, moms):
    steps = 6
    vm = pl.BlockSpec(memory_space=pltpu.VMEM)

    def tiles(a):
        return pl.BlockSpec((a.shape[0] // steps, a.shape[1]), lambda i: (i, 0))

    def whole(shape):
        return pl.BlockSpec(shape, lambda i: (0, 0))

    like = [jax.ShapeDtypeStruct(w.shape, f32) for w in weights]
    flat = jax.ShapeDtypeStruct((12, D), f32)
    last = jax.ShapeDtypeStruct((1, D), f32)
    block_out, dx = kept[4], kept[5]
    own = [jax.ShapeDtypeStruct(block_out.shape, bf16), jax.ShapeDtypeStruct(dx.shape, f32)]
    return pl.pallas_call(
        finish_kernel,
        grid=(steps,),
        out_shape=(*own, *like, *like, *like, flat, flat, flat, flat, last),
        in_specs=[vm] * 10 + [tiles(w) for w in weights] * 2,
        out_specs=(whole(block_out.shape), whole(dx.shape), *([tiles(w) for w in weights] * 3), *([whole((12, D))] * 4), whole((1, D))),
        compiler_params=pltpu.CompilerParams(vmem_limit_bytes=24 * 1024 * 1024),
    )(*kept, *small, *weights, *moms)


def shards(block_input, cotangent, lengths, block_order, w_qkv, w_out, w_fc, w_proj, mom_qkv, mom_out, mom_fc, mom_proj, small_params, small_first, small_second):
    cube = w_qkv.shape

    def turned(a):
        return a.transpose(1, 2, 0).reshape(-1, D)

    def back(a):
        return a.reshape(cube[1], cube[2], D).transpose(2, 0, 1)

    weights = (turned(w_qkv), w_out, w_fc, w_proj)
    moms = (turned(mom_qkv), mom_out, mom_fc, mom_proj)
    block_output, input_grad, sums_one, sums_two, small_sum, factors, u_fc = run_block(block_input, cotangent, lengths, block_order, *weights, *moms, small_params)
    kept = [sums_one, sums_two, factors, u_fc, block_output, input_grad, small_sum]
    kept = [pltpu.with_memory_space_constraint(a, pltpu.VMEM) for a in kept]
    weights, moms = ([pltpu.with_memory_space_constraint(a, pltpu.HBM) for a in group] for group in (weights, moms))
    block_output, input_grad, gq, go, gf, gp, nq, no, nf, np_, rq, ro, rf, rp, grad_small, first, second, new_small, last = finish(
        kept, (small_params, small_first, small_second), weights, moms
    )
    return (
        block_output, input_grad, back(gq), go, gf, gp, grad_small, back(nq), no, nf, np_, back(rq), ro, rf, rp, first, second, new_small, last[0],
    )


def solution(mesh):
    rows = P(("rep", "shard"), None)
    mats = (P(None, None, "shard"), P("shard", None), P(None, "shard"), P("shard", None))
    in_specs = (rows, rows, P("rep"), P("rep", None), *mats, *mats, P(), P(), P())
    out_specs = (rows, rows, *mats, P(), *mats, *mats, P(), P(), P(), P())
    return jax.shard_map(shards, mesh=mesh, in_specs=in_specs, out_specs=out_specs, check_vma=False)
```

```python
import math

import jax
import jax.numpy as jnp
from jax import lax
from jax.experimental import pallas as pl
from jax.experimental.pallas import tpu as pltpu
from jax.sharding import PartitionSpec as P

D = 768
HD = 64
FF = 3072
BLOCK = 128
STEP = 10
momentum_decay = 0.95
muon_rate = 0.15
out_rate = 0.75
muon_decay = 0.01
adam_rate = 0.4
beta_one = 0.9
beta_two = 0.999
adam_eps = 1e-08
norm_eps = 1e-05
poly_a = 3.4445
poly_b = -4.775
poly_c = 2.0315
masked_score = -1e30
bf16 = jnp.bfloat16
f32 = jnp.float32


def dot(left, right, dims=((1,), (0,))):
    return lax.dot_general(left, right, (dims, ((), ())), preferred_element_type=f32)


MESH = pl.DeviceIdType.MESH
HALF = 384
SENDS = 48
RECVS = 160


def place():
    rep = lax.axis_index("rep")
    return rep % 4, rep // 8, (rep // 4) % 2, lax.axis_index("shard")


def device(x, y, z, shard):
    return ((y * 2 + z) * 4 + x, shard)


class GroupSum:
    def __init__(self, sides, across, copy, here, total_rows, parts, out, got_one, got_two, got_z, pass_one, pass_two, mid):
        self.sides, self.across, self.copy, self.here = sides, across, copy, here
        self.parts, self.out, self.got, self.got_z = parts, out, (got_one, got_two), got_z
        self.passing, self.mid, self.ends = (pass_one, pass_two), mid, pass_two
        self.big, self.little = total_rows // 4, total_rows // 16
        self.cuts = (self.big // 2, (self.little // 2 + 15) // 16 * 16)

    @staticmethod
    def rows(start, size):
        return pl.ds(pl.multiple_of(start, 16), size)

    def reduce_start(self, step, ref, axis, k):
        p, left, right, over = self.sides[axis]
        n, cut, got = (self.big, self.little)[step], self.cuts[step], self.got[step].at[k]
        opp, nxt, prv = (p + 2) % 4, (p + 1) % 4, (p + 3) % 4
        rows, copy = self.rows, self.copy
        if step == 1:
            direct = [copy(ref.at[rows(c * n, n), :], got.at[i], target) for i, (c, target) in enumerate(((nxt, right), (prv, left), (opp, over)))]
            return direct, (p, ref, n, got)
        first = (
            copy(ref.at[rows(opp * n, cut), :], got.at[0, 0:cut, :], right),
            copy(ref.at[rows(opp * n + cut, n - cut), :], got.at[0, cut:n, :], left),
            copy(ref.at[rows(nxt * n + cut, n - cut), :], got.at[1, cut:n, :], right),
            copy(ref.at[rows(prv * n, cut), :], got.at[1, 0:cut, :], left),
        )
        return first, (p, left, right, nxt, prv, ref, n, cut, got, self.passing[step].at[k])

    def reduce_pass(self, state):
        first, (p, left, right, nxt, prv, ref, n, cut, got, passing) = state
        rows = self.rows
        first[0].wait_recv()
        passing[0:cut, :] = (ref[rows(nxt * n, cut), :].astype(f32) + got[0, 0:cut, :].astype(f32)).astype(bf16)
        second = [self.copy(passing.at[0:cut, :], got.at[2, 0:cut, :], right)]
        first[1].wait_recv()
        passing[cut:n, :] = (ref[rows(prv * n + cut, n - cut), :].astype(f32) + got[0, cut:n, :].astype(f32)).astype(bf16)
        second.append(self.copy(passing.at[cut:n, :], got.at[2, cut:n, :], left))
        return second

    def reduce_end_direct(self, state, dst):
        copies, (p, ref, n, got) = state
        for c in copies:
            c.wait_recv()
        dst[...] = (ref[self.rows(p * n, n), :].astype(f32) + got[0].astype(f32) + got[1].astype(f32) + got[2].astype(f32)).astype(bf16)
        for c in copies:
            c.wait_send()

    def reduce_end(self, state, second, dst):
        first, (p, left, right, nxt, prv, ref, n, cut, got, passing) = state
        for c in (first[2], first[3], *second):
            c.wait_recv()
        dst[...] = (ref[self.rows(p * n, n), :].astype(f32) + got[1].astype(f32) + got[2].astype(f32)).astype(bf16)
        for c in (*first, *second):
            c.wait_send()

    def gather_start(self, step, ref, axis, base):
        p, left, right, over = self.sides[axis]
        n, cut = (self.big, self.little)[step], self.cuts[step]

        def send(chunk, head, target):
            spot = self.rows(base + chunk * n + (0 if head else cut), cut if head else n - cut)
            return self.copy(ref.at[spot, :], ref.at[spot, :], target)

        if step == 1:
            spot = self.rows(base + p * n, n)
            return [self.copy(ref.at[spot, :], ref.at[spot, :], target) for target in (right, left, over)]
        return (send(p, True, right), send(p, False, left), send(p, False, right), send(p, True, left)), (p, left, right, send)

    def gather_pass(self, state):
        first, (p, left, right, send) = state
        first[0].wait_recv()
        second = [send((p + 3) % 4, True, right)]
        first[1].wait_recv()
        second.append(send((p + 1) % 4, False, left))
        return second

    def gather_end(self, state, second):
        for c in (*state[0][2:], *second):
            c.wait_recv()
        for c in (*state[0], *second):
            c.wait_send()

    def one_start(self):
        self.state = [self.reduce_start(0, self.parts.at[k], "xy"[k], k) for k in range(2)]

    def one_pass(self):
        self.second = [self.reduce_pass(state) for state in self.state]

    def two_start(self):
        for k in range(2):
            self.reduce_end(self.state[k], self.second[k], self.mid.at[k])
        self.state = [self.reduce_start(1, self.mid.at[k], "yx"[k], k) for k in range(2)]

    def z_start(self):
        for k in range(2):
            self.reduce_end_direct(self.state[k], self.ends.at[2 + k])
        self.over = [self.copy(self.ends.at[2 + k], self.got_z.at[k], self.across) for k in range(2)]

    def back_start(self):
        x, y = self.here
        self.state = []
        for k in range(2):
            base = (x, y)[k] * self.big
            at = base + (y, x)[k] * self.little
            self.over[k].wait()
            self.out[k, self.rows(at, self.little), :] = (self.ends[2 + k].astype(f32) + self.got_z[k].astype(f32)).astype(bf16)
            self.state.append(self.gather_start(1, self.out.at[k], "yx"[k], base))

    def last_start(self):
        for c in (*self.state[0], *self.state[1]):
            c.wait()
        self.state = [self.gather_start(0, self.out.at[k], "xy"[k], 0) for k in range(2)]

    def last_pass(self):
        self.second = [self.gather_pass(state) for state in self.state]

    def last_end(self):
        for k in range(2):
            self.gather_end(self.state[k], self.second[k])


def sum_scratch(total_rows):
    big, little = total_rows // 4, total_rows // 16
    return [
        pltpu.VMEM((2, 3, big, HALF), bf16),
        pltpu.VMEM((2, 3, little, HALF), bf16),
        pltpu.VMEM((2, little, HALF), bf16),
        pltpu.VMEM((2, big, HALF), bf16),
        pltpu.VMEM((4, little, HALF), bf16),
        pltpu.VMEM((2, big, HALF), bf16),
    ]


def make_gather(sides, copy):
    def start(axis, ref, base, n, cut, unit):
        p, left, right, over = sides[axis]

        def rows(chunk, first):
            at = base + chunk * n + (0 if first else cut)
            return pl.ds(pl.multiple_of(at, unit), cut if first else n - cut)

        def send(chunk, first, target):
            spot = rows(chunk, first)
            return copy(ref.at[spot, :], ref.at[spot, :], target)

        first = (send(p, True, right), send(p, False, left), send(p, False, right), send(p, True, left))
        return first, (p, left, right, send)

    def start_direct(axis, ref, base, n, unit):
        p, *targets = sides[axis]
        spot = pl.ds(pl.multiple_of(base + p * n, unit), n)
        return [copy(ref.at[spot, :], ref.at[spot, :], target) for target in targets]

    def onward(state):
        first, (p, left, right, send) = state
        first[0].wait_recv()
        second = [send((p + 3) % 4, True, right)]
        first[1].wait_recv()
        second.append(send((p + 1) % 4, False, left))
        return second

    def end(state, second):
        for c in (*state[0][2:], *second):
            c.wait_recv()
        for c in (*state[0], *second):
            c.wait_send()

    def both(refs, orders, base, sizes, unit):
        n, cut = sizes[0]
        direct = [c for k in range(2) for c in start_direct(orders[k][0], refs[k], base[k], n, unit)]
        for c in direct:
            c.wait()
        n, cut = sizes[1]
        states = [start(orders[k][1], refs[k], 0, n, cut, unit) for k in range(2)]
        seconds = [onward(state) for state in states]
        for state, second in zip(states, seconds):
            end(state, second)

    return both


def orth_factors(here, sides, sibling, over_z, over_z_next, copy, at, piece, got, halves, gram, gram_low, poly, factor, factor_low, q_all, small_step):
    x, y, z, shard = here
    gather = make_gather(sides, copy)
    n = D // 16
    sib, par = shard + 1 - 2 * (shard % 2), (shard + 2) % 4
    ps = (sib + 2) % 4
    sums = [copy(piece.at[sib], got.at[0], sibling)]
    for k in range(2):
        sums.append(copy(piece.at[par, k], got.at[1, k], over_z[k]))
        sums.append(copy(piece.at[ps, k], got.at[2, k], over_z_next[k]))
    for c in sums:
        c.wait_recv()
    for k in range(2):
        halves[k, pl.ds(at[k], n), :] = piece[shard, k] + got[0, k] + got[1, k] + got[2, k]
    orders = (("y", "x"), ("x", "y"))
    base = (x * 4 * n, y * 4 * n)
    gather([halves.at[0], halves.at[1]], orders, base, ((n, 24), (4 * n, 2 * n)), 8)
    for c in sums:
        c.wait_send()

    tile = 256
    blocks = D // tile

    def eye(r, width, first):
        return (lax.broadcasted_iota(jnp.int32, (tile, width), 0) + r * tile == lax.broadcasted_iota(jnp.int32, (tile, width), 1) + first).astype(f32)

    trace = jnp.zeros((1, 1), f32)
    for r in range(blocks):
        for k in range(2):
            part = halves[k, r * tile : (r + 1) * tile, :] * eye(r, HALF, k * HALF)
            trace = trace + jnp.sum(jnp.sum(part, axis=1, keepdims=True), axis=0, keepdims=True)
    inv = 1.0 / (jnp.sqrt(trace) + 1e-07)
    for r in range(blocks):
        spot = slice(r * tile, (r + 1) * tile)
        for k in range(2):
            cols = slice(k * HALF, k * HALF + HALF)
            g = halves[k, spot, :] * (inv * inv)
            gram[spot, cols] = g
            gram_low[0, spot, cols] = g.astype(bf16)

    for k in range(4):
        small_step()
        now, later = k % 2, (k + 1) % 2

        def poly_rows(r):
            spot = slice(r * tile, (r + 1) * tile)
            poly[spot, :] = (poly_b * gram[spot, :] + poly_c * dot(gram_low[now, spot, :], gram_low[now])).astype(bf16)

        def update_rows(r):
            spot = slice(r * tile, (r + 1) * tile)
            p = poly[spot, :]
            if k == 0:
                q = p.astype(f32) + poly_a * eye(r, D, 0)
            else:
                q = poly_a * factor[spot, :] + dot(p, factor_low[now])
            factor[spot, :] = q
            if k < 3:
                factor_low[later, spot, :] = q.astype(bf16)
                t = poly_a * gram[spot, :] + dot(p, gram_low[now])
                g = poly_a * t + dot(t.astype(bf16), poly[...])
                gram[spot, :] = g
                gram_low[later, spot, :] = g.astype(bf16)

        for r in range(blocks):
            poly_rows(r)
        for r in range(blocks):
            update_rows(r)
    small_step()
    q_all[shard, 0] = (factor[0:HALF, 0:HALF] * inv).astype(bf16)
    q_all[shard, 1] = (factor[0:HALF, HALF:D] * inv).astype(bf16)
    q_all[shard, 2] = (factor[HALF:D, HALF:D] * inv).astype(bf16)
    top, low_part = pl.ds(0, HALF // 2), pl.ds(HALF // 2, HALF // 2)
    cross = []
    for k in range(2):
        for block, spot in ((1, (top, low_part)[k]), (2 * k, pl.ds(0, HALF))):
            view = q_all.at[shard, block, spot, :]
            cross.append((copy(view, view, over_z[k]), block, spot))
    near = copy(q_all.at[shard], q_all.at[shard], sibling)
    away = (shard + 2) % 4
    onward = []
    for c, block, spot in (cross[0], cross[2], cross[1], cross[3]):
        c.wait_recv()
        view = q_all.at[away, block, spot, :]
        onward.append(copy(view, view, sibling))
    near.wait_recv()
    for c in onward:
        c.wait_recv()
    for c in (*[c for c, block, spot in cross], near, *onward):
        c.wait_send()


def block_kernel(
    x_ref, cot_ref, length_ref, order_ref, wq_hbm, wo_hbm, wf_hbm, wp_hbm, mq_hbm, mo_hbm, mf_hbm, mp_hbm, small_ref,
    out_ref, dx_ref, sums_one, sums_two, small_out, q_all, u_fc,
    nrm, mlow, nrm2, branch, mixed, probs, bias, head_out, part, got, passing, wo32, wf32, wp32, wq, wo, wf, wp,
    gact, act, gpre, gheads, gmixed, xhat1, xhat2, resid, gres, parts_one, parts_two, *rest,
):
    one_refs, two_refs = rest[:6], rest[6:12]
    momq, small, qkv_bias, row_place, uq, piece, gram_got, halves, gram_low, poly, factor_low = rest[12:23]
    small_got, send, recv, local = rest[23:]
    x, y, z, shard = place()
    sib = shard + 1 - 2 * (shard % 2)
    par = (shard + 2) % 4
    sibling, partner = device(x, y, z, sib), device(x, y, z, par)
    sides = {
        "x": (x, *[device((x + d) % 4, y, z, shard) for d in (3, 1, 2)]),
        "y": (y, *[device(x, (y + d) % 4, z, shard) for d in (3, 1, 2)]),
    }
    across = device(x, y, 1 - z, shard)
    far_sib = (sib + 2) % 4
    partners = (sibling, partner, device(x, y, z, far_sib), device(x, y, 1 - z, par), device(x, y, 1 - z, far_sib), *sides["x"][1:], *sides["y"][1:], across)
    barrier = pltpu.get_barrier_semaphore()
    for other in partners:
        pl.semaphore_signal(barrier, inc=1, device_id=other, device_id_type=MESH)
    loads = [pltpu.make_async_copy(src, dst, local.at[k]) for k, (src, dst) in enumerate(((wq_hbm, momq), (wo_hbm, wo32), (wf_hbm, wf32), (wp_hbm, wp32)))]
    for load in loads:
        load.start()

    rows = BLOCK

    def chunk(index, size=rows, at=0):
        return pl.ds(pl.multiple_of(index * rows + at, 16), size)

    own, own_sib, own_par, own_ps = chunk(shard), chunk(sib), chunk(par), chunk((sib + 2) % 4)
    near = pl.multiple_of((shard // 2) * 256, 256)
    far = pl.multiple_of(256 - near, 256)
    used = [0]

    free = list(range(SENDS))

    class Copy:
        def __init__(self, src, dst, target):
            self.slot = free.pop(0)
            self.copy = pltpu.make_async_remote_copy(
                src_ref=src, dst_ref=dst, send_sem=send.at[self.slot], recv_sem=recv.at[used[0]], device_id=target, device_id_type=MESH
            )
            used[0] += 1
            self.copy.start()

        def wait_recv(self):
            self.copy.wait_recv()

        def wait_send(self):
            self.copy.wait_send()
            free.append(self.slot)

        def wait(self):
            self.wait_recv()
            self.wait_send()

    copy = Copy
    sum_one = GroupSum(sides, across, copy, (x, y), 2 * D, parts_one, sums_one, *one_refs)
    sum_two = GroupSum(sides, across, copy, (x, y), D, parts_two, sums_two, *two_refs)
    steps = [
        sibling,
        partner,
        across,
        device(x + 1 - 2 * (x % 2), y, z, shard),
        device(3 - x, y, z, shard),
        device(x, y + 1 - 2 * (y % 2), z, shard),
        device(x, 3 - y, z, shard),
    ]
    small_copies = []

    def small_step():
        k = len(small_copies)
        if k > 0:
            small_copies[-1].wait()
            small_out[...] += small_got[k - 1]
        if k < len(steps):
            small_copies.append(copy(small_out, small_got.at[k], steps[k]))

    one_way, both_ways = (partner, partner), (partner, device(x, y, 1 - z, par))

    class Spread:
        def __init__(self, ref, ways):
            self.ref = ref
            self.cross = [self.to(shard, 64 * i, ways[i]) for i in range(2)]
            self.direct = copy(ref.at[own, :], ref.at[own, :], sibling)

        def to(self, index, at, target):
            spot = chunk(index, 64, at)
            return copy(self.ref.at[spot, :], self.ref.at[spot, :], target)

        def near(self):
            self.direct.wait_recv()

        def far(self):
            onward = []
            for i in range(2):
                self.cross[i].wait_recv()
                onward.append(self.to(par, 64 * i, sibling))
            for c in onward:
                c.wait_recv()
            for c in (*self.cross, self.direct, *onward):
                c.wait_send()

    class Fold:
        def __init__(self, k, ways):
            self.k, self.ways = k, ways

        def start_far(self):
            self.a = copy(part.at[self.k, own_ps, :], got.at[self.k, 0], sibling)

        def start_near(self):
            self.b = copy(part.at[self.k, own_sib, :], got.at[self.k, 1], sibling)

        def cross(self):
            self.a.wait_recv()
            passing[self.k] = (part[self.k, own_par, :].astype(f32) + got[self.k, 0].astype(f32)).astype(bf16)
            halves = (pl.ds(0, 64), pl.ds(64, 64))
            self.c = [copy(passing.at[self.k, spot, :], got.at[self.k, 2, spot, :], way) for spot, way in zip(halves, self.ways)]

        def end(self):
            self.b.wait_recv()
            for c in self.c:
                c.wait_recv()
            for c in (self.a, self.b, *self.c):
                c.wait_send()
            return part[self.k, own, :].astype(f32) + got[self.k, 1].astype(f32) + got[self.k, 2].astype(f32)

    def norm(v):
        centred = v - jnp.mean(v, axis=-1, keepdims=True)
        r = lax.rsqrt(jnp.mean(centred * centred, axis=-1, keepdims=True) + norm_eps)
        return centred * r, r

    def norm_grad(xhat, r, gain, c):
        cg = c * gain
        return r * (cg - jnp.mean(cg, -1, keepdims=True) - xhat * jnp.mean(cg * xhat, -1, keepdims=True))

    def total(v):
        return jnp.sum(v, axis=0, keepdims=True)

    nt, tn = ((1,), (1,)), ((0,), (0,))
    hc = wq.shape[0] // 3
    heads = hc // HD
    scale = HD ** -0.5

    small[...] = small_ref[...].astype(bf16).astype(f32)
    length = length_ref[0]

    def places(slot, axis):
        return lax.broadcasted_iota(jnp.int32, (rows, 1) if axis == 0 else (1, rows), axis) + order_ref[0, slot] * rows

    live = (places(shard, 0) < length).astype(f32)
    xf = x_ref[...].astype(f32)
    hat, r_one = norm(xf)
    xhat1[...] = hat
    nrm[own, :] = (hat * small[0:1, :] + small[1:2, :]).astype(bf16)
    mlow[own, :] = (cot_ref[...] * live).astype(bf16)
    pl.semaphore_wait(barrier, len(partners))
    go_nrm = Spread(nrm, one_way)
    go_mlow = Spread(mlow, both_ways)
    for slot in range(4):
        row_place[:, slot * rows : (slot + 1) * rows] = places(slot, 1)
    row = row_place[...]
    for slot in range(4):
        bias[slot * rows : (slot + 1) * rows, :] = jnp.where((row <= places(slot, 0)) & (row < length), 0.0, masked_score)
    for part_of, line in ((0, 4), (2, 5)):
        mine = jnp.zeros((1, hc), f32)
        for s in range(4):
            mine = jnp.where(shard == s, small[line : line + 1, s * hc : (s + 1) * hc], mine)
        qkv_bias[:, part_of * hc : (part_of + 1) * hc] = mine
    qkv_bias[:, hc : 2 * hc] = jnp.zeros((1, hc), f32)
    fc_bias = small[pl.ds(7 + shard, 1), :]
    loads[0].wait()
    wq[...] = momq[...].astype(bf16)
    loads[1].wait()
    wo[...] = wo32[...].astype(bf16)

    def mix(at):
        spot = pl.ds(at, 256)
        mixed[spot, :] = (dot(nrm[spot, :], wq[...], nt) + qkv_bias[...]).astype(bf16)

    go_nrm.near()
    mix(near)
    go_nrm.far()
    mix(far)

    def head(h, part_of):
        lo = part_of * hc + h * HD
        return slice(lo, lo + HD)

    for h in range(heads):

        def attend(i, carry):
            spot = pl.ds(pl.multiple_of(i * 256, 256), 256)
            s = dot(mixed[spot, head(h, 0)], mixed[:, head(h, 1)], nt) * scale + bias[spot, :]
            e = jnp.exp(s - jnp.max(s, axis=-1, keepdims=True))
            p = (e * (1.0 / jnp.sum(e, axis=-1, keepdims=True))).astype(bf16)
            probs[h, spot, :] = p
            head_out[spot, head(h, 0)] = dot(p, mixed[:, head(h, 2)]).astype(bf16)
            return carry

        lax.fori_loop(0, 2, attend, 0)

    fold = Fold(0, one_way)
    part[0, pl.ds(far, 256), :] = dot(head_out[pl.ds(far, 256), :], wo[...]).astype(bf16)
    fold.start_far()
    part[0, pl.ds(near, 256), :] = dot(head_out[pl.ds(near, 256), :], wo[...]).astype(bf16)
    fold.start_near()
    fold.cross()
    go_mlow.near()
    go_mlow.far()
    loads[2].wait()
    wf[...] = wf32[...].astype(bf16)
    loads[3].wait()
    wp[...] = wp32[...].astype(bf16)

    mom_loads = [pltpu.make_async_copy(src, dst, local.at[4 + k]) for k, (src, dst) in enumerate(((mo_hbm, wo32), (mf_hbm, wf32), (mp_hbm, wp32), (mq_hbm, momq)))]
    for load in mom_loads:
        load.start()

    def activation_grad(i, carry):
        spot = pl.ds(pl.multiple_of(i * 256, 256), 256)
        gact[spot, :] = dot(mlow[spot, :], wp[...], nt)
        return carry

    lax.fori_loop(0, 2, activation_grad, 0)
    res = x_ref[...].astype(f32) + fold.end() + small[6:7, :]
    resid[...] = res
    hat, r_two = norm(res)
    xhat2[...] = hat
    nrm2[own, :] = (hat * small[2:3, :] + small[3:4, :]).astype(bf16)
    go_nrm2 = Spread(nrm2, both_ways)

    def feed(at):
        spot = pl.ds(at, 256)
        hidden = dot(nrm2[spot, :], wf[...]) + fc_bias
        k = 0.7978845608028654
        square = hidden * hidden
        t = jnp.tanh(k * (hidden + 0.044715 * hidden * square))
        half = 0.5 * (1.0 + t)
        act[spot, :] = (hidden * half).astype(bf16)
        slope = half + 0.5 * hidden * (1.0 - t * t) * (k + (3 * 0.044715 * k) * square)
        gpre[spot, :] = (slope * gact[spot, :]).astype(bf16)

    go_nrm2.near()
    feed(near)
    go_nrm2.far()
    feed(far)
    fold = Fold(1, both_ways)
    part[1, pl.ds(far, 256), :] = dot(gpre[pl.ds(far, 256), :], wf[...], nt).astype(bf16)
    fold.start_far()
    part[1, pl.ds(near, 256), :] = dot(gpre[pl.ds(near, 256), :], wf[...], nt).astype(bf16)
    fold.start_near()
    fold.cross()

    def grad_columns(parts, base, left, right, width):
        for c in range(left.shape[1] // width):
            value = dot(left[:, c * width : (c + 1) * width], right[...], tn).astype(bf16)
            spot = pl.ds(base + c * width, width)
            parts[0, spot, :] = value[:, :HALF]
            parts[1, spot, :] = value[:, HALF:]

    grad_columns(parts_one, 0, nrm2, gpre, 256)
    grad_columns(parts_one, D, act, mlow, 256)
    sum_one.one_start()
    small_out[11:12, :] = total(mlow[own, :].astype(f32))
    c_two = fold.end()
    hat = xhat2[...]
    small_out[2:3, :] = total(c_two * hat)
    small_out[3:4, :] = total(c_two)
    g = cot_ref[...] * live + norm_grad(hat, r_two, small[2:3, :], c_two)
    gres[...] = g
    branch[own, :] = g.astype(bf16)
    go_branch = Spread(branch, one_way)
    sum_one.one_pass()
    small_out[6:7, :] = total(branch[own, :].astype(f32))
    pre_sum = total(gpre[...].astype(f32))
    small_out[7:11, :] = jnp.where(lax.broadcasted_iota(jnp.int32, (4, D), 0) == shard, pre_sum, 0.0)

    def head_grads(at):
        spot = pl.ds(at, 256)
        gheads[spot, :] = dot(branch[spot, :], wo[...], nt).astype(bf16)

    fold_out = Fold(2, both_ways)
    part[2, pl.ds(far, 256), :] = dot(act[pl.ds(far, 256), :], wp[...]).astype(bf16)
    fold_out.start_far()
    part[2, pl.ds(near, 256), :] = dot(act[pl.ds(near, 256), :], wp[...]).astype(bf16)
    fold_out.start_near()
    go_branch.near()
    head_grads(near)
    go_branch.far()
    head_grads(far)
    fold_out.cross()
    sum_one.two_start()
    for h in range(heads):
        q, k, v = (mixed[:, head(h, i)] for i in range(3))
        gh = gheads[:, head(h, 0)]
        gmixed[:, head(h, 2)] = dot(gh, probs[h], tn).T.astype(bf16)

        def scores_grad(i, carry):
            spot = pl.ds(pl.multiple_of(i * 256, 256), 256)
            p = probs[h, spot, :].astype(f32)
            gp = dot(gheads[spot, head(h, 0)], mixed[:, head(h, 2)], nt)
            gs = (p * (gp - jnp.sum(p * gp, axis=-1, keepdims=True))).astype(bf16)
            probs[h, spot, :] = gs
            gmixed[spot, head(h, 0)] = (dot(gs, mixed[:, head(h, 1)]) * scale).astype(bf16)
            return carry

        lax.fori_loop(0, 2, scores_grad, 0)
        gmixed[:, head(h, 1)] = (dot(q, probs[h], tn).T * scale).astype(bf16)
        if h == 1:
            sum_one.z_start()

    fold = Fold(3, one_way)
    part[3, pl.ds(far, 256), :] = dot(gmixed[pl.ds(far, 256), :], wq[...]).astype(bf16)
    fold.start_far()
    part[3, pl.ds(near, 256), :] = dot(gmixed[pl.ds(near, 256), :], wq[...]).astype(bf16)
    fold.start_near()
    grad_columns(parts_two, 0, head_out, branch, hc)
    grad_columns(parts_two, hc, gmixed, nrm, hc)
    sum_two.one_start()
    fold.cross()
    mixed_sum = total(gmixed[...].astype(f32))
    spread_out = (lax.broadcasted_iota(jnp.int32, (hc, D), 0) + shard * hc == lax.broadcasted_iota(jnp.int32, (hc, D), 1)).astype(f32)
    for row, lo in ((4, 0), (5, 2 * hc)):
        small_out[row : row + 1, :] = jnp.dot(mixed_sum[:, lo : lo + hc], spread_out, precision=lax.Precision.HIGHEST, preferred_element_type=f32)
    out_ref[...] = ((resid[...] + fold_out.end() + small[11:12, :]) * live).astype(bf16)
    sum_two.one_pass()
    sum_one.back_start()
    c_one = fold.end()
    hat = xhat1[...]
    small_out[0:1, :] = total(c_one * hat)
    small_out[1:2, :] = total(c_one)
    small_step()
    dx_ref[...] = gres[...] + norm_grad(hat, r_one, small[0:1, :], c_one)
    sum_two.two_start()
    sum_one.last_start()
    small_step()
    sum_two.z_start()
    sum_one.last_pass()
    sum_two.back_start()
    small_step()
    sum_one.last_end()

    def update(u, base, mom, sums):
        count = u.shape[0]
        for k in range(2):
            cols = slice(k * HALF, k * HALF + HALF)
            g = sums[k, base : base + count, :].astype(f32)
            u[:, cols] = (g + momentum_decay * (momentum_decay * mom[:, cols] + g)).astype(bf16)

    n = D // 16
    at = (pl.multiple_of((x * 4 + y) * n, 16), pl.multiple_of((y * 4 + x) * n, 16))

    def gram_rows(m, u, whole):
        for k in range(2):
            cols = slice(k * HALF, k * HALF + HALF)
            if whole:
                piece[m, k] = dot(u[pl.ds(at[k], n), :], u[cols, :], nt)
            else:
                pick = (lax.broadcasted_iota(jnp.int32, (D, n), 0) == lax.broadcasted_iota(jnp.int32, (D, n), 1) + at[k]).astype(f32).astype(bf16)
                piece[m, k] = dot(dot(u[...], pick).astype(bf16), u[:, cols], tn)

    for load in mom_loads:
        load.wait()
    update(u_fc, 0, wf32, sums_one)
    update(wp, D, wp32, sums_one)
    gram_rows(2, u_fc, True)
    gram_rows(3, wp, False)
    sum_two.last_start()
    sum_two.last_pass()
    sum_two.last_end()
    update(wo, 0, wo32, sums_two)
    update(uq, hc, momq, sums_two)
    gram_rows(1, wo, False)
    gram_rows(0, uq, False)
    over_z = [partner, device(x, y, 1 - z, par)]
    over_z_next = [device(x, y, z, (sib + 2) % 4), device(x, y, 1 - z, (sib + 2) % 4)]
    orth_factors(place(), sides, sibling, over_z, over_z_next, copy, at, piece, gram_got, halves, wf32, gram_low, poly, wp32, factor_low, q_all, small_step)
    assert used[0] <= RECVS and len(free) == SENDS


def run_block(x_own, cot, lengths, order, wq, wo, wf, wp, mq, mo, mf, mp, small):
    vm = pl.BlockSpec(memory_space=pltpu.VMEM)
    sm = pl.BlockSpec(memory_space=pltpu.SMEM)
    hbm = pl.BlockSpec(memory_space=pl.ANY)
    rows, wide = x_own.shape[0], wq.shape[0]
    hc = wide // 3
    group = 4 * rows
    vmem = pltpu.VMEM
    return pl.pallas_call(
        block_kernel,
        out_shape=(
            pltpu.VMEM((rows, D), bf16),
            pltpu.VMEM((rows, D), f32),
            pltpu.VMEM((2, 2 * D, HALF), bf16),
            pltpu.VMEM((2, D, HALF), bf16),
            pltpu.VMEM((12, D), f32),
            pltpu.VMEM((4, 3, HALF, HALF), bf16),
            pltpu.VMEM((D, D), bf16),
        ),
        in_specs=[vm, vm, sm, sm] + [hbm] * 8 + [vm],
        out_specs=(vm,) * 7,
        scratch_shapes=[
            vmem((group, D), bf16),
            vmem((group, D), bf16),
            vmem((group, D), bf16),
            vmem((group, D), bf16),
            vmem((group, wide), bf16),
            vmem((hc // HD, group, group), bf16),
            vmem((group, group), f32),
            vmem((group, hc), bf16),
            vmem((4, group, D), bf16),
            vmem((4, 3, rows, D), bf16),
            vmem((4, rows, D), bf16),
            vmem(wo.shape, f32),
            vmem(wf.shape, f32),
            vmem(wp.shape, f32),
            vmem(wq.shape, bf16),
            vmem(wo.shape, bf16),
            vmem(wf.shape, bf16),
            vmem(wp.shape, bf16),
            vmem((group, D), f32),
            vmem((group, D), bf16),
            vmem((group, D), bf16),
            vmem((group, hc), bf16),
            vmem((group, wide), bf16),
            vmem((rows, D), f32),
            vmem((rows, D), f32),
            vmem((rows, D), f32),
            vmem((rows, D), f32),
            vmem((2, 2 * D, HALF), bf16),
            vmem((2, D, HALF), bf16),
            *sum_scratch(2 * D),
            *sum_scratch(D),
            vmem((wide, D), f32),
            vmem((12, D), f32),
            vmem((1, wide), f32),
            vmem((1, group), jnp.int32),
            vmem((wide, D), bf16),
            vmem((4, 2, D // 16, HALF), f32),
            vmem((3, 2, D // 16, HALF), f32),
            vmem((2, D, HALF), f32),
            vmem((2, D, D), bf16),
            vmem((D, D), bf16),
            vmem((2, D, D), bf16),
            vmem((7, 12, D), f32),
            pltpu.SemaphoreType.DMA((SENDS,)),
            pltpu.SemaphoreType.DMA((RECVS,)),
            pltpu.SemaphoreType.DMA((8,)),
        ],
        compiler_params=pltpu.CompilerParams(collective_id=1, has_side_effects=True, vmem_limit_bytes=50 * 1024 * 1024),
    )(x_own, cot, lengths, order, wq, wo, wf, wp, mq, mo, mf, mp, small)


def finish_kernel(
    sums_one, sums_two, q_all, u_fc, out_in, dx_in, small_sum, small_params, small_first, small_second,
    wq, wo, wf, wp, mq, mo, mf, mp,
    out_ref, dx_ref, gq, go, gf, gp, nq, no, nf, np_, rq, ro, rf, rp, small_grad, first_ref, second_ref, small_new, last_bias,
):
    i = pl.program_id(0)
    nt, tn = ((1,), (1,)), ((0,), (0,))

    @pl.when(i == 0)
    def _():
        out_ref[...] = out_in[...]
        dx_ref[...] = dx_in[...]
        g = small_sum[...]
        small_grad[...] = g
        last_bias[...] = g[11:12, :]
        first = beta_one * small_first[...] + (1.0 - beta_one) * g
        second = beta_two * small_second[...] + (1.0 - beta_two) * g * g
        first_ref[...] = first
        second_ref[...] = second
        first_hat = first / (1.0 - beta_one**STEP)
        second_hat = second / (1.0 - beta_two**STEP)
        small_new[...] = small_params[...] - adam_rate * first_hat / (jnp.sqrt(second_hat) + adam_eps)

    def renew(owner, sums, base, w, m, g_out, w_out, m_out, longest, rate, rows_of=None):
        count = w.shape[0]
        keep_rate, step_rate = 1.0 - rate * muon_decay, rate * 0.2 * math.sqrt(longest)
        spot = pl.ds(pl.multiple_of(base + i * count, 16), count)
        low = []
        for k in range(2):
            cols = slice(k * HALF, k * HALF + HALF)
            g = sums[k, spot, :].astype(f32)
            moved = momentum_decay * m[:, cols] + g
            g_out[:, cols] = g
            m_out[:, cols] = moved
            low.append((g + momentum_decay * moved).astype(bf16))
        q11, q12, q22 = q_all[owner, 0], q_all[owner, 1], q_all[owner, 2]
        w_out[:, :HALF] = keep_rate * w[:, :HALF] - step_rate * (dot(low[0], q11) + dot(low[1], q12, nt))
        w_out[:, HALF:] = keep_rate * w[:, HALF:] - step_rate * (dot(low[0], q12) + dot(low[1], q22))

    renew(0, sums_two, 192, wq, mq, gq, nq, rq, 3 * D, muon_rate)
    renew(1, sums_two, 0, wo, mo, go, no, ro, D, out_rate)
    renew(3, sums_one, D, wp, mp, gp, np_, rp, FF, muon_rate)
    count = wf.shape[0]
    keep_rate, step_rate = 1.0 - muon_rate * muon_decay, muon_rate * 0.2 * math.sqrt(FF)
    spot = pl.ds(pl.multiple_of(i * count, 16), count)
    for k in range(2):
        cols = slice(k * HALF, k * HALF + HALF)
        g = sums_one[k, spot, :].astype(f32)
        gf[:, cols] = g
        rf[:, cols] = momentum_decay * mf[:, cols] + g
    half_steps = HALF // count

    @pl.when(i < half_steps)
    def _():
        at = pl.ds(pl.multiple_of(i * count, count), count)
        nf[...] = keep_rate * wf[...] - step_rate * (dot(q_all[2, 0, at, :], u_fc[:HALF, :]) + dot(q_all[2, 1, at, :], u_fc[HALF:, :]))

    @pl.when(i >= half_steps)
    def _():
        at = pl.ds(pl.multiple_of((i - half_steps) * count, count), count)
        nf[...] = keep_rate * wf[...] - step_rate * (dot(q_all[2, 1, :, at], u_fc[:HALF, :], tn) + dot(q_all[2, 2, at, :], u_fc[HALF:, :]))


def finish(kept, small, weights, moms):
    steps = 6
    vm = pl.BlockSpec(memory_space=pltpu.VMEM)

    def tiles(a):
        return pl.BlockSpec((a.shape[0] // steps, a.shape[1]), lambda i: (i, 0))

    def whole(shape):
        return pl.BlockSpec(shape, lambda i: (0, 0))

    like = [jax.ShapeDtypeStruct(w.shape, f32) for w in weights]
    flat = jax.ShapeDtypeStruct((12, D), f32)
    last = jax.ShapeDtypeStruct((1, D), f32)
    block_out, dx = kept[4], kept[5]
    own = [jax.ShapeDtypeStruct(block_out.shape, bf16), jax.ShapeDtypeStruct(dx.shape, f32)]
    return pl.pallas_call(
        finish_kernel,
        grid=(steps,),
        out_shape=(*own, *like, *like, *like, flat, flat, flat, flat, last),
        in_specs=[vm] * 10 + [tiles(w) for w in weights] * 2,
        out_specs=(whole(block_out.shape), whole(dx.shape), *([tiles(w) for w in weights] * 3), *([whole((12, D))] * 4), whole((1, D))),
        compiler_params=pltpu.CompilerParams(vmem_limit_bytes=24 * 1024 * 1024),
    )(*kept, *small, *weights, *moms)


def shards(block_input, cotangent, lengths, block_order, w_qkv, w_out, w_fc, w_proj, mom_qkv, mom_out, mom_fc, mom_proj, small_params, small_first, small_second):
    cube = w_qkv.shape

    def turned(a):
        return a.transpose(1, 2, 0).reshape(-1, D)

    def back(a):
        return a.reshape(cube[1], cube[2], D).transpose(2, 0, 1)

    weights = (turned(w_qkv), w_out, w_fc, w_proj)
    moms = (turned(mom_qkv), mom_out, mom_fc, mom_proj)
    block_output, input_grad, sums_one, sums_two, small_sum, factors, u_fc = run_block(block_input, cotangent, lengths, block_order, *weights, *moms, small_params)
    kept = [sums_one, sums_two, factors, u_fc, block_output, input_grad, small_sum]
    kept = [pltpu.with_memory_space_constraint(a, pltpu.VMEM) for a in kept]
    weights, moms = ([pltpu.with_memory_space_constraint(a, pltpu.HBM) for a in group] for group in (weights, moms))
    block_output, input_grad, gq, go, gf, gp, nq, no, nf, np_, rq, ro, rf, rp, grad_small, first, second, new_small, last = finish(
        kept, (small_params, small_first, small_second), weights, moms
    )
    return (
        block_output, input_grad, back(gq), go, gf, gp, grad_small, back(nq), no, nf, np_, back(rq), ro, rf, rp, first, second, new_small, last[0],
    )


def solution(mesh):
    rows = P(("rep", "shard"), None)
    mats = (P(None, None, "shard"), P("shard", None), P(None, "shard"), P("shard", None))
    in_specs = (rows, rows, P("rep"), P("rep", None), *mats, *mats, P(), P(), P())
    out_specs = (rows, rows, *mats, P(), *mats, *mats, P(), P(), P(), P())
    return jax.shard_map(shards, mesh=mesh, in_specs=in_specs, out_specs=out_specs, check_vma=False)
```

```python
import math

import jax
import jax.numpy as jnp
from jax import lax
from jax.experimental import pallas as pl
from jax.experimental.pallas import tpu as pltpu
from jax.sharding import PartitionSpec as P

D = 768
HD = 64
FF = 3072
BLOCK = 128
STEP = 10
momentum_decay = 0.95
muon_rate = 0.15
out_rate = 0.75
muon_decay = 0.01
adam_rate = 0.4
beta_one = 0.9
beta_two = 0.999
adam_eps = 1e-08
norm_eps = 1e-05
poly_a = 3.4445
poly_b = -4.775
poly_c = 2.0315
masked_score = -1e30
bf16 = jnp.bfloat16
f32 = jnp.float32


def dot(left, right, dims=((1,), (0,))):
    return lax.dot_general(left, right, (dims, ((), ())), preferred_element_type=f32)


MESH = pl.DeviceIdType.MESH
HALF = 384
SENDS = 48
RECVS = 160


def place():
    rep = lax.axis_index("rep")
    return rep % 4, rep // 8, (rep // 4) % 2, lax.axis_index("shard")


def device(x, y, z, shard):
    return ((y * 2 + z) * 4 + x, shard)


class GroupSum:
    def __init__(self, sides, across, copy, here, total_rows, parts, out, got_one, got_two, got_z, pass_one, pass_two, mid):
        self.sides, self.across, self.copy, self.here = sides, across, copy, here
        self.parts, self.out, self.got, self.got_z = parts, out, (got_one, got_two), got_z
        self.passing, self.mid, self.ends = (pass_one, pass_two), mid, pass_two
        self.big, self.little = total_rows // 4, total_rows // 16
        self.cuts = (self.big // 2, (self.little // 2 + 15) // 16 * 16)

    @staticmethod
    def rows(start, size):
        return pl.ds(pl.multiple_of(start, 16), size)

    def reduce_start(self, step, ref, axis, k):
        p, left, right, over = self.sides[axis]
        n, cut, got = (self.big, self.little)[step], self.cuts[step], self.got[step].at[k]
        opp, nxt, prv = (p + 2) % 4, (p + 1) % 4, (p + 3) % 4
        rows, copy = self.rows, self.copy
        if step == 1:
            direct = [copy(ref.at[rows(c * n, n), :], got.at[i], target) for i, (c, target) in enumerate(((nxt, right), (prv, left), (opp, over)))]
            return direct, (p, ref, n, got)
        first = (
            copy(ref.at[rows(opp * n, cut), :], got.at[0, 0:cut, :], right),
            copy(ref.at[rows(opp * n + cut, n - cut), :], got.at[0, cut:n, :], left),
            copy(ref.at[rows(nxt * n + cut, n - cut), :], got.at[1, cut:n, :], right),
            copy(ref.at[rows(prv * n, cut), :], got.at[1, 0:cut, :], left),
        )
        return first, (p, left, right, nxt, prv, ref, n, cut, got, self.passing[step].at[k])

    def reduce_pass(self, state):
        first, (p, left, right, nxt, prv, ref, n, cut, got, passing) = state
        rows = self.rows
        first[0].wait_recv()
        passing[0:cut, :] = (ref[rows(nxt * n, cut), :].astype(f32) + got[0, 0:cut, :].astype(f32)).astype(bf16)
        second = [self.copy(passing.at[0:cut, :], got.at[2, 0:cut, :], right)]
        first[1].wait_recv()
        passing[cut:n, :] = (ref[rows(prv * n + cut, n - cut), :].astype(f32) + got[0, cut:n, :].astype(f32)).astype(bf16)
        second.append(self.copy(passing.at[cut:n, :], got.at[2, cut:n, :], left))
        return second

    def reduce_end_direct(self, state, dst):
        copies, (p, ref, n, got) = state
        for c in copies:
            c.wait_recv()
        dst[...] = (ref[self.rows(p * n, n), :].astype(f32) + got[0].astype(f32) + got[1].astype(f32) + got[2].astype(f32)).astype(bf16)
        for c in copies:
            c.wait_send()

    def reduce_end(self, state, second, dst):
        first, (p, left, right, nxt, prv, ref, n, cut, got, passing) = state
        for c in (first[2], first[3], *second):
            c.wait_recv()
        dst[...] = (ref[self.rows(p * n, n), :].astype(f32) + got[1].astype(f32) + got[2].astype(f32)).astype(bf16)
        for c in (*first, *second):
            c.wait_send()

    def gather_start(self, step, ref, axis, base):
        p, left, right, over = self.sides[axis]
        n, cut = (self.big, self.little)[step], self.cuts[step]

        def send(chunk, head, target):
            spot = self.rows(base + chunk * n + (0 if head else cut), cut if head else n - cut)
            return self.copy(ref.at[spot, :], ref.at[spot, :], target)

        if step == 1:
            spot = self.rows(base + p * n, n)
            return [self.copy(ref.at[spot, :], ref.at[spot, :], target) for target in (right, left, over)]
        return (send(p, True, right), send(p, False, left), send(p, False, right), send(p, True, left)), (p, left, right, send)

    def gather_pass(self, state):
        first, (p, left, right, send) = state
        first[0].wait_recv()
        second = [send((p + 3) % 4, True, right)]
        first[1].wait_recv()
        second.append(send((p + 1) % 4, False, left))
        return second

    def gather_end(self, state, second):
        for c in (*state[0][2:], *second):
            c.wait_recv()
        for c in (*state[0], *second):
            c.wait_send()

    def one_start(self):
        self.state = [self.reduce_start(0, self.parts.at[k], "xy"[k], k) for k in range(2)]

    def one_pass(self):
        self.second = [self.reduce_pass(state) for state in self.state]

    def two_start(self):
        for k in range(2):
            self.reduce_end(self.state[k], self.second[k], self.mid.at[k])
        self.state = [self.reduce_start(1, self.mid.at[k], "yx"[k], k) for k in range(2)]

    def z_start(self):
        for k in range(2):
            self.reduce_end_direct(self.state[k], self.ends.at[2 + k])
        self.over = [self.copy(self.ends.at[2 + k], self.got_z.at[k], self.across) for k in range(2)]

    def back_start(self):
        x, y = self.here
        self.state = []
        for k in range(2):
            base = (x, y)[k] * self.big
            at = base + (y, x)[k] * self.little
            self.over[k].wait()
            self.out[k, self.rows(at, self.little), :] = (self.ends[2 + k].astype(f32) + self.got_z[k].astype(f32)).astype(bf16)
            self.state.append(self.gather_start(1, self.out.at[k], "yx"[k], base))

    def last_start(self):
        for c in (*self.state[0], *self.state[1]):
            c.wait()
        self.state = [self.gather_start(0, self.out.at[k], "xy"[k], 0) for k in range(2)]

    def last_pass(self):
        self.second = [self.gather_pass(state) for state in self.state]

    def last_end(self):
        for k in range(2):
            self.gather_end(self.state[k], self.second[k])


def sum_scratch(total_rows):
    big, little = total_rows // 4, total_rows // 16
    return [
        pltpu.VMEM((2, 3, big, HALF), bf16),
        pltpu.VMEM((2, 3, little, HALF), bf16),
        pltpu.VMEM((2, little, HALF), bf16),
        pltpu.VMEM((2, big, HALF), bf16),
        pltpu.VMEM((4, little, HALF), bf16),
        pltpu.VMEM((2, big, HALF), bf16),
    ]


def make_gather(sides, copy):
    def start(axis, ref, base, n, cut, unit):
        p, left, right, over = sides[axis]

        def rows(chunk, first):
            at = base + chunk * n + (0 if first else cut)
            return pl.ds(pl.multiple_of(at, unit), cut if first else n - cut)

        def send(chunk, first, target):
            spot = rows(chunk, first)
            return copy(ref.at[spot, :], ref.at[spot, :], target)

        first = (send(p, True, right), send(p, False, left), send(p, False, right), send(p, True, left))
        return first, (p, left, right, send)

    def start_direct(axis, ref, base, n, unit):
        p, *targets = sides[axis]
        spot = pl.ds(pl.multiple_of(base + p * n, unit), n)
        return [copy(ref.at[spot, :], ref.at[spot, :], target) for target in targets]

    def onward(state):
        first, (p, left, right, send) = state
        first[0].wait_recv()
        second = [send((p + 3) % 4, True, right)]
        first[1].wait_recv()
        second.append(send((p + 1) % 4, False, left))
        return second

    def end(state, second):
        for c in (*state[0][2:], *second):
            c.wait_recv()
        for c in (*state[0], *second):
            c.wait_send()

    def both(refs, orders, base, sizes, unit):
        n, cut = sizes[0]
        direct = [c for k in range(2) for c in start_direct(orders[k][0], refs[k], base[k], n, unit)]
        for c in direct:
            c.wait()
        n, cut = sizes[1]
        states = [start(orders[k][1], refs[k], 0, n, cut, unit) for k in range(2)]
        seconds = [onward(state) for state in states]
        for state, second in zip(states, seconds):
            end(state, second)

    return both


def orth_factors(here, sides, sibling, over_z, over_z_next, copy, at, piece, got, halves, gram, gram_low, poly, factor_low, q_all, small_step):
    x, y, z, shard = here
    gather = make_gather(sides, copy)
    n = D // 16
    sib, par = shard + 1 - 2 * (shard % 2), (shard + 2) % 4
    ps = (sib + 2) % 4
    sums = [copy(piece.at[sib], got.at[0], sibling)]
    for k in range(2):
        sums.append(copy(piece.at[par, k], got.at[1, k], over_z[k]))
        sums.append(copy(piece.at[ps, k], got.at[2, k], over_z_next[k]))
    for c in sums:
        c.wait_recv()
    for k in range(2):
        halves[k, pl.ds(at[k], n), :] = piece[shard, k] + got[0, k] + got[1, k] + got[2, k]
    orders = (("y", "x"), ("x", "y"))
    base = (x * 4 * n, y * 4 * n)
    gather([halves.at[0], halves.at[1]], orders, base, ((n, 24), (4 * n, 2 * n)), 8)
    for c in sums:
        c.wait_send()

    tile = 256
    blocks = D // tile

    def eye(r, width, first):
        return (lax.broadcasted_iota(jnp.int32, (tile, width), 0) + r * tile == lax.broadcasted_iota(jnp.int32, (tile, width), 1) + first).astype(f32)

    trace = jnp.zeros((1, 1), f32)
    for r in range(blocks):
        for k in range(2):
            part = halves[k, r * tile : (r + 1) * tile, :] * eye(r, HALF, k * HALF)
            trace = trace + jnp.sum(jnp.sum(part, axis=1, keepdims=True), axis=0, keepdims=True)
    inv = 1.0 / (jnp.sqrt(trace) + 1e-07)
    for r in range(blocks):
        spot = slice(r * tile, (r + 1) * tile)
        for k in range(2):
            cols = slice(k * HALF, k * HALF + HALF)
            g = halves[k, spot, :] * (inv * inv)
            gram[spot, cols] = g
            gram_low[0][spot, cols] = g.astype(bf16)

    for k in range(4):
        small_step()
        now, later = k % 2, (k + 1) % 2

        def poly_rows(r):
            spot = slice(r * tile, (r + 1) * tile)
            poly[spot, :] = (poly_b * gram[spot, :] + poly_c * dot(gram_low[now][spot, :], gram_low[now][...])).astype(bf16)

        def update_rows(r):
            spot = slice(r * tile, (r + 1) * tile)
            p = poly[spot, :]
            if k == 0:
                q = p.astype(f32) + poly_a * eye(r, D, 0)
            else:
                q = poly_a * jnp.concatenate([halves[0, spot, :], halves[1, spot, :]], 1) + dot(p, factor_low[now][...])
            halves[0, spot, :] = q[:, :HALF]
            halves[1, spot, :] = q[:, HALF:]
            if k < 3:
                factor_low[later][spot, :] = q.astype(bf16)
                t = poly_a * gram[spot, :] + dot(p, gram_low[now][...])
                g = poly_a * t + dot(t.astype(bf16), poly[...])
                gram[spot, :] = g
                gram_low[later][spot, :] = g.astype(bf16)

        for r in range(blocks):
            poly_rows(r)
        for r in range(blocks):
            update_rows(r)
    small_step()
    q_all[shard, 0] = (halves[0, 0:HALF, :] * inv).astype(bf16)
    q_all[shard, 1] = (halves[1, 0:HALF, :] * inv).astype(bf16)
    q_all[shard, 2] = (halves[1, HALF:D, :] * inv).astype(bf16)
    top, low_part = pl.ds(0, HALF // 2), pl.ds(HALF // 2, HALF // 2)
    cross = []
    for k in range(2):
        for block, spot in ((1, (top, low_part)[k]), (2 * k, pl.ds(0, HALF))):
            view = q_all.at[shard, block, spot, :]
            cross.append((copy(view, view, over_z[k]), block, spot))
    near = copy(q_all.at[shard], q_all.at[shard], sibling)
    away = (shard + 2) % 4
    onward = []
    for c, block, spot in (cross[0], cross[2], cross[1], cross[3]):
        c.wait_recv()
        view = q_all.at[away, block, spot, :]
        onward.append(copy(view, view, sibling))
    near.wait_recv()
    for c in onward:
        c.wait_recv()
    for c in (*[c for c, block, spot in cross], near, *onward):
        c.wait_send()


def block_kernel(
    x_ref, cot_ref, length_ref, order_ref, wq_hbm, wo_hbm, wf_hbm, wp_hbm, mq_hbm, mo_hbm, mf_hbm, mp_hbm, small_ref,
    out_ref, dx_ref, sums_one, sums_two, small_out, q_all, u_fc, momq, wo32, wf32, wp32, wf_held, wp_held,
    tokens, mixed, probs, bias, head_out, terms, got, passing, wq, wo, wf, wp,
    gact, act, gpre, gheads, gmixed, xhat1, xhat2, resid, gres, parts_one, parts_two, *rest,
):
    one_refs, two_refs = rest[:6], rest[6:12]
    small, qkv_bias, row_place, uq, piece, gram_got, halves, gram, poly = rest[12:21]
    small_got, send, recv, local = rest[21:]
    group = 4 * BLOCK
    nrm, mlow, nrm2, branch = (tokens.at[pl.ds(k * group, group), :] for k in range(4))
    part = [terms.at[pl.ds(k * group, group), :] for k in range(4)]
    gram_low, factor_low = ([ref.at[pl.ds(k * D, D), :] for k in range(2)] for ref in (tokens, terms))
    x, y, z, shard = place()
    sib = shard + 1 - 2 * (shard % 2)
    par = (shard + 2) % 4
    sibling, partner = device(x, y, z, sib), device(x, y, z, par)
    sides = {
        "x": (x, *[device((x + d) % 4, y, z, shard) for d in (3, 1, 2)]),
        "y": (y, *[device(x, (y + d) % 4, z, shard) for d in (3, 1, 2)]),
    }
    across = device(x, y, 1 - z, shard)
    far_sib = (sib + 2) % 4
    partners = (sibling, partner, device(x, y, z, far_sib), device(x, y, 1 - z, par), device(x, y, 1 - z, far_sib), *sides["x"][1:], *sides["y"][1:], across)
    barrier = pltpu.get_barrier_semaphore()
    for other in partners:
        pl.semaphore_signal(barrier, inc=1, device_id=other, device_id_type=MESH)
    loads = [pltpu.make_async_copy(src, dst, local.at[k]) for k, (src, dst) in enumerate(((wq_hbm, momq), (wo_hbm, wo32), (wf_hbm, wf32), (wp_hbm, wp32)))]
    for load in loads:
        load.start()

    rows = BLOCK

    def chunk(index, size=rows, at=0):
        return pl.ds(pl.multiple_of(index * rows + at, 16), size)

    own, own_sib, own_par, own_ps = chunk(shard), chunk(sib), chunk(par), chunk((sib + 2) % 4)
    near = pl.multiple_of((shard // 2) * 256, 256)
    far = pl.multiple_of(256 - near, 256)
    used = [0]

    free = list(range(SENDS))

    class Copy:
        def __init__(self, src, dst, target):
            self.slot = free.pop(0)
            self.copy = pltpu.make_async_remote_copy(
                src_ref=src, dst_ref=dst, send_sem=send.at[self.slot], recv_sem=recv.at[used[0]], device_id=target, device_id_type=MESH
            )
            used[0] += 1
            self.copy.start()

        def wait_recv(self):
            self.copy.wait_recv()

        def wait_send(self):
            self.copy.wait_send()
            free.append(self.slot)

        def wait(self):
            self.wait_recv()
            self.wait_send()

    copy = Copy
    sum_one = GroupSum(sides, across, copy, (x, y), 2 * D, parts_one, sums_one, *one_refs)
    sum_two = GroupSum(sides, across, copy, (x, y), D, parts_two, sums_two, *two_refs)
    steps = [
        sibling,
        partner,
        across,
        device(x + 1 - 2 * (x % 2), y, z, shard),
        device(3 - x, y, z, shard),
        device(x, y + 1 - 2 * (y % 2), z, shard),
        device(x, 3 - y, z, shard),
    ]
    small_copies = []

    def small_step():
        k = len(small_copies)
        if k > 0:
            small_copies[-1].wait()
            small_out[...] += small_got[k - 1]
        if k < len(steps):
            small_copies.append(copy(small_out, small_got.at[k], steps[k]))

    one_way, both_ways = (partner, partner), (partner, device(x, y, 1 - z, par))

    class Spread:
        def __init__(self, ref, ways):
            self.ref = ref
            self.cross = [self.to(shard, 64 * i, ways[i]) for i in range(2)]
            self.direct = copy(ref.at[own, :], ref.at[own, :], sibling)

        def to(self, index, at, target):
            spot = chunk(index, 64, at)
            return copy(self.ref.at[spot, :], self.ref.at[spot, :], target)

        def near(self):
            self.direct.wait_recv()

        def far(self):
            onward = []
            for i in range(2):
                self.cross[i].wait_recv()
                onward.append(self.to(par, 64 * i, sibling))
            for c in onward:
                c.wait_recv()
            for c in (*self.cross, self.direct, *onward):
                c.wait_send()

    class Fold:
        def __init__(self, k, ways):
            self.k, self.ways = k, ways

        def start_far(self):
            self.a = copy(part[self.k].at[own_ps, :], got.at[self.k, 0], sibling)

        def start_near(self):
            self.b = copy(part[self.k].at[own_sib, :], got.at[self.k, 1], sibling)

        def cross(self):
            self.a.wait_recv()
            passing[self.k] = (part[self.k][own_par, :].astype(f32) + got[self.k, 0].astype(f32)).astype(bf16)
            halves = (pl.ds(0, 64), pl.ds(64, 64))
            self.c = [copy(passing.at[self.k, spot, :], got.at[self.k, 2, spot, :], way) for spot, way in zip(halves, self.ways)]

        def end(self):
            self.b.wait_recv()
            for c in self.c:
                c.wait_recv()
            for c in (self.a, self.b, *self.c):
                c.wait_send()
            return part[self.k][own, :].astype(f32) + got[self.k, 1].astype(f32) + got[self.k, 2].astype(f32)

    def norm(v):
        centred = v - jnp.mean(v, axis=-1, keepdims=True)
        r = lax.rsqrt(jnp.mean(centred * centred, axis=-1, keepdims=True) + norm_eps)
        return centred * r, r

    def norm_grad(xhat, r, gain, c):
        cg = c * gain
        return r * (cg - jnp.mean(cg, -1, keepdims=True) - xhat * jnp.mean(cg * xhat, -1, keepdims=True))

    def total(v):
        return jnp.sum(v, axis=0, keepdims=True)

    nt, tn = ((1,), (1,)), ((0,), (0,))
    hc = wq.shape[0] // 3
    heads = hc // HD
    scale = HD ** -0.5

    small[...] = small_ref[...].astype(bf16).astype(f32)
    length = length_ref[0]

    def places(slot, axis):
        return lax.broadcasted_iota(jnp.int32, (rows, 1) if axis == 0 else (1, rows), axis) + order_ref[0, slot] * rows

    live = (places(shard, 0) < length).astype(f32)
    xf = x_ref[...].astype(f32)
    hat, r_one = norm(xf)
    xhat1[...] = hat
    nrm[own, :] = (hat * small[0:1, :] + small[1:2, :]).astype(bf16)
    mlow[own, :] = (cot_ref[...] * live).astype(bf16)
    pl.semaphore_wait(barrier, len(partners))
    go_nrm = Spread(nrm, one_way)
    go_mlow = Spread(mlow, both_ways)
    for slot in range(4):
        row_place[:, slot * rows : (slot + 1) * rows] = places(slot, 1)
    row = row_place[...]
    for slot in range(4):
        bias[slot * rows : (slot + 1) * rows, :] = jnp.where((row <= places(slot, 0)) & (row < length), 0.0, masked_score)
    for part_of, line in ((0, 4), (2, 5)):
        mine = jnp.zeros((1, hc), f32)
        for s in range(4):
            mine = jnp.where(shard == s, small[line : line + 1, s * hc : (s + 1) * hc], mine)
        qkv_bias[:, part_of * hc : (part_of + 1) * hc] = mine
    qkv_bias[:, hc : 2 * hc] = jnp.zeros((1, hc), f32)
    fc_bias = small[pl.ds(7 + shard, 1), :]
    loads[0].wait()
    wq[...] = momq[...].astype(bf16)
    loads[1].wait()
    wo[...] = wo32[...].astype(bf16)

    def mix(at):
        spot = pl.ds(at, 256)
        mixed[spot, :] = (dot(nrm[spot, :], wq[...], nt) + qkv_bias[...]).astype(bf16)

    go_nrm.near()
    mix(near)
    go_nrm.far()
    mix(far)

    def head(h, part_of):
        lo = part_of * hc + h * HD
        return slice(lo, lo + HD)

    for h in range(heads):

        def attend(i, carry):
            spot = pl.ds(pl.multiple_of(i * 256, 256), 256)
            s = dot(mixed[spot, head(h, 0)], mixed[:, head(h, 1)], nt) * scale + bias[spot, :]
            e = jnp.exp(s - jnp.max(s, axis=-1, keepdims=True))
            p = (e * (1.0 / jnp.sum(e, axis=-1, keepdims=True))).astype(bf16)
            probs[h, spot, :] = p
            head_out[spot, head(h, 0)] = dot(p, mixed[:, head(h, 2)]).astype(bf16)
            return carry

        lax.fori_loop(0, 2, attend, 0)

    fold = Fold(0, one_way)
    part[0][pl.ds(far, 256), :] = dot(head_out[pl.ds(far, 256), :], wo[...]).astype(bf16)
    fold.start_far()
    part[0][pl.ds(near, 256), :] = dot(head_out[pl.ds(near, 256), :], wo[...]).astype(bf16)
    fold.start_near()
    fold.cross()
    go_mlow.near()
    go_mlow.far()
    loads[2].wait()
    wf[...] = wf32[...].astype(bf16)
    loads[3].wait()
    wp[...] = wp32[...].astype(bf16)

    mom_loads = [pltpu.make_async_copy(src, dst, local.at[4 + k]) for k, (src, dst) in enumerate(((mo_hbm, wo32), (mf_hbm, wf32), (mp_hbm, wp32), (mq_hbm, momq), (wf_hbm, wf_held), (wp_hbm, wp_held)))]
    for load in mom_loads:
        load.start()

    def activation_grad(i, carry):
        spot = pl.ds(pl.multiple_of(i * 256, 256), 256)
        gact[spot, :] = dot(mlow[spot, :], wp[...], nt)
        return carry

    lax.fori_loop(0, 2, activation_grad, 0)
    res = x_ref[...].astype(f32) + fold.end() + small[6:7, :]
    resid[...] = res
    hat, r_two = norm(res)
    xhat2[...] = hat
    nrm2[own, :] = (hat * small[2:3, :] + small[3:4, :]).astype(bf16)
    go_nrm2 = Spread(nrm2, both_ways)

    def feed(at):
        spot = pl.ds(at, 256)
        hidden = dot(nrm2[spot, :], wf[...]) + fc_bias
        k = 0.7978845608028654
        square = hidden * hidden
        t = jnp.tanh(k * (hidden + 0.044715 * hidden * square))
        half = 0.5 * (1.0 + t)
        act[spot, :] = (hidden * half).astype(bf16)
        slope = half + 0.5 * hidden * (1.0 - t * t) * (k + (3 * 0.044715 * k) * square)
        gpre[spot, :] = (slope * gact[spot, :]).astype(bf16)

    go_nrm2.near()
    feed(near)
    go_nrm2.far()
    feed(far)
    fold = Fold(1, both_ways)
    part[1][pl.ds(far, 256), :] = dot(gpre[pl.ds(far, 256), :], wf[...], nt).astype(bf16)
    fold.start_far()
    part[1][pl.ds(near, 256), :] = dot(gpre[pl.ds(near, 256), :], wf[...], nt).astype(bf16)
    fold.start_near()
    fold.cross()

    def grad_columns(parts, base, left, right, width):
        for c in range(left.shape[1] // width):
            value = dot(left[:, c * width : (c + 1) * width], right[...], tn).astype(bf16)
            spot = pl.ds(base + c * width, width)
            parts[0, spot, :] = value[:, :HALF]
            parts[1, spot, :] = value[:, HALF:]

    grad_columns(parts_one, 0, nrm2, gpre, 256)
    grad_columns(parts_one, D, act, mlow, 256)
    sum_one.one_start()
    small_out[11:12, :] = total(mlow[own, :].astype(f32))
    c_two = fold.end()
    hat = xhat2[...]
    small_out[2:3, :] = total(c_two * hat)
    small_out[3:4, :] = total(c_two)
    g = cot_ref[...] * live + norm_grad(hat, r_two, small[2:3, :], c_two)
    gres[...] = g
    branch[own, :] = g.astype(bf16)
    go_branch = Spread(branch, one_way)
    sum_one.one_pass()
    small_out[6:7, :] = total(branch[own, :].astype(f32))
    pre_sum = total(gpre[...].astype(f32))
    small_out[7:11, :] = jnp.where(lax.broadcasted_iota(jnp.int32, (4, D), 0) == shard, pre_sum, 0.0)

    def head_grads(at):
        spot = pl.ds(at, 256)
        gheads[spot, :] = dot(branch[spot, :], wo[...], nt).astype(bf16)

    fold_out = Fold(2, both_ways)
    part[2][pl.ds(far, 256), :] = dot(act[pl.ds(far, 256), :], wp[...]).astype(bf16)
    fold_out.start_far()
    part[2][pl.ds(near, 256), :] = dot(act[pl.ds(near, 256), :], wp[...]).astype(bf16)
    fold_out.start_near()
    go_branch.near()
    head_grads(near)
    go_branch.far()
    head_grads(far)
    fold_out.cross()
    sum_one.two_start()
    for h in range(heads):
        q, k, v = (mixed[:, head(h, i)] for i in range(3))
        gh = gheads[:, head(h, 0)]
        gmixed[:, head(h, 2)] = dot(gh, probs[h], tn).T.astype(bf16)

        def scores_grad(i, carry):
            spot = pl.ds(pl.multiple_of(i * 256, 256), 256)
            p = probs[h, spot, :].astype(f32)
            gp = dot(gheads[spot, head(h, 0)], mixed[:, head(h, 2)], nt)
            gs = (p * (gp - jnp.sum(p * gp, axis=-1, keepdims=True))).astype(bf16)
            probs[h, spot, :] = gs
            gmixed[spot, head(h, 0)] = (dot(gs, mixed[:, head(h, 1)]) * scale).astype(bf16)
            return carry

        lax.fori_loop(0, 2, scores_grad, 0)
        gmixed[:, head(h, 1)] = (dot(q, probs[h], tn).T * scale).astype(bf16)

    grad_columns(parts_two, 0, head_out, branch, hc)
    grad_columns(parts_two, hc, gmixed, nrm, hc)
    sum_two.one_start()
    sum_one.z_start()
    fold = Fold(3, one_way)
    part[3][pl.ds(far, 256), :] = dot(gmixed[pl.ds(far, 256), :], wq[...]).astype(bf16)
    fold.start_far()
    part[3][pl.ds(near, 256), :] = dot(gmixed[pl.ds(near, 256), :], wq[...]).astype(bf16)
    fold.start_near()
    fold.cross()
    mixed_sum = total(gmixed[...].astype(f32))
    spread_out = (lax.broadcasted_iota(jnp.int32, (hc, D), 0) + shard * hc == lax.broadcasted_iota(jnp.int32, (hc, D), 1)).astype(f32)
    for row, lo in ((4, 0), (5, 2 * hc)):
        small_out[row : row + 1, :] = jnp.dot(mixed_sum[:, lo : lo + hc], spread_out, precision=lax.Precision.HIGHEST, preferred_element_type=f32)
    out_ref[...] = ((resid[...] + fold_out.end() + small[11:12, :]) * live).astype(bf16)
    sum_two.one_pass()
    sum_one.back_start()
    sum_two.two_start()
    c_one = fold.end()
    hat = xhat1[...]
    small_out[0:1, :] = total(c_one * hat)
    small_out[1:2, :] = total(c_one)
    small_step()
    dx_ref[...] = gres[...] + norm_grad(hat, r_one, small[0:1, :], c_one)
    sum_one.last_start()
    small_step()
    sum_two.z_start()
    sum_one.last_pass()
    sum_two.back_start()
    small_step()

    def update(u, base, mom, sums):
        count = u.shape[0]
        for k in range(2):
            cols = slice(k * HALF, k * HALF + HALF)
            g = sums[k, base : base + count, :].astype(f32)
            u[:, cols] = (g + momentum_decay * (momentum_decay * mom[:, cols] + g)).astype(bf16)

    n = D // 16
    at = (pl.multiple_of((x * 4 + y) * n, 16), pl.multiple_of((y * 4 + x) * n, 16))

    def gram_rows(m, u, whole):
        for k in range(2):
            cols = slice(k * HALF, k * HALF + HALF)
            if whole:
                piece[m, k] = dot(u[pl.ds(at[k], n), :], u[cols, :], nt)
            else:
                pick = (lax.broadcasted_iota(jnp.int32, (D, n), 0) == lax.broadcasted_iota(jnp.int32, (D, n), 1) + at[k]).astype(f32).astype(bf16)
                piece[m, k] = dot(dot(u[...], pick).astype(bf16), u[:, cols], tn)

    sum_two.last_start()
    sum_one.last_end()
    for load in mom_loads:
        load.wait()
    update(u_fc, 0, wf32, sums_one)
    update(wp, D, wp32, sums_one)
    gram_rows(2, u_fc, True)
    gram_rows(3, wp, False)
    sum_two.last_pass()
    sum_two.last_end()
    update(wo, 0, wo32, sums_two)
    update(uq, hc, momq, sums_two)
    gram_rows(1, wo, False)
    gram_rows(0, uq, False)
    over_z = [partner, device(x, y, 1 - z, par)]
    over_z_next = [device(x, y, z, (sib + 2) % 4), device(x, y, 1 - z, (sib + 2) % 4)]
    orth_factors(place(), sides, sibling, over_z, over_z_next, copy, at, piece, gram_got, halves, gram, gram_low, poly, factor_low, q_all, small_step)
    assert used[0] <= RECVS and len(free) == SENDS


def run_block(x_own, cot, lengths, order, wq, wo, wf, wp, mq, mo, mf, mp, small):
    vm = pl.BlockSpec(memory_space=pltpu.VMEM)
    sm = pl.BlockSpec(memory_space=pltpu.SMEM)
    hbm = pl.BlockSpec(memory_space=pl.ANY)
    rows, wide = x_own.shape[0], wq.shape[0]
    hc = wide // 3
    group = 4 * rows
    vmem = pltpu.VMEM
    return pl.pallas_call(
        block_kernel,
        out_shape=(
            pltpu.VMEM((rows, D), bf16),
            pltpu.VMEM((rows, D), f32),
            pltpu.VMEM((2, 2 * D, HALF), bf16),
            pltpu.VMEM((2, D, HALF), bf16),
            pltpu.VMEM((12, D), f32),
            pltpu.VMEM((4, 3, HALF, HALF), bf16),
            pltpu.VMEM((D, D), bf16),
            *[pltpu.VMEM(w.shape, f32) for w in (wq, wo, wf, wp, wf, wp)],
        ),
        in_specs=[vm, vm, sm, sm] + [hbm] * 8 + [vm],
        out_specs=(vm,) * 13,
        scratch_shapes=[
            vmem((4 * group, D), bf16),
            vmem((group, wide), bf16),
            vmem((hc // HD, group, group), bf16),
            vmem((group, group), f32),
            vmem((group, hc), bf16),
            vmem((4 * group, D), bf16),
            vmem((4, 3, rows, D), bf16),
            vmem((4, rows, D), bf16),
            vmem(wq.shape, bf16),
            vmem(wo.shape, bf16),
            vmem(wf.shape, bf16),
            vmem(wp.shape, bf16),
            vmem((group, D), f32),
            vmem((group, D), bf16),
            vmem((group, D), bf16),
            vmem((group, hc), bf16),
            vmem((group, wide), bf16),
            vmem((rows, D), f32),
            vmem((rows, D), f32),
            vmem((rows, D), f32),
            vmem((rows, D), f32),
            vmem((2, 2 * D, HALF), bf16),
            vmem((2, D, HALF), bf16),
            *sum_scratch(2 * D),
            *sum_scratch(D),
            vmem((12, D), f32),
            vmem((1, wide), f32),
            vmem((1, group), jnp.int32),
            vmem((wide, D), bf16),
            vmem((4, 2, D // 16, HALF), f32),
            vmem((3, 2, D // 16, HALF), f32),
            vmem((2, D, HALF), f32),
            vmem((D, D), f32),
            vmem((D, D), bf16),
            vmem((7, 12, D), f32),
            pltpu.SemaphoreType.DMA((SENDS,)),
            pltpu.SemaphoreType.DMA((RECVS,)),
            pltpu.SemaphoreType.DMA((10,)),
        ],
        compiler_params=pltpu.CompilerParams(collective_id=1, has_side_effects=True, vmem_limit_bytes=40 * 1024 * 1024),
    )(x_own, cot, lengths, order, wq, wo, wf, wp, mq, mo, mf, mp, small)


def finish_kernel(
    sums_one, sums_two, q_all, u_fc, mq, mo, mf, mp, wf, wp, out_in, dx_in, small_sum, small_params, small_first, small_second,
    wq, wo,
    out_ref, dx_ref, gq, go, gf, gp, nq, no, nf, np_, rq, ro, rf, rp, small_grad, first_ref, second_ref, small_new, last_bias,
):
    i = pl.program_id(0)
    nt, tn = ((1,), (1,)), ((0,), (0,))

    @pl.when(i == 0)
    def _():
        out_ref[...] = out_in[...]
        dx_ref[...] = dx_in[...]
        g = small_sum[...]
        small_grad[...] = g
        last_bias[...] = g[11:12, :]
        first = beta_one * small_first[...] + (1.0 - beta_one) * g
        second = beta_two * small_second[...] + (1.0 - beta_two) * g * g
        first_ref[...] = first
        second_ref[...] = second
        first_hat = first / (1.0 - beta_one**STEP)
        second_hat = second / (1.0 - beta_two**STEP)
        small_new[...] = small_params[...] - adam_rate * first_hat / (jnp.sqrt(second_hat) + adam_eps)

    def renew(owner, sums, base, w, m, g_out, w_out, m_out, longest, rate):
        count = g_out.shape[0]
        keep_rate, step_rate = 1.0 - rate * muon_decay, rate * 0.2 * math.sqrt(longest)
        spot = pl.ds(pl.multiple_of(base + i * count, 16), count)
        mine = pl.ds(pl.multiple_of(i * count, 16), count)
        held = mine if w.shape[0] > count else pl.ds(0, count)
        low = []
        for k in range(2):
            cols = slice(k * HALF, k * HALF + HALF)
            g = sums[k, spot, :].astype(f32)
            moved = momentum_decay * m[mine, cols] + g
            g_out[:, cols] = g
            m_out[:, cols] = moved
            low.append((g + momentum_decay * moved).astype(bf16))
        q11, q12, q22 = q_all[owner, 0], q_all[owner, 1], q_all[owner, 2]
        w_out[:, :HALF] = keep_rate * w[held, :HALF] - step_rate * (dot(low[0], q11) + dot(low[1], q12, nt))
        w_out[:, HALF:] = keep_rate * w[held, HALF:] - step_rate * (dot(low[0], q12) + dot(low[1], q22))

    renew(0, sums_two, 192, wq, mq, gq, nq, rq, 3 * D, muon_rate)
    renew(1, sums_two, 0, wo, mo, go, no, ro, D, out_rate)
    renew(3, sums_one, D, wp, mp, gp, np_, rp, FF, muon_rate)
    count = gf.shape[0]
    keep_rate, step_rate = 1.0 - muon_rate * muon_decay, muon_rate * 0.2 * math.sqrt(FF)
    spot = pl.ds(pl.multiple_of(i * count, 16), count)
    for k in range(2):
        cols = slice(k * HALF, k * HALF + HALF)
        g = sums_one[k, spot, :].astype(f32)
        gf[:, cols] = g
        rf[:, cols] = momentum_decay * mf[spot, cols] + g
    half_steps = HALF // count

    @pl.when(i < half_steps)
    def _():
        at = pl.ds(pl.multiple_of(i * count, count), count)
        nf[...] = keep_rate * wf[spot, :] - step_rate * (dot(q_all[2, 0, at, :], u_fc[:HALF, :]) + dot(q_all[2, 1, at, :], u_fc[HALF:, :]))

    @pl.when(i >= half_steps)
    def _():
        at = pl.ds(pl.multiple_of((i - half_steps) * count, count), count)
        nf[...] = keep_rate * wf[spot, :] - step_rate * (dot(q_all[2, 1, :, at], u_fc[:HALF, :], tn) + dot(q_all[2, 2, at, :], u_fc[HALF:, :]))


def finish(kept, small, weights):
    steps = 6
    vm = pl.BlockSpec(memory_space=pltpu.VMEM)

    def tiles(a):
        return pl.BlockSpec((a.shape[0] // steps, a.shape[1]), lambda i: (i, 0))

    def whole(shape):
        return pl.BlockSpec(shape, lambda i: (0, 0))

    like = [jax.ShapeDtypeStruct(w.shape, f32) for w in weights]
    flat = jax.ShapeDtypeStruct((12, D), f32)
    last = jax.ShapeDtypeStruct((1, D), f32)
    block_out, dx = kept[10], kept[11]
    own = [jax.ShapeDtypeStruct(block_out.shape, bf16), jax.ShapeDtypeStruct(dx.shape, f32)]
    return pl.pallas_call(
        finish_kernel,
        grid=(steps,),
        out_shape=(*own, *like, *like, *like, flat, flat, flat, flat, last),
        in_specs=[vm] * 16 + [tiles(w) for w in weights[:2]],
        out_specs=(whole(block_out.shape), whole(dx.shape), *([tiles(w) for w in weights] * 3), *([whole((12, D))] * 4), whole((1, D))),
        compiler_params=pltpu.CompilerParams(vmem_limit_bytes=24 * 1024 * 1024),
    )(*kept, *small, *weights[:2])


def shards(block_input, cotangent, lengths, block_order, w_qkv, w_out, w_fc, w_proj, mom_qkv, mom_out, mom_fc, mom_proj, small_params, small_first, small_second):
    cube = w_qkv.shape

    def turned(a):
        return a.transpose(1, 2, 0).reshape(-1, D)

    def back(a):
        return a.reshape(cube[1], cube[2], D).transpose(2, 0, 1)

    weights = (turned(w_qkv), w_out, w_fc, w_proj)
    moms = (turned(mom_qkv), mom_out, mom_fc, mom_proj)
    block_output, input_grad, sums_one, sums_two, small_sum, factors, u_fc, *held = run_block(block_input, cotangent, lengths, block_order, *weights, *moms, small_params)
    kept = [sums_one, sums_two, factors, u_fc, *held, block_output, input_grad, small_sum]
    kept = [pltpu.with_memory_space_constraint(a, pltpu.VMEM) for a in kept]
    weights = [pltpu.with_memory_space_constraint(a, pltpu.HBM) for a in weights]
    block_output, input_grad, gq, go, gf, gp, nq, no, nf, np_, rq, ro, rf, rp, grad_small, first, second, new_small, last = finish(
        kept, (small_params, small_first, small_second), weights
    )
    return (
        block_output, input_grad, back(gq), go, gf, gp, grad_small, back(nq), no, nf, np_, back(rq), ro, rf, rp, first, second, new_small, last.reshape(D),
    )


def solution(mesh):
    rows = P(("rep", "shard"), None)
    mats = (P(None, None, "shard"), P("shard", None), P(None, "shard"), P("shard", None))
    in_specs = (rows, rows, P("rep"), P("rep", None), *mats, *mats, P(), P(), P())
    out_specs = (rows, rows, *mats, P(), *mats, *mats, P(), P(), P(), P())
    return jax.shard_map(shards, mesh=mesh, in_specs=in_specs, out_specs=out_specs, check_vma=False)
```

```python
import math

import jax
import jax.numpy as jnp
from jax import lax
from jax.experimental import pallas as pl
from jax.experimental.pallas import tpu as pltpu
from jax.sharding import PartitionSpec as P

D = 768
HD = 64
FF = 3072
BLOCK = 128
STEP = 10
momentum_decay = 0.95
muon_rate = 0.15
out_rate = 0.75
muon_decay = 0.01
adam_rate = 0.4
beta_one = 0.9
beta_two = 0.999
adam_eps = 1e-08
norm_eps = 1e-05
poly_a = 3.4445
poly_b = -4.775
poly_c = 2.0315
masked_score = -1e30
bf16 = jnp.bfloat16
f32 = jnp.float32


def dot(left, right, dims=((1,), (0,))):
    return lax.dot_general(left, right, (dims, ((), ())), preferred_element_type=f32)


MESH = pl.DeviceIdType.MESH
HALF = 384
SENDS = 40
RECVS = 151


def place():
    rep = lax.axis_index("rep")
    return rep % 4, rep // 8, (rep // 4) % 2, lax.axis_index("shard")


def device(x, y, z, shard):
    return ((y * 2 + z) * 4 + x, shard)


class GroupSum:
    def __init__(self, sides, across, copy, here, total_rows, parts, out, got_one, got_two, got_z, pass_one, pass_two, mid):
        self.sides, self.across, self.copy, self.here = sides, across, copy, here
        self.parts, self.out, self.got, self.got_z = parts, out, (got_one, got_two), got_z
        self.passing, self.mid, self.ends = (pass_one, pass_two), mid, pass_two
        self.big, self.little = total_rows // 4, total_rows // 16
        self.cuts = (self.big // 2, (self.little // 2 + 15) // 16 * 16)

    @staticmethod
    def rows(start, size):
        return pl.ds(pl.multiple_of(start, 16), size)

    def reduce_start(self, step, ref, axis, k):
        p, left, right, over = self.sides[axis]
        n, cut, got = (self.big, self.little)[step], self.cuts[step], self.got[step].at[k]
        opp, nxt, prv = (p + 2) % 4, (p + 1) % 4, (p + 3) % 4
        rows, copy = self.rows, self.copy
        if step == 1:
            direct = [copy(ref.at[rows(c * n, n), :], got.at[i], target) for i, (c, target) in enumerate(((nxt, right), (prv, left), (opp, over)))]
            return direct, (p, ref, n, got)
        first = (
            copy(ref.at[rows(opp * n, cut), :], got.at[0, 0:cut, :], right),
            copy(ref.at[rows(opp * n + cut, n - cut), :], got.at[0, cut:n, :], left),
            copy(ref.at[rows(nxt * n + cut, n - cut), :], got.at[1, cut:n, :], right),
            copy(ref.at[rows(prv * n, cut), :], got.at[1, 0:cut, :], left),
        )
        return first, (p, left, right, nxt, prv, ref, n, cut, got, self.passing[step].at[k])

    def reduce_pass(self, state):
        first, (p, left, right, nxt, prv, ref, n, cut, got, passing) = state
        rows = self.rows
        first[0].wait_recv()
        passing[0:cut, :] = (ref[rows(nxt * n, cut), :].astype(f32) + got[0, 0:cut, :].astype(f32)).astype(bf16)
        second = [self.copy(passing.at[0:cut, :], got.at[2, 0:cut, :], right)]
        first[1].wait_recv()
        passing[cut:n, :] = (ref[rows(prv * n + cut, n - cut), :].astype(f32) + got[0, cut:n, :].astype(f32)).astype(bf16)
        second.append(self.copy(passing.at[cut:n, :], got.at[2, cut:n, :], left))
        return second

    def reduce_end_direct(self, state, dst):
        copies, (p, ref, n, got) = state
        for c in copies:
            c.wait_recv()
        dst[...] = (ref[self.rows(p * n, n), :].astype(f32) + got[0].astype(f32) + got[1].astype(f32) + got[2].astype(f32)).astype(bf16)
        for c in copies:
            c.wait_send()

    def reduce_end(self, state, second, dst):
        first, (p, left, right, nxt, prv, ref, n, cut, got, passing) = state
        for c in (first[2], first[3], *second):
            c.wait_recv()
        dst[...] = (ref[self.rows(p * n, n), :].astype(f32) + got[1].astype(f32) + got[2].astype(f32)).astype(bf16)
        for c in (*first, *second):
            c.wait_send()

    def gather_start(self, step, ref, axis, base):
        p, left, right, over = self.sides[axis]
        n, cut = (self.big, self.little)[step], self.cuts[step]

        def send(chunk, head, target):
            spot = self.rows(base + chunk * n + (0 if head else cut), cut if head else n - cut)
            return self.copy(ref.at[spot, :], ref.at[spot, :], target)

        if step == 1:
            spot = self.rows(base + p * n, n)
            return [self.copy(ref.at[spot, :], ref.at[spot, :], target) for target in (right, left, over)]
        return (send(p, True, right), send(p, False, left), send(p, False, right), send(p, True, left)), (p, left, right, send)

    def gather_pass(self, state):
        first, (p, left, right, send) = state
        first[0].wait_recv()
        second = [send((p + 3) % 4, True, right)]
        first[1].wait_recv()
        second.append(send((p + 1) % 4, False, left))
        return second

    def gather_end(self, state, second):
        for c in (*state[0][2:], *second):
            c.wait_recv()
        for c in (*state[0], *second):
            c.wait_send()

    def one_start(self):
        self.state = [self.reduce_start(0, self.parts.at[k], "xy"[k], k) for k in range(2)]

    def one_pass(self):
        self.second = [self.reduce_pass(state) for state in self.state]

    def two_start(self):
        for k in range(2):
            self.reduce_end(self.state[k], self.second[k], self.mid.at[k])
        self.state = [self.reduce_start(1, self.mid.at[k], "yx"[k], k) for k in range(2)]

    def z_start(self):
        for k in range(2):
            self.reduce_end_direct(self.state[k], self.ends.at[2 + k])
        self.over = [self.copy(self.ends.at[2 + k], self.got_z.at[k], self.across) for k in range(2)]

    def back_start(self):
        x, y = self.here
        self.state = []
        for k in range(2):
            base = (x, y)[k] * self.big
            at = base + (y, x)[k] * self.little
            self.over[k].wait()
            self.out[k, self.rows(at, self.little), :] = (self.ends[2 + k].astype(f32) + self.got_z[k].astype(f32)).astype(bf16)
            self.state.append(self.gather_start(1, self.out.at[k], "yx"[k], base))

    def last_start(self):
        for c in (*self.state[0], *self.state[1]):
            c.wait()
        self.state = [self.gather_start(0, self.out.at[k], "xy"[k], 0) for k in range(2)]

    def last_pass(self):
        self.second = [self.gather_pass(state) for state in self.state]

    def last_end(self):
        for k in range(2):
            self.gather_end(self.state[k], self.second[k])


def sum_scratch(total_rows):
    big, little = total_rows // 4, total_rows // 16
    return [
        pltpu.VMEM((2, 3, big, HALF), bf16),
        pltpu.VMEM((2, 3, little, HALF), bf16),
        pltpu.VMEM((2, little, HALF), bf16),
        pltpu.VMEM((2, big, HALF), bf16),
        pltpu.VMEM((4, little, HALF), bf16),
        pltpu.VMEM((2, big, HALF), bf16),
    ]


def make_gather(sides, copy):
    def start(axis, ref, base, n, cut, unit):
        p, left, right, over = sides[axis]

        def rows(chunk, first):
            at = base + chunk * n + (0 if first else cut)
            return pl.ds(pl.multiple_of(at, unit), cut if first else n - cut)

        def send(chunk, first, target):
            spot = rows(chunk, first)
            return copy(ref.at[spot, :], ref.at[spot, :], target)

        first = (send(p, True, right), send(p, False, left), send(p, False, right), send(p, True, left))
        return first, (p, left, right, send)

    def start_direct(axis, ref, base, n, unit):
        p, *targets = sides[axis]
        spot = pl.ds(pl.multiple_of(base + p * n, unit), n)
        return [copy(ref.at[spot, :], ref.at[spot, :], target) for target in targets]

    def onward(state):
        first, (p, left, right, send) = state
        first[0].wait_recv()
        second = [send((p + 3) % 4, True, right)]
        first[1].wait_recv()
        second.append(send((p + 1) % 4, False, left))
        return second

    def end(state, second):
        for c in (*state[0][2:], *second):
            c.wait_recv()
        for c in (*state[0], *second):
            c.wait_send()

    def both(refs, orders, base, sizes, unit):
        n, cut = sizes[0]
        direct = [c for k in range(2) for c in start_direct(orders[k][0], refs[k], base[k], n, unit)]
        for c in direct:
            c.wait()
        n, cut = sizes[1]
        states = [start(orders[k][1], refs[k], 0, n, cut, unit) for k in range(2)]
        seconds = [onward(state) for state in states]
        for state, second in zip(states, seconds):
            end(state, second)

    return both


def orth_factors(here, sides, sibling, over_z, over_z_next, copy, at, piece, got, halves, gram, gram_low, poly, factor_low, q_all, small_step):
    x, y, z, shard = here
    gather = make_gather(sides, copy)
    n = D // 16
    sib, par = shard + 1 - 2 * (shard % 2), (shard + 2) % 4
    ps = (sib + 2) % 4
    sums = [copy(piece.at[sib], got.at[0], sibling)]
    for k in range(2):
        sums.append(copy(piece.at[par, k], got.at[1, k], over_z[k]))
        sums.append(copy(piece.at[ps, k], got.at[2, k], over_z_next[k]))
    for c in sums:
        c.wait_recv()
    for k in range(2):
        halves[k, pl.ds(at[k], n), :] = piece[shard, k] + got[0, k] + got[1, k] + got[2, k]
    orders = (("y", "x"), ("x", "y"))
    base = (x * 4 * n, y * 4 * n)
    gather([halves.at[0], halves.at[1]], orders, base, ((n, 24), (4 * n, 2 * n)), 8)
    for c in sums:
        c.wait_send()

    tile = 256
    blocks = D // tile

    def eye(r, width, first):
        return (lax.broadcasted_iota(jnp.int32, (tile, width), 0) + r * tile == lax.broadcasted_iota(jnp.int32, (tile, width), 1) + first).astype(f32)

    trace = jnp.zeros((1, 1), f32)
    for r in range(blocks):
        for k in range(2):
            part = halves[k, r * tile : (r + 1) * tile, :] * eye(r, HALF, k * HALF)
            trace = trace + jnp.sum(jnp.sum(part, axis=1, keepdims=True), axis=0, keepdims=True)
    inv = 1.0 / (jnp.sqrt(trace) + 1e-07)
    for r in range(blocks):
        spot = slice(r * tile, (r + 1) * tile)
        for k in range(2):
            cols = slice(k * HALF, k * HALF + HALF)
            g = halves[k, spot, :] * (inv * inv)
            gram[spot, cols] = g
            gram_low[0][spot, cols] = g.astype(bf16)

    for k in range(4):
        small_step()
        now, later = k % 2, (k + 1) % 2

        def poly_rows(r):
            spot = slice(r * tile, (r + 1) * tile)
            poly[spot, :] = (poly_b * gram[spot, :] + poly_c * dot(gram_low[now][spot, :], gram_low[now][...])).astype(bf16)

        def update_rows(r):
            spot = slice(r * tile, (r + 1) * tile)
            p = poly[spot, :]
            if k == 0:
                q = p.astype(f32) + poly_a * eye(r, D, 0)
            else:
                q = poly_a * jnp.concatenate([halves[0, spot, :], halves[1, spot, :]], 1) + dot(p, factor_low[now][...])
            halves[0, spot, :] = q[:, :HALF]
            halves[1, spot, :] = q[:, HALF:]
            if k < 3:
                factor_low[later][spot, :] = q.astype(bf16)
                t = poly_a * gram[spot, :] + dot(p, gram_low[now][...])
                g = poly_a * t + dot(t.astype(bf16), poly[...])
                gram[spot, :] = g
                gram_low[later][spot, :] = g.astype(bf16)

        for r in range(blocks):
            poly_rows(r)
        for r in range(blocks):
            update_rows(r)
    small_step()
    q_all[shard, 0] = (halves[0, 0:HALF, :] * inv).astype(bf16)
    q_all[shard, 1] = (halves[1, 0:HALF, :] * inv).astype(bf16)
    q_all[shard, 2] = (halves[1, HALF:D, :] * inv).astype(bf16)
    top, low_part = pl.ds(0, HALF // 2), pl.ds(HALF // 2, HALF // 2)
    cross = []
    for k in range(2):
        for block, spot in ((1, (top, low_part)[k]), (2 * k, pl.ds(0, HALF))):
            view = q_all.at[shard, block, spot, :]
            cross.append((copy(view, view, over_z[k]), block, spot))
    near = copy(q_all.at[shard], q_all.at[shard], sibling)
    away = (shard + 2) % 4
    onward = []
    for c, block, spot in (cross[0], cross[2], cross[1], cross[3]):
        c.wait_recv()
        view = q_all.at[away, block, spot, :]
        onward.append(copy(view, view, sibling))
    near.wait_recv()
    for c in onward:
        c.wait_recv()
    for c in (*[c for c, block, spot in cross], near, *onward):
        c.wait_send()


def block_kernel(
    x_ref, cot_ref, length_ref, order_ref, wq_hbm, wo_hbm, wf_hbm, wp_hbm, mq_hbm, mo_hbm, mf_hbm, mp_hbm, small_ref,
    out_ref, dx_ref, sums_one, sums_two, small_out, q_all, u_fc, momq, wo32, wf32, wp32, wf_held, wp_held,
    tokens, mixed, probs, bias, head_out, terms, got, passing, wq, wo, wf, wp,
    gact, act, gpre, gheads, gmixed, xhat1, xhat2, resid, gres, parts_one, parts_two, *rest,
):
    one_refs, two_refs = rest[:6], rest[6:12]
    small, qkv_bias, row_place, uq, piece, gram_got, halves, gram, poly = rest[12:21]
    small_got, send, recv, local = rest[21:]
    group = 4 * BLOCK
    nrm, mlow, nrm2, branch = (tokens.at[pl.ds(k * group, group), :] for k in range(4))
    part = [terms.at[pl.ds(k * group, group), :] for k in range(4)]
    gram_low, factor_low = ([ref.at[pl.ds(k * D, D), :] for k in range(2)] for ref in (tokens, terms))
    x, y, z, shard = place()
    sib = shard + 1 - 2 * (shard % 2)
    par = (shard + 2) % 4
    sibling, partner = device(x, y, z, sib), device(x, y, z, par)
    sides = {
        "x": (x, *[device((x + d) % 4, y, z, shard) for d in (3, 1, 2)]),
        "y": (y, *[device(x, (y + d) % 4, z, shard) for d in (3, 1, 2)]),
    }
    across = device(x, y, 1 - z, shard)
    far_sib = (sib + 2) % 4
    partners = (sibling, partner, device(x, y, z, far_sib), device(x, y, 1 - z, par), device(x, y, 1 - z, far_sib), *sides["x"][1:], *sides["y"][1:], across)
    barrier = pltpu.get_barrier_semaphore()
    for other in partners:
        pl.semaphore_signal(barrier, inc=1, device_id=other, device_id_type=MESH)
    loads = [pltpu.make_async_copy(src, dst, local.at[k]) for k, (src, dst) in enumerate(((wq_hbm, momq), (wo_hbm, wo32), (wf_hbm, wf32), (wp_hbm, wp32)))]
    for load in loads:
        load.start()

    rows = BLOCK

    def chunk(index, size=rows, at=0):
        return pl.ds(pl.multiple_of(index * rows + at, 16), size)

    own, own_sib, own_par, own_ps = chunk(shard), chunk(sib), chunk(par), chunk((sib + 2) % 4)
    near = pl.multiple_of((shard // 2) * 256, 256)
    far = pl.multiple_of(256 - near, 256)
    used = [0]

    free = list(range(SENDS))

    class Copy:
        def __init__(self, src, dst, target):
            self.slot = free.pop(0)
            self.copy = pltpu.make_async_remote_copy(
                src_ref=src, dst_ref=dst, send_sem=send.at[self.slot], recv_sem=recv.at[used[0]], device_id=target, device_id_type=MESH
            )
            used[0] += 1
            self.copy.start()

        def wait_recv(self):
            self.copy.wait_recv()

        def wait_send(self):
            self.copy.wait_send()
            free.append(self.slot)

        def wait(self):
            self.wait_recv()
            self.wait_send()

    copy = Copy
    sum_one = GroupSum(sides, across, copy, (x, y), 2 * D, parts_one, sums_one, *one_refs)
    sum_two = GroupSum(sides, across, copy, (x, y), D, parts_two, sums_two, *two_refs)
    steps = [
        sibling,
        partner,
        across,
        device(x + 1 - 2 * (x % 2), y, z, shard),
        device(3 - x, y, z, shard),
        device(x, y + 1 - 2 * (y % 2), z, shard),
        device(x, 3 - y, z, shard),
    ]
    small_copies = []

    def small_step():
        k = len(small_copies)
        if k > 0:
            small_copies[-1].wait()
            small_out[...] += small_got[k - 1]
        if k < len(steps):
            small_copies.append(copy(small_out, small_got.at[k], steps[k]))

    one_way, both_ways = (partner, partner), (partner, device(x, y, 1 - z, par))

    class Spread:
        def __init__(self, ref, ways):
            self.ref = ref
            self.cross = [self.to(shard, 64 * i, ways[i]) for i in range(2)]
            self.direct = copy(ref.at[own, :], ref.at[own, :], sibling)

        def to(self, index, at, target):
            spot = chunk(index, 64, at)
            return copy(self.ref.at[spot, :], self.ref.at[spot, :], target)

        def near(self):
            self.direct.wait_recv()

        def far(self):
            onward = []
            for i in range(2):
                self.cross[i].wait_recv()
                onward.append(self.to(par, 64 * i, sibling))
            for c in onward:
                c.wait_recv()
            for c in (*self.cross, self.direct, *onward):
                c.wait_send()

    class Fold:
        def __init__(self, k, ways):
            self.k, self.ways = k, ways

        def start_far(self):
            self.a = copy(part[self.k].at[own_ps, :], got.at[self.k, 0], sibling)

        def start_near(self):
            self.b = copy(part[self.k].at[own_sib, :], got.at[self.k, 1], sibling)

        def cross(self):
            self.a.wait_recv()
            passing[self.k] = (part[self.k][own_par, :].astype(f32) + got[self.k, 0].astype(f32)).astype(bf16)
            halves = (pl.ds(0, 64), pl.ds(64, 64))
            self.c = [copy(passing.at[self.k, spot, :], got.at[self.k, 2, spot, :], way) for spot, way in zip(halves, self.ways)]

        def end(self):
            self.b.wait_recv()
            for c in self.c:
                c.wait_recv()
            for c in (self.a, self.b, *self.c):
                c.wait_send()
            return part[self.k][own, :].astype(f32) + got[self.k, 1].astype(f32) + got[self.k, 2].astype(f32)

    def norm(v):
        centred = v - jnp.mean(v, axis=-1, keepdims=True)
        r = lax.rsqrt(jnp.mean(centred * centred, axis=-1, keepdims=True) + norm_eps)
        return centred * r, r

    def norm_grad(xhat, r, gain, c):
        cg = c * gain
        return r * (cg - jnp.mean(cg, -1, keepdims=True) - xhat * jnp.mean(cg * xhat, -1, keepdims=True))

    def total(v):
        return jnp.sum(v, axis=0, keepdims=True)

    nt, tn = ((1,), (1,)), ((0,), (0,))
    hc = wq.shape[0] // 3
    heads = hc // HD
    scale = HD ** -0.5

    small[...] = small_ref[...].astype(bf16).astype(f32)
    length = length_ref[0]

    def places(slot, axis):
        return lax.broadcasted_iota(jnp.int32, (rows, 1) if axis == 0 else (1, rows), axis) + order_ref[0, slot] * rows

    live = (places(shard, 0) < length).astype(f32)
    xf = x_ref[...].astype(f32)
    hat, r_one = norm(xf)
    xhat1[...] = hat
    nrm[own, :] = (hat * small[0:1, :] + small[1:2, :]).astype(bf16)
    mlow[own, :] = (cot_ref[...] * live).astype(bf16)
    pl.semaphore_wait(barrier, len(partners))
    go_nrm = Spread(nrm, one_way)
    go_mlow = Spread(mlow, both_ways)
    for slot in range(4):
        row_place[:, slot * rows : (slot + 1) * rows] = places(slot, 1)
    row = row_place[...]
    for slot in range(4):
        bias[slot * rows : (slot + 1) * rows, :] = jnp.where((row <= places(slot, 0)) & (row < length), 0.0, masked_score)
    for part_of, line in ((0, 4), (2, 5)):
        mine = jnp.zeros((1, hc), f32)
        for s in range(4):
            mine = jnp.where(shard == s, small[line : line + 1, s * hc : (s + 1) * hc], mine)
        qkv_bias[:, part_of * hc : (part_of + 1) * hc] = mine
    qkv_bias[:, hc : 2 * hc] = jnp.zeros((1, hc), f32)
    fc_bias = small[pl.ds(7 + shard, 1), :]
    loads[0].wait()
    wq[...] = momq[...].astype(bf16)
    loads[1].wait()
    wo[...] = wo32[...].astype(bf16)

    def mix(at):
        spot = pl.ds(at, 256)
        mixed[spot, :] = (dot(nrm[spot, :], wq[...], nt) + qkv_bias[...]).astype(bf16)

    go_nrm.near()
    mix(near)
    go_nrm.far()
    mix(far)

    def head(h, part_of):
        lo = part_of * hc + h * HD
        return slice(lo, lo + HD)

    for h in range(heads):

        def attend(i):
            spot = slice(i * 256, i * 256 + 256)
            s = dot(mixed[spot, head(h, 0)], mixed[:, head(h, 1)], nt) * scale + bias[spot, :]
            e = jnp.exp(s - jnp.max(s, axis=-1, keepdims=True))
            p = (e * (1.0 / jnp.sum(e, axis=-1, keepdims=True))).astype(bf16)
            probs[h, spot, :] = p
            head_out[spot, head(h, 0)] = dot(p, mixed[:, head(h, 2)]).astype(bf16)

        for i in range(2):
            attend(i)

    fold = Fold(0, one_way)
    part[0][pl.ds(far, 256), :] = dot(head_out[pl.ds(far, 256), :], wo[...]).astype(bf16)
    fold.start_far()
    part[0][pl.ds(near, 256), :] = dot(head_out[pl.ds(near, 256), :], wo[...]).astype(bf16)
    fold.start_near()
    fold.cross()
    go_mlow.near()
    go_mlow.far()
    loads[2].wait()
    wf[...] = wf32[...].astype(bf16)
    loads[3].wait()
    wp[...] = wp32[...].astype(bf16)

    mom_loads = [pltpu.make_async_copy(src, dst, local.at[4 + k]) for k, (src, dst) in enumerate(((mo_hbm, wo32), (mf_hbm, wf32), (mp_hbm, wp32), (mq_hbm, momq), (wf_hbm, wf_held), (wp_hbm, wp_held)))]
    for load in mom_loads:
        load.start()

    def activation_grad(i):
        spot = slice(i * 256, i * 256 + 256)
        gact[spot, :] = dot(mlow[spot, :], wp[...], nt)

    for i in range(2):
        activation_grad(i)
    res = x_ref[...].astype(f32) + fold.end() + small[6:7, :]
    resid[...] = res
    hat, r_two = norm(res)
    xhat2[...] = hat
    nrm2[own, :] = (hat * small[2:3, :] + small[3:4, :]).astype(bf16)
    go_nrm2 = Spread(nrm2, both_ways)

    def feed(at):
        spot = pl.ds(at, 256)
        hidden = dot(nrm2[spot, :], wf[...]) + fc_bias
        k = 0.7978845608028654
        square = hidden * hidden
        t = jnp.tanh(k * (hidden + 0.044715 * hidden * square))
        half = 0.5 * (1.0 + t)
        act[spot, :] = (hidden * half).astype(bf16)
        slope = half + 0.5 * hidden * (1.0 - t * t) * (k + (3 * 0.044715 * k) * square)
        gpre[spot, :] = (slope * gact[spot, :]).astype(bf16)

    go_nrm2.near()
    feed(near)
    go_nrm2.far()
    feed(far)
    fold = Fold(1, both_ways)
    part[1][pl.ds(far, 256), :] = dot(gpre[pl.ds(far, 256), :], wf[...], nt).astype(bf16)
    fold.start_far()
    part[1][pl.ds(near, 256), :] = dot(gpre[pl.ds(near, 256), :], wf[...], nt).astype(bf16)
    fold.start_near()
    fold.cross()

    def grad_columns(parts, base, left, right, width):
        for c in range(left.shape[1] // width):
            value = dot(left[:, c * width : (c + 1) * width], right[...], tn).astype(bf16)
            spot = pl.ds(base + c * width, width)
            parts[0, spot, :] = value[:, :HALF]
            parts[1, spot, :] = value[:, HALF:]

    grad_columns(parts_one, 0, nrm2, gpre, 256)
    grad_columns(parts_one, D, act, mlow, 256)
    sum_one.one_start()
    small_out[11:12, :] = total(mlow[own, :].astype(f32))
    c_two = fold.end()
    hat = xhat2[...]
    small_out[2:3, :] = total(c_two * hat)
    small_out[3:4, :] = total(c_two)
    g = cot_ref[...] * live + norm_grad(hat, r_two, small[2:3, :], c_two)
    gres[...] = g
    branch[own, :] = g.astype(bf16)
    go_branch = Spread(branch, one_way)
    sum_one.one_pass()
    small_out[6:7, :] = total(branch[own, :].astype(f32))
    pre_sum = total(gpre[...].astype(f32))
    small_out[7:11, :] = jnp.where(lax.broadcasted_iota(jnp.int32, (4, D), 0) == shard, pre_sum, 0.0)

    def head_grads(at):
        spot = pl.ds(at, 256)
        gheads[spot, :] = dot(branch[spot, :], wo[...], nt).astype(bf16)

    fold_out = Fold(2, both_ways)
    part[2][pl.ds(far, 256), :] = dot(act[pl.ds(far, 256), :], wp[...]).astype(bf16)
    fold_out.start_far()
    part[2][pl.ds(near, 256), :] = dot(act[pl.ds(near, 256), :], wp[...]).astype(bf16)
    fold_out.start_near()
    go_branch.near()
    head_grads(near)
    go_branch.far()
    head_grads(far)
    fold_out.cross()
    sum_one.two_start()
    for h in range(heads):
        q, k, v = (mixed[:, head(h, i)] for i in range(3))
        gh = gheads[:, head(h, 0)]
        gmixed[:, head(h, 2)] = dot(gh, probs[h], tn).T.astype(bf16)

        def scores_grad(i):
            spot = slice(i * 256, i * 256 + 256)
            p = probs[h, spot, :].astype(f32)
            gp = dot(gheads[spot, head(h, 0)], mixed[:, head(h, 2)], nt)
            gs = (p * (gp - jnp.sum(p * gp, axis=-1, keepdims=True))).astype(bf16)
            probs[h, spot, :] = gs
            gmixed[spot, head(h, 0)] = (dot(gs, mixed[:, head(h, 1)]) * scale).astype(bf16)

        for i in range(2):
            scores_grad(i)
        gmixed[:, head(h, 1)] = (dot(q, probs[h], tn).T * scale).astype(bf16)

    grad_columns(parts_two, 0, head_out, branch, hc)
    grad_columns(parts_two, hc, gmixed, nrm, hc)
    sum_two.one_start()
    sum_one.z_start()
    fold = Fold(3, one_way)
    part[3][pl.ds(far, 256), :] = dot(gmixed[pl.ds(far, 256), :], wq[...]).astype(bf16)
    fold.start_far()
    part[3][pl.ds(near, 256), :] = dot(gmixed[pl.ds(near, 256), :], wq[...]).astype(bf16)
    fold.start_near()
    fold.cross()
    mixed_sum = total(gmixed[...].astype(f32))
    spread_out = (lax.broadcasted_iota(jnp.int32, (hc, D), 0) + shard * hc == lax.broadcasted_iota(jnp.int32, (hc, D), 1)).astype(f32)
    for row, lo in ((4, 0), (5, 2 * hc)):
        small_out[row : row + 1, :] = jnp.dot(mixed_sum[:, lo : lo + hc], spread_out, precision=lax.Precision.HIGHEST, preferred_element_type=f32)
    out_ref[...] = ((resid[...] + fold_out.end() + small[11:12, :]) * live).astype(bf16)
    sum_two.one_pass()
    sum_one.back_start()
    sum_two.two_start()
    c_one = fold.end()
    hat = xhat1[...]
    small_out[0:1, :] = total(c_one * hat)
    small_out[1:2, :] = total(c_one)
    small_step()
    dx_ref[...] = gres[...] + norm_grad(hat, r_one, small[0:1, :], c_one)
    sum_one.last_start()
    small_step()
    sum_two.z_start()
    sum_one.last_pass()
    sum_two.back_start()
    small_step()

    def update(u, base, mom, sums):
        count = u.shape[0]
        for k in range(2):
            cols = slice(k * HALF, k * HALF + HALF)
            g = sums[k, base : base + count, :].astype(f32)
            u[:, cols] = (g + momentum_decay * (momentum_decay * mom[:, cols] + g)).astype(bf16)

    n = D // 16
    at = (pl.multiple_of((x * 4 + y) * n, 16), pl.multiple_of((y * 4 + x) * n, 16))

    def gram_rows(m, u, whole):
        for k in range(2):
            cols = slice(k * HALF, k * HALF + HALF)
            if whole:
                piece[m, k] = dot(u[pl.ds(at[k], n), :], u[cols, :], nt)
            else:
                pick = (lax.broadcasted_iota(jnp.int32, (D, n), 0) == lax.broadcasted_iota(jnp.int32, (D, n), 1) + at[k]).astype(f32).astype(bf16)
                piece[m, k] = dot(dot(u[...], pick).astype(bf16), u[:, cols], tn)

    sum_two.last_start()
    sum_one.last_end()
    for load in mom_loads:
        load.wait()
    update(u_fc, 0, wf32, sums_one)
    update(wp, D, wp32, sums_one)
    gram_rows(2, u_fc, True)
    gram_rows(3, wp, False)
    sum_two.last_pass()
    sum_two.last_end()
    update(wo, 0, wo32, sums_two)
    update(uq, hc, momq, sums_two)
    gram_rows(1, wo, False)
    gram_rows(0, uq, False)
    over_z = [partner, device(x, y, 1 - z, par)]
    over_z_next = [device(x, y, z, (sib + 2) % 4), device(x, y, 1 - z, (sib + 2) % 4)]
    orth_factors(place(), sides, sibling, over_z, over_z_next, copy, at, piece, gram_got, halves, gram, gram_low, poly, factor_low, q_all, small_step)
    assert used[0] <= RECVS and len(free) == SENDS


def run_block(x_own, cot, lengths, order, wq, wo, wf, wp, mq, mo, mf, mp, small):
    vm = pl.BlockSpec(memory_space=pltpu.VMEM)
    sm = pl.BlockSpec(memory_space=pltpu.SMEM)
    hbm = pl.BlockSpec(memory_space=pl.ANY)
    rows, wide = x_own.shape[0], wq.shape[0]
    hc = wide // 3
    group = 4 * rows
    vmem = pltpu.VMEM
    return pl.pallas_call(
        block_kernel,
        out_shape=(
            pltpu.VMEM((rows, D), bf16),
            pltpu.VMEM((rows, D), f32),
            pltpu.VMEM((2, 2 * D, HALF), bf16),
            pltpu.VMEM((2, D, HALF), bf16),
            pltpu.VMEM((12, D), f32),
            pltpu.VMEM((4, 3, HALF, HALF), bf16),
            pltpu.VMEM((D, D), bf16),
            *[pltpu.VMEM(w.shape, f32) for w in (wq, wo, wf, wp, wf, wp)],
        ),
        in_specs=[vm, vm, sm, sm] + [hbm] * 8 + [vm],
        out_specs=(vm,) * 13,
        scratch_shapes=[
            vmem((4 * group, D), bf16),
            vmem((group, wide), bf16),
            vmem((hc // HD, group, group), bf16),
            vmem((group, group), f32),
            vmem((group, hc), bf16),
            vmem((4 * group, D), bf16),
            vmem((4, 3, rows, D), bf16),
            vmem((4, rows, D), bf16),
            vmem(wq.shape, bf16),
            vmem(wo.shape, bf16),
            vmem(wf.shape, bf16),
            vmem(wp.shape, bf16),
            vmem((group, D), f32),
            vmem((group, D), bf16),
            vmem((group, D), bf16),
            vmem((group, hc), bf16),
            vmem((group, wide), bf16),
            vmem((rows, D), f32),
            vmem((rows, D), f32),
            vmem((rows, D), f32),
            vmem((rows, D), f32),
            vmem((2, 2 * D, HALF), bf16),
            vmem((2, D, HALF), bf16),
            *sum_scratch(2 * D),
            *sum_scratch(D),
            vmem((12, D), f32),
            vmem((1, wide), f32),
            vmem((1, group), jnp.int32),
            vmem((wide, D), bf16),
            vmem((4, 2, D // 16, HALF), f32),
            vmem((3, 2, D // 16, HALF), f32),
            vmem((2, D, HALF), f32),
            vmem((D, D), f32),
            vmem((D, D), bf16),
            vmem((7, 12, D), f32),
            pltpu.SemaphoreType.DMA((SENDS,)),
            pltpu.SemaphoreType.DMA((RECVS,)),
            pltpu.SemaphoreType.DMA((10,)),
        ],
        compiler_params=pltpu.CompilerParams(collective_id=1, has_side_effects=True, vmem_limit_bytes=40 * 1024 * 1024),
    )(x_own, cot, lengths, order, wq, wo, wf, wp, mq, mo, mf, mp, small)


def finish_kernel(
    sums_one, sums_two, q_all, u_fc, mq, mo, mf, mp, wf, wp, out_in, dx_in, small_sum, small_params, small_first, small_second,
    wq, wo,
    out_ref, dx_ref, gq, go, gf, gp, nq, no, nf, np_, rq, ro, rf, rp, small_grad, first_ref, second_ref, small_new, last_bias,
):
    i = pl.program_id(0)
    nt, tn = ((1,), (1,)), ((0,), (0,))

    @pl.when(i == 0)
    def _():
        out_ref[...] = out_in[...]
        dx_ref[...] = dx_in[...]
        g = small_sum[...]
        small_grad[...] = g
        last_bias[...] = g[11:12, :]
        first = beta_one * small_first[...] + (1.0 - beta_one) * g
        second = beta_two * small_second[...] + (1.0 - beta_two) * g * g
        first_ref[...] = first
        second_ref[...] = second
        first_hat = first / (1.0 - beta_one**STEP)
        second_hat = second / (1.0 - beta_two**STEP)
        small_new[...] = small_params[...] - adam_rate * first_hat / (jnp.sqrt(second_hat) + adam_eps)

    def renew(owner, sums, base, w, m, g_out, w_out, m_out, longest, rate):
        count = g_out.shape[0]
        keep_rate, step_rate = 1.0 - rate * muon_decay, rate * 0.2 * math.sqrt(longest)
        spot = pl.ds(pl.multiple_of(base + i * count, 16), count)
        mine = pl.ds(pl.multiple_of(i * count, 16), count)
        held = mine if w.shape[0] > count else pl.ds(0, count)
        low = []
        for k in range(2):
            cols = slice(k * HALF, k * HALF + HALF)
            g = sums[k, spot, :].astype(f32)
            moved = momentum_decay * m[mine, cols] + g
            g_out[:, cols] = g
            m_out[:, cols] = moved
            low.append((g + momentum_decay * moved).astype(bf16))
        q11, q12, q22 = q_all[owner, 0], q_all[owner, 1], q_all[owner, 2]
        w_out[:, :HALF] = keep_rate * w[held, :HALF] - step_rate * (dot(low[0], q11) + dot(low[1], q12, nt))
        w_out[:, HALF:] = keep_rate * w[held, HALF:] - step_rate * (dot(low[0], q12) + dot(low[1], q22))

    renew(0, sums_two, 192, wq, mq, gq, nq, rq, 3 * D, muon_rate)
    renew(1, sums_two, 0, wo, mo, go, no, ro, D, out_rate)
    renew(3, sums_one, D, wp, mp, gp, np_, rp, FF, muon_rate)
    count = gf.shape[0]
    keep_rate, step_rate = 1.0 - muon_rate * muon_decay, muon_rate * 0.2 * math.sqrt(FF)
    spot = pl.ds(pl.multiple_of(i * count, 16), count)
    for k in range(2):
        cols = slice(k * HALF, k * HALF + HALF)
        g = sums_one[k, spot, :].astype(f32)
        gf[:, cols] = g
        rf[:, cols] = momentum_decay * mf[spot, cols] + g
    half_steps = HALF // count

    @pl.when(i < half_steps)
    def _():
        at = pl.ds(pl.multiple_of(i * count, count), count)
        nf[...] = keep_rate * wf[spot, :] - step_rate * (dot(q_all[2, 0, at, :], u_fc[:HALF, :]) + dot(q_all[2, 1, at, :], u_fc[HALF:, :]))

    @pl.when(i >= half_steps)
    def _():
        at = pl.ds(pl.multiple_of((i - half_steps) * count, count), count)
        nf[...] = keep_rate * wf[spot, :] - step_rate * (dot(q_all[2, 1, :, at], u_fc[:HALF, :], tn) + dot(q_all[2, 2, at, :], u_fc[HALF:, :]))


def finish(kept, small, weights):
    steps = 6
    vm = pl.BlockSpec(memory_space=pltpu.VMEM)

    def tiles(a):
        return pl.BlockSpec((a.shape[0] // steps, a.shape[1]), lambda i: (i, 0))

    def whole(shape):
        return pl.BlockSpec(shape, lambda i: (0, 0))

    like = [jax.ShapeDtypeStruct(w.shape, f32) for w in weights]
    flat = jax.ShapeDtypeStruct((12, D), f32)
    last = jax.ShapeDtypeStruct((1, D), f32)
    block_out, dx = kept[10], kept[11]
    own = [jax.ShapeDtypeStruct(block_out.shape, bf16), jax.ShapeDtypeStruct(dx.shape, f32)]
    return pl.pallas_call(
        finish_kernel,
        grid=(steps,),
        out_shape=(*own, *like, *like, *like, flat, flat, flat, flat, last),
        in_specs=[vm] * 16 + [tiles(w) for w in weights[:2]],
        out_specs=(whole(block_out.shape), whole(dx.shape), *([tiles(w) for w in weights] * 3), *([whole((12, D))] * 4), whole((1, D))),
        compiler_params=pltpu.CompilerParams(vmem_limit_bytes=24 * 1024 * 1024),
    )(*kept, *small, *weights[:2])


def shards(block_input, cotangent, lengths, block_order, w_qkv, w_out, w_fc, w_proj, mom_qkv, mom_out, mom_fc, mom_proj, small_params, small_first, small_second):
    cube = w_qkv.shape

    def turned(a):
        return a.transpose(1, 2, 0).reshape(-1, D)

    def back(a):
        return a.reshape(cube[1], cube[2], D).transpose(2, 0, 1)

    weights = (turned(w_qkv), w_out, w_fc, w_proj)
    moms = (turned(mom_qkv), mom_out, mom_fc, mom_proj)
    block_output, input_grad, sums_one, sums_two, small_sum, factors, u_fc, *held = run_block(block_input, cotangent, lengths, block_order, *weights, *moms, small_params)
    kept = [sums_one, sums_two, factors, u_fc, *held, block_output, input_grad, small_sum]
    kept = [pltpu.with_memory_space_constraint(a, pltpu.VMEM) for a in kept]
    weights = [pltpu.with_memory_space_constraint(a, pltpu.HBM) for a in weights]
    block_output, input_grad, gq, go, gf, gp, nq, no, nf, np_, rq, ro, rf, rp, grad_small, first, second, new_small, last = finish(
        kept, (small_params, small_first, small_second), weights
    )
    return (
        block_output, input_grad, back(gq), go, gf, gp, grad_small, back(nq), no, nf, np_, back(rq), ro, rf, rp, first, second, new_small, last.reshape(D),
    )


def solution(mesh):
    rows = P(("rep", "shard"), None)
    mats = (P(None, None, "shard"), P("shard", None), P(None, "shard"), P("shard", None))
    in_specs = (rows, rows, P("rep"), P("rep", None), *mats, *mats, P(), P(), P())
    out_specs = (rows, rows, *mats, P(), *mats, *mats, P(), P(), P(), P())
    return jax.shard_map(shards, mesh=mesh, in_specs=in_specs, out_specs=out_specs, check_vma=False)
```

```python
import math

import jax
import jax.numpy as jnp
from jax import lax
from jax.experimental import pallas as pl
from jax.experimental.pallas import tpu as pltpu
from jax.sharding import PartitionSpec as P

D = 768
HD = 64
FF = 3072
BLOCK = 128
STEP = 10
momentum_decay = 0.95
muon_rate = 0.15
out_rate = 0.75
muon_decay = 0.01
adam_rate = 0.4
beta_one = 0.9
beta_two = 0.999
adam_eps = 1e-08
norm_eps = 1e-05
poly_a = 3.4445
poly_b = -4.775
poly_c = 2.0315
masked_score = -1e30
bf16 = jnp.bfloat16
f32 = jnp.float32


def dot(left, right, dims=((1,), (0,))):
    return lax.dot_general(left, right, (dims, ((), ())), preferred_element_type=f32)


MESH = pl.DeviceIdType.MESH
HALF = 384
SENDS = 40
RECVS = 151


def place():
    rep = lax.axis_index("rep")
    return rep % 4, rep // 8, (rep // 4) % 2, lax.axis_index("shard")


def device(x, y, z, shard):
    return ((y * 2 + z) * 4 + x, shard)


class GroupSum:
    def __init__(self, sides, across, copy, here, total_rows, parts, out, got_one, got_two, got_z, pass_one, pass_two, mid):
        self.sides, self.across, self.copy, self.here = sides, across, copy, here
        self.parts, self.out, self.got, self.got_z = parts, out, (got_one, got_two), got_z
        self.passing, self.mid, self.ends = (pass_one, pass_two), mid, pass_two
        self.big, self.little = total_rows // 4, total_rows // 16
        self.cuts = (self.big // 2, (self.little // 2 + 15) // 16 * 16)

    @staticmethod
    def rows(start, size):
        return pl.ds(pl.multiple_of(start, 16), size)

    def reduce_start(self, step, ref, axis, k):
        p, left, right, over = self.sides[axis]
        n, cut, got = (self.big, self.little)[step], self.cuts[step], self.got[step].at[k]
        opp, nxt, prv = (p + 2) % 4, (p + 1) % 4, (p + 3) % 4
        rows, copy = self.rows, self.copy
        if step == 1:
            direct = [copy(ref.at[rows(c * n, n), :], got.at[i], target) for i, (c, target) in enumerate(((nxt, right), (prv, left), (opp, over)))]
            return direct, (p, ref, n, got)
        first = (
            copy(ref.at[rows(opp * n, cut), :], got.at[0, 0:cut, :], right),
            copy(ref.at[rows(opp * n + cut, n - cut), :], got.at[0, cut:n, :], left),
            copy(ref.at[rows(nxt * n + cut, n - cut), :], got.at[1, cut:n, :], right),
            copy(ref.at[rows(prv * n, cut), :], got.at[1, 0:cut, :], left),
        )
        return first, (p, left, right, nxt, prv, ref, n, cut, got, self.passing[step].at[k])

    def reduce_pass(self, state):
        first, (p, left, right, nxt, prv, ref, n, cut, got, passing) = state
        rows = self.rows
        first[0].wait_recv()
        passing[0:cut, :] = (ref[rows(nxt * n, cut), :].astype(f32) + got[0, 0:cut, :].astype(f32)).astype(bf16)
        second = [self.copy(passing.at[0:cut, :], got.at[2, 0:cut, :], right)]
        first[1].wait_recv()
        passing[cut:n, :] = (ref[rows(prv * n + cut, n - cut), :].astype(f32) + got[0, cut:n, :].astype(f32)).astype(bf16)
        second.append(self.copy(passing.at[cut:n, :], got.at[2, cut:n, :], left))
        return second

    def reduce_end_direct(self, state, dst):
        copies, (p, ref, n, got) = state
        for c in copies:
            c.wait_recv()
        dst[...] = (ref[self.rows(p * n, n), :].astype(f32) + got[0].astype(f32) + got[1].astype(f32) + got[2].astype(f32)).astype(bf16)
        for c in copies:
            c.wait_send()

    def reduce_end(self, state, second, dst):
        first, (p, left, right, nxt, prv, ref, n, cut, got, passing) = state
        for c in (first[2], first[3], *second):
            c.wait_recv()
        dst[...] = (ref[self.rows(p * n, n), :].astype(f32) + got[1].astype(f32) + got[2].astype(f32)).astype(bf16)
        for c in (*first, *second):
            c.wait_send()

    def gather_start(self, step, ref, axis, base):
        p, left, right, over = self.sides[axis]
        n, cut = (self.big, self.little)[step], self.cuts[step]

        def send(chunk, head, target):
            spot = self.rows(base + chunk * n + (0 if head else cut), cut if head else n - cut)
            return self.copy(ref.at[spot, :], ref.at[spot, :], target)

        if step == 1:
            spot = self.rows(base + p * n, n)
            return [self.copy(ref.at[spot, :], ref.at[spot, :], target) for target in (right, left, over)]
        return (send(p, True, right), send(p, False, left), send(p, False, right), send(p, True, left)), (p, left, right, send)

    def gather_pass(self, state):
        first, (p, left, right, send) = state
        first[0].wait_recv()
        second = [send((p + 3) % 4, True, right)]
        first[1].wait_recv()
        second.append(send((p + 1) % 4, False, left))
        return second

    def gather_end(self, state, second):
        for c in (*state[0][2:], *second):
            c.wait_recv()
        for c in (*state[0], *second):
            c.wait_send()

    def one_start(self):
        self.state = [self.reduce_start(0, self.parts.at[k], "xy"[k], k) for k in range(2)]

    def one_pass(self):
        self.second = [self.reduce_pass(state) for state in self.state]

    def two_start(self):
        for k in range(2):
            self.reduce_end(self.state[k], self.second[k], self.mid.at[k])
        self.state = [self.reduce_start(1, self.mid.at[k], "yx"[k], k) for k in range(2)]

    def z_start(self):
        for k in range(2):
            self.reduce_end_direct(self.state[k], self.ends.at[2 + k])
        self.over = [self.copy(self.ends.at[2 + k], self.got_z.at[k], self.across) for k in range(2)]

    def back_start(self):
        x, y = self.here
        self.state = []
        for k in range(2):
            base = (x, y)[k] * self.big
            at = base + (y, x)[k] * self.little
            self.over[k].wait()
            self.out[k, self.rows(at, self.little), :] = (self.ends[2 + k].astype(f32) + self.got_z[k].astype(f32)).astype(bf16)
            self.state.append(self.gather_start(1, self.out.at[k], "yx"[k], base))

    def last_start(self):
        for c in (*self.state[0], *self.state[1]):
            c.wait()
        self.state = [self.gather_start(0, self.out.at[k], "xy"[k], 0) for k in range(2)]

    def last_pass(self):
        self.second = [self.gather_pass(state) for state in self.state]

    def last_end(self):
        for k in range(2):
            self.gather_end(self.state[k], self.second[k])


def sum_scratch(total_rows):
    big, little = total_rows // 4, total_rows // 16
    return [
        pltpu.VMEM((2, 3, big, HALF), bf16),
        pltpu.VMEM((2, 3, little, HALF), bf16),
        pltpu.VMEM((2, little, HALF), bf16),
        pltpu.VMEM((2, big, HALF), bf16),
        pltpu.VMEM((4, little, HALF), bf16),
        pltpu.VMEM((2, big, HALF), bf16),
    ]


def make_gather(sides, copy):
    def start(axis, ref, base, n, cut, unit):
        p, left, right, over = sides[axis]

        def rows(chunk, first):
            at = base + chunk * n + (0 if first else cut)
            return pl.ds(pl.multiple_of(at, unit), cut if first else n - cut)

        def send(chunk, first, target):
            spot = rows(chunk, first)
            return copy(ref.at[spot, :], ref.at[spot, :], target)

        first = (send(p, True, right), send(p, False, left), send(p, False, right), send(p, True, left))
        return first, (p, left, right, send)

    def start_direct(axis, ref, base, n, unit):
        p, *targets = sides[axis]
        spot = pl.ds(pl.multiple_of(base + p * n, unit), n)
        return [copy(ref.at[spot, :], ref.at[spot, :], target) for target in targets]

    def onward(state):
        first, (p, left, right, send) = state
        first[0].wait_recv()
        second = [send((p + 3) % 4, True, right)]
        first[1].wait_recv()
        second.append(send((p + 1) % 4, False, left))
        return second

    def end(state, second):
        for c in (*state[0][2:], *second):
            c.wait_recv()
        for c in (*state[0], *second):
            c.wait_send()

    def both(refs, orders, base, sizes, unit):
        n, cut = sizes[0]
        direct = [c for k in range(2) for c in start_direct(orders[k][0], refs[k], base[k], n, unit)]
        for c in direct:
            c.wait()
        n, cut = sizes[1]
        states = [start(orders[k][1], refs[k], 0, n, cut, unit) for k in range(2)]
        seconds = [onward(state) for state in states]
        for state, second in zip(states, seconds):
            end(state, second)

    return both


def orth_factors(here, sides, sibling, over_z, over_z_next, copy, at, piece, got, halves, gram, gram_low, poly, factor_low, q_all, small_step):
    x, y, z, shard = here
    gather = make_gather(sides, copy)
    n = D // 16
    sib, par = shard + 1 - 2 * (shard % 2), (shard + 2) % 4
    ps = (sib + 2) % 4
    sums = [copy(piece.at[sib], got.at[0], sibling)]
    for k in range(2):
        sums.append(copy(piece.at[par, k], got.at[1, k], over_z[k]))
        sums.append(copy(piece.at[ps, k], got.at[2, k], over_z_next[k]))
    for c in sums:
        c.wait_recv()
    for k in range(2):
        halves[k, pl.ds(at[k], n), :] = piece[shard, k] + got[0, k] + got[1, k] + got[2, k]
    orders = (("y", "x"), ("x", "y"))
    base = (x * 4 * n, y * 4 * n)
    gather([halves.at[0], halves.at[1]], orders, base, ((n, 24), (4 * n, 2 * n)), 8)
    for c in sums:
        c.wait_send()

    tile = 256
    blocks = D // tile

    def eye(r, width, first):
        return (lax.broadcasted_iota(jnp.int32, (tile, width), 0) + r * tile == lax.broadcasted_iota(jnp.int32, (tile, width), 1) + first).astype(f32)

    trace = jnp.zeros((1, 1), f32)
    for r in range(blocks):
        for k in range(2):
            part = halves[k, r * tile : (r + 1) * tile, :] * eye(r, HALF, k * HALF)
            trace = trace + jnp.sum(jnp.sum(part, axis=1, keepdims=True), axis=0, keepdims=True)
    inv = 1.0 / (jnp.sqrt(trace) + 1e-07)
    for r in range(blocks):
        spot = slice(r * tile, (r + 1) * tile)
        for k in range(2):
            cols = slice(k * HALF, k * HALF + HALF)
            g = halves[k, spot, :] * (inv * inv)
            gram[spot, cols] = g
            gram_low[0][spot, cols] = g.astype(bf16)

    for k in range(4):
        small_step()
        now, later = k % 2, (k + 1) % 2

        def poly_rows(r):
            spot = slice(r * tile, (r + 1) * tile)
            poly[spot, :] = (poly_b * gram[spot, :] + poly_c * dot(gram_low[now][spot, :], gram_low[now][...])).astype(bf16)

        def update_rows(r):
            spot = slice(r * tile, (r + 1) * tile)
            p = poly[spot, :]
            if k == 0:
                q = p.astype(f32) + poly_a * eye(r, D, 0)
            else:
                q = poly_a * jnp.concatenate([halves[0, spot, :], halves[1, spot, :]], 1) + dot(p, factor_low[now][...])
            halves[0, spot, :] = q[:, :HALF]
            halves[1, spot, :] = q[:, HALF:]
            if k < 3:
                factor_low[later][spot, :] = q.astype(bf16)
                t = poly_a * gram[spot, :] + dot(p, gram_low[now][...])
                g = poly_a * t + dot(t.astype(bf16), poly[...])
                gram[spot, :] = g
                gram_low[later][spot, :] = g.astype(bf16)

        if k < 3:
            for r in range(blocks):
                poly_rows(r)
            for r in range(blocks):
                update_rows(r)
    top, low_part, every = pl.ds(0, HALF // 2), pl.ds(HALF // 2, HALF // 2), pl.ds(0, HALF)
    cross = []

    def send(way, block, spot):
        view = q_all.at[shard, block, spot, :]
        cross.append((copy(view, view, over_z[way]), block, spot))

    for r in range(2):
        poly_rows(r)
        update_rows(r)
    q_all[shard, 0] = (halves[0, 0:HALF, :] * inv).astype(bf16)
    q_all[shard, 1] = (halves[1, 0:HALF, :] * inv).astype(bf16)
    send(0, 1, top)
    send(1, 1, low_part)
    send(0, 0, every)
    poly_rows(2)
    update_rows(2)
    q_all[shard, 2] = (halves[1, HALF:D, :] * inv).astype(bf16)
    send(1, 2, every)
    near = copy(q_all.at[shard], q_all.at[shard], sibling)
    small_step()
    away = (shard + 2) % 4
    onward = []
    for c, block, spot in cross:
        c.wait_recv()
        view = q_all.at[away, block, spot, :]
        onward.append(copy(view, view, sibling))
    near.wait_recv()
    for c in onward:
        c.wait_recv()
    for c in (*[c for c, block, spot in cross], near, *onward):
        c.wait_send()


def block_kernel(
    x_ref, cot_ref, length_ref, order_ref, wq_hbm, wo_hbm, wf_hbm, wp_hbm, mq_hbm, mo_hbm, mf_hbm, mp_hbm, small_ref,
    out_ref, dx_ref, sums_one, sums_two, small_out, q_all, u_fc, momq, wo32, wf32, wp32, wf_held, wp_held,
    tokens, mixed, probs, bias, head_out, terms, got, passing, wq, wo, wf, wp,
    gact, act, gpre, gheads, gmixed, xhat1, xhat2, resid, gres, parts_one, parts_two, *rest,
):
    one_refs, two_refs = rest[:6], rest[6:12]
    small, qkv_bias, row_place, uq, piece, gram_got, halves, gram, poly = rest[12:21]
    small_got, send, recv, local = rest[21:]
    group = 4 * BLOCK
    nrm, mlow, nrm2, branch = (tokens.at[pl.ds(k * group, group), :] for k in range(4))
    part = [terms.at[pl.ds(k * group, group), :] for k in range(4)]
    gram_low, factor_low = ([ref.at[pl.ds(k * D, D), :] for k in range(2)] for ref in (tokens, terms))
    x, y, z, shard = place()
    sib = shard + 1 - 2 * (shard % 2)
    par = (shard + 2) % 4
    sibling, partner = device(x, y, z, sib), device(x, y, z, par)
    sides = {
        "x": (x, *[device((x + d) % 4, y, z, shard) for d in (3, 1, 2)]),
        "y": (y, *[device(x, (y + d) % 4, z, shard) for d in (3, 1, 2)]),
    }
    across = device(x, y, 1 - z, shard)
    far_sib = (sib + 2) % 4
    partners = (sibling, partner, device(x, y, z, far_sib), device(x, y, 1 - z, par), device(x, y, 1 - z, far_sib), *sides["x"][1:], *sides["y"][1:], across)
    barrier = pltpu.get_barrier_semaphore()
    for other in partners:
        pl.semaphore_signal(barrier, inc=1, device_id=other, device_id_type=MESH)
    loads = [pltpu.make_async_copy(src, dst, local.at[k]) for k, (src, dst) in enumerate(((wq_hbm, momq), (wo_hbm, wo32), (wf_hbm, wf32), (wp_hbm, wp32)))]
    for load in loads:
        load.start()

    rows = BLOCK

    def chunk(index, size=rows, at=0):
        return pl.ds(pl.multiple_of(index * rows + at, 16), size)

    own, own_sib, own_par, own_ps = chunk(shard), chunk(sib), chunk(par), chunk((sib + 2) % 4)
    near = pl.multiple_of((shard // 2) * 256, 256)
    far = pl.multiple_of(256 - near, 256)
    used = [0]

    free = list(range(SENDS))

    class Copy:
        def __init__(self, src, dst, target):
            self.slot = free.pop(0)
            self.copy = pltpu.make_async_remote_copy(
                src_ref=src, dst_ref=dst, send_sem=send.at[self.slot], recv_sem=recv.at[used[0]], device_id=target, device_id_type=MESH
            )
            used[0] += 1
            self.copy.start()

        def wait_recv(self):
            self.copy.wait_recv()

        def wait_send(self):
            self.copy.wait_send()
            free.append(self.slot)

        def wait(self):
            self.wait_recv()
            self.wait_send()

    copy = Copy
    sum_one = GroupSum(sides, across, copy, (x, y), 2 * D, parts_one, sums_one, *one_refs)
    sum_two = GroupSum(sides, across, copy, (x, y), D, parts_two, sums_two, *two_refs)
    steps = [
        sibling,
        partner,
        across,
        device(x + 1 - 2 * (x % 2), y, z, shard),
        device(3 - x, y, z, shard),
        device(x, y + 1 - 2 * (y % 2), z, shard),
        device(x, 3 - y, z, shard),
    ]
    small_copies = []

    def small_step():
        k = len(small_copies)
        if k > 0:
            small_copies[-1].wait()
            small_out[...] += small_got[k - 1]
        if k < len(steps):
            small_copies.append(copy(small_out, small_got.at[k], steps[k]))

    one_way, both_ways = (partner, partner), (partner, device(x, y, 1 - z, par))

    class Spread:
        def __init__(self, ref, ways):
            self.ref = ref
            self.cross = [self.to(shard, 64 * i, ways[i]) for i in range(2)]
            self.direct = copy(ref.at[own, :], ref.at[own, :], sibling)

        def to(self, index, at, target):
            spot = chunk(index, 64, at)
            return copy(self.ref.at[spot, :], self.ref.at[spot, :], target)

        def near(self):
            self.direct.wait_recv()

        def far(self):
            onward = []
            for i in range(2):
                self.cross[i].wait_recv()
                onward.append(self.to(par, 64 * i, sibling))
            for c in onward:
                c.wait_recv()
            for c in (*self.cross, self.direct, *onward):
                c.wait_send()

    class Fold:
        def __init__(self, k, ways):
            self.k, self.ways = k, ways

        def start_far(self):
            self.a = copy(part[self.k].at[own_ps, :], got.at[self.k, 0], sibling)

        def start_near(self):
            self.b = copy(part[self.k].at[own_sib, :], got.at[self.k, 1], sibling)

        def cross(self):
            self.a.wait_recv()
            passing[self.k] = (part[self.k][own_par, :].astype(f32) + got[self.k, 0].astype(f32)).astype(bf16)
            halves = (pl.ds(0, 64), pl.ds(64, 64))
            self.c = [copy(passing.at[self.k, spot, :], got.at[self.k, 2, spot, :], way) for spot, way in zip(halves, self.ways)]

        def end(self):
            self.b.wait_recv()
            for c in self.c:
                c.wait_recv()
            for c in (self.a, self.b, *self.c):
                c.wait_send()
            return part[self.k][own, :].astype(f32) + got[self.k, 1].astype(f32) + got[self.k, 2].astype(f32)

    def norm(v):
        centred = v - jnp.mean(v, axis=-1, keepdims=True)
        r = lax.rsqrt(jnp.mean(centred * centred, axis=-1, keepdims=True) + norm_eps)
        return centred * r, r

    def norm_grad(xhat, r, gain, c):
        cg = c * gain
        return r * (cg - jnp.mean(cg, -1, keepdims=True) - xhat * jnp.mean(cg * xhat, -1, keepdims=True))

    def total(v):
        return jnp.sum(v, axis=0, keepdims=True)

    nt, tn = ((1,), (1,)), ((0,), (0,))
    hc = wq.shape[0] // 3
    heads = hc // HD
    scale = HD ** -0.5

    small[...] = small_ref[...].astype(bf16).astype(f32)
    length = length_ref[0]

    def places(slot, axis):
        return lax.broadcasted_iota(jnp.int32, (rows, 1) if axis == 0 else (1, rows), axis) + order_ref[0, slot] * rows

    live = (places(shard, 0) < length).astype(f32)
    xf = x_ref[...].astype(f32)
    hat, r_one = norm(xf)
    xhat1[...] = hat
    nrm[own, :] = (hat * small[0:1, :] + small[1:2, :]).astype(bf16)
    mlow[own, :] = (cot_ref[...] * live).astype(bf16)
    pl.semaphore_wait(barrier, len(partners))
    go_nrm = Spread(nrm, one_way)
    go_mlow = Spread(mlow, both_ways)
    for slot in range(4):
        row_place[:, slot * rows : (slot + 1) * rows] = places(slot, 1)
    row = row_place[...]
    for slot in range(4):
        bias[slot * rows : (slot + 1) * rows, :] = jnp.where((row <= places(slot, 0)) & (row < length), 0.0, masked_score)
    for part_of, line in ((0, 4), (2, 5)):
        mine = jnp.zeros((1, hc), f32)
        for s in range(4):
            mine = jnp.where(shard == s, small[line : line + 1, s * hc : (s + 1) * hc], mine)
        qkv_bias[:, part_of * hc : (part_of + 1) * hc] = mine
    qkv_bias[:, hc : 2 * hc] = jnp.zeros((1, hc), f32)
    fc_bias = small[pl.ds(7 + shard, 1), :]
    loads[0].wait()
    wq[...] = momq[...].astype(bf16)
    loads[1].wait()
    wo[...] = wo32[...].astype(bf16)

    def mix(at):
        spot = pl.ds(at, 256)
        mixed[spot, :] = (dot(nrm[spot, :], wq[...], nt) + qkv_bias[...]).astype(bf16)

    go_nrm.near()
    mix(near)
    go_nrm.far()
    mix(far)

    def head(h, part_of):
        lo = part_of * hc + h * HD
        return slice(lo, lo + HD)

    for h in range(heads):

        def attend(i):
            spot = slice(i * 256, i * 256 + 256)
            s = dot(mixed[spot, head(h, 0)], mixed[:, head(h, 1)], nt) * scale + bias[spot, :]
            e = jnp.exp(s - jnp.max(s, axis=-1, keepdims=True))
            p = (e * (1.0 / jnp.sum(e, axis=-1, keepdims=True))).astype(bf16)
            probs[h, spot, :] = p
            head_out[spot, head(h, 0)] = dot(p, mixed[:, head(h, 2)]).astype(bf16)

        for i in range(2):
            attend(i)

    fold = Fold(0, one_way)
    part[0][pl.ds(far, 256), :] = dot(head_out[pl.ds(far, 256), :], wo[...]).astype(bf16)
    fold.start_far()
    part[0][pl.ds(near, 256), :] = dot(head_out[pl.ds(near, 256), :], wo[...]).astype(bf16)
    fold.start_near()
    fold.cross()
    go_mlow.near()
    go_mlow.far()
    loads[2].wait()
    wf[...] = wf32[...].astype(bf16)
    loads[3].wait()
    wp[...] = wp32[...].astype(bf16)

    mom_loads = [pltpu.make_async_copy(src, dst, local.at[4 + k]) for k, (src, dst) in enumerate(((mo_hbm, wo32), (mf_hbm, wf32), (mp_hbm, wp32), (mq_hbm, momq), (wf_hbm, wf_held), (wp_hbm, wp_held)))]
    for load in mom_loads:
        load.start()

    def activation_grad(i):
        spot = slice(i * 256, i * 256 + 256)
        gact[spot, :] = dot(mlow[spot, :], wp[...], nt)

    for i in range(2):
        activation_grad(i)
    res = x_ref[...].astype(f32) + fold.end() + small[6:7, :]
    resid[...] = res
    hat, r_two = norm(res)
    xhat2[...] = hat
    nrm2[own, :] = (hat * small[2:3, :] + small[3:4, :]).astype(bf16)
    go_nrm2 = Spread(nrm2, both_ways)

    def feed(at):
        spot = pl.ds(at, 256)
        hidden = dot(nrm2[spot, :], wf[...]) + fc_bias
        k = 0.7978845608028654
        square = hidden * hidden
        t = jnp.tanh(k * (hidden + 0.044715 * hidden * square))
        half = 0.5 * (1.0 + t)
        act[spot, :] = (hidden * half).astype(bf16)
        slope = half + 0.5 * hidden * (1.0 - t * t) * (k + (3 * 0.044715 * k) * square)
        gpre[spot, :] = (slope * gact[spot, :]).astype(bf16)

    go_nrm2.near()
    feed(near)
    go_nrm2.far()
    feed(far)
    fold = Fold(1, both_ways)
    part[1][pl.ds(far, 256), :] = dot(gpre[pl.ds(far, 256), :], wf[...], nt).astype(bf16)
    fold.start_far()
    part[1][pl.ds(near, 256), :] = dot(gpre[pl.ds(near, 256), :], wf[...], nt).astype(bf16)
    fold.start_near()
    fold.cross()

    def grad_columns(parts, base, left, right, width):
        for c in range(left.shape[1] // width):
            value = dot(left[:, c * width : (c + 1) * width], right[...], tn).astype(bf16)
            spot = pl.ds(base + c * width, width)
            parts[0, spot, :] = value[:, :HALF]
            parts[1, spot, :] = value[:, HALF:]

    grad_columns(parts_one, 0, nrm2, gpre, 256)
    grad_columns(parts_one, D, act, mlow, 256)
    sum_one.one_start()
    small_out[11:12, :] = total(mlow[own, :].astype(f32))
    c_two = fold.end()
    hat = xhat2[...]
    small_out[2:3, :] = total(c_two * hat)
    small_out[3:4, :] = total(c_two)
    g = cot_ref[...] * live + norm_grad(hat, r_two, small[2:3, :], c_two)
    gres[...] = g
    branch[own, :] = g.astype(bf16)
    go_branch = Spread(branch, one_way)
    sum_one.one_pass()
    small_out[6:7, :] = total(branch[own, :].astype(f32))
    pre_sum = total(gpre[...].astype(f32))
    small_out[7:11, :] = jnp.where(lax.broadcasted_iota(jnp.int32, (4, D), 0) == shard, pre_sum, 0.0)

    def head_grads(at):
        spot = pl.ds(at, 256)
        gheads[spot, :] = dot(branch[spot, :], wo[...], nt).astype(bf16)

    fold_out = Fold(2, both_ways)
    part[2][pl.ds(far, 256), :] = dot(act[pl.ds(far, 256), :], wp[...]).astype(bf16)
    fold_out.start_far()
    part[2][pl.ds(near, 256), :] = dot(act[pl.ds(near, 256), :], wp[...]).astype(bf16)
    fold_out.start_near()
    go_branch.near()
    head_grads(near)
    go_branch.far()
    head_grads(far)
    fold_out.cross()
    sum_one.two_start()
    for h in range(heads):
        q, k, v = (mixed[:, head(h, i)] for i in range(3))
        gh = gheads[:, head(h, 0)]
        gmixed[:, head(h, 2)] = dot(gh, probs[h], tn).T.astype(bf16)

        def scores_grad(i):
            spot = slice(i * 256, i * 256 + 256)
            p = probs[h, spot, :].astype(f32)
            gp = dot(gheads[spot, head(h, 0)], mixed[:, head(h, 2)], nt)
            gs = (p * (gp - jnp.sum(p * gp, axis=-1, keepdims=True))).astype(bf16)
            probs[h, spot, :] = gs
            gmixed[spot, head(h, 0)] = (dot(gs, mixed[:, head(h, 1)]) * scale).astype(bf16)

        for i in range(2):
            scores_grad(i)
        gmixed[:, head(h, 1)] = (dot(q, probs[h], tn).T * scale).astype(bf16)

    grad_columns(parts_two, 0, head_out, branch, hc)
    grad_columns(parts_two, hc, gmixed, nrm, hc)
    sum_two.one_start()
    sum_one.z_start()
    fold = Fold(3, one_way)
    part[3][pl.ds(far, 256), :] = dot(gmixed[pl.ds(far, 256), :], wq[...]).astype(bf16)
    fold.start_far()
    part[3][pl.ds(near, 256), :] = dot(gmixed[pl.ds(near, 256), :], wq[...]).astype(bf16)
    fold.start_near()
    fold.cross()
    mixed_sum = total(gmixed[...].astype(f32))
    spread_out = (lax.broadcasted_iota(jnp.int32, (hc, D), 0) + shard * hc == lax.broadcasted_iota(jnp.int32, (hc, D), 1)).astype(f32)
    for row, lo in ((4, 0), (5, 2 * hc)):
        small_out[row : row + 1, :] = jnp.dot(mixed_sum[:, lo : lo + hc], spread_out, precision=lax.Precision.HIGHEST, preferred_element_type=f32)
    out_ref[...] = ((resid[...] + fold_out.end() + small[11:12, :]) * live).astype(bf16)
    sum_two.one_pass()
    sum_one.back_start()
    sum_two.two_start()
    c_one = fold.end()
    hat = xhat1[...]
    small_out[0:1, :] = total(c_one * hat)
    small_out[1:2, :] = total(c_one)
    small_step()
    dx_ref[...] = gres[...] + norm_grad(hat, r_one, small[0:1, :], c_one)
    sum_one.last_start()
    small_step()
    sum_two.z_start()
    sum_one.last_pass()
    sum_two.back_start()
    small_step()

    def update(u, base, mom, sums):
        count = u.shape[0]
        for k in range(2):
            cols = slice(k * HALF, k * HALF + HALF)
            g = sums[k, base : base + count, :].astype(f32)
            u[:, cols] = (g + momentum_decay * (momentum_decay * mom[:, cols] + g)).astype(bf16)

    n = D // 16
    at = (pl.multiple_of((x * 4 + y) * n, 16), pl.multiple_of((y * 4 + x) * n, 16))

    def gram_rows(m, u, whole):
        for k in range(2):
            cols = slice(k * HALF, k * HALF + HALF)
            if whole:
                piece[m, k] = dot(u[pl.ds(at[k], n), :], u[cols, :], nt)
            else:
                pick = (lax.broadcasted_iota(jnp.int32, (D, n), 0) == lax.broadcasted_iota(jnp.int32, (D, n), 1) + at[k]).astype(f32).astype(bf16)
                piece[m, k] = dot(dot(u[...], pick).astype(bf16), u[:, cols], tn)

    sum_two.last_start()
    sum_one.last_end()
    for load in mom_loads:
        load.wait()
    update(u_fc, 0, wf32, sums_one)
    update(wp, D, wp32, sums_one)
    gram_rows(2, u_fc, True)
    gram_rows(3, wp, False)
    sum_two.last_pass()
    sum_two.last_end()
    update(wo, 0, wo32, sums_two)
    update(uq, hc, momq, sums_two)
    gram_rows(1, wo, False)
    gram_rows(0, uq, False)
    over_z = [partner, device(x, y, 1 - z, par)]
    over_z_next = [device(x, y, z, (sib + 2) % 4), device(x, y, 1 - z, (sib + 2) % 4)]
    orth_factors(place(), sides, sibling, over_z, over_z_next, copy, at, piece, gram_got, halves, gram, gram_low, poly, factor_low, q_all, small_step)
    assert used[0] <= RECVS and len(free) == SENDS


def run_block(x_own, cot, lengths, order, wq, wo, wf, wp, mq, mo, mf, mp, small):
    vm = pl.BlockSpec(memory_space=pltpu.VMEM)
    sm = pl.BlockSpec(memory_space=pltpu.SMEM)
    hbm = pl.BlockSpec(memory_space=pl.ANY)
    rows, wide = x_own.shape[0], wq.shape[0]
    hc = wide // 3
    group = 4 * rows
    vmem = pltpu.VMEM
    return pl.pallas_call(
        block_kernel,
        out_shape=(
            pltpu.VMEM((rows, D), bf16),
            pltpu.VMEM((rows, D), f32),
            pltpu.VMEM((2, 2 * D, HALF), bf16),
            pltpu.VMEM((2, D, HALF), bf16),
            pltpu.VMEM((12, D), f32),
            pltpu.VMEM((4, 3, HALF, HALF), bf16),
            pltpu.VMEM((D, D), bf16),
            *[pltpu.VMEM(w.shape, f32) for w in (wq, wo, wf, wp, wf, wp)],
        ),
        in_specs=[vm, vm, sm, sm] + [hbm] * 8 + [vm],
        out_specs=(vm,) * 13,
        scratch_shapes=[
            vmem((4 * group, D), bf16),
            vmem((group, wide), bf16),
            vmem((hc // HD, group, group), bf16),
            vmem((group, group), f32),
            vmem((group, hc), bf16),
            vmem((4 * group, D), bf16),
            vmem((4, 3, rows, D), bf16),
            vmem((4, rows, D), bf16),
            vmem(wq.shape, bf16),
            vmem(wo.shape, bf16),
            vmem(wf.shape, bf16),
            vmem(wp.shape, bf16),
            vmem((group, D), f32),
            vmem((group, D), bf16),
            vmem((group, D), bf16),
            vmem((group, hc), bf16),
            vmem((group, wide), bf16),
            vmem((rows, D), f32),
            vmem((rows, D), f32),
            vmem((rows, D), f32),
            vmem((rows, D), f32),
            vmem((2, 2 * D, HALF), bf16),
            vmem((2, D, HALF), bf16),
            *sum_scratch(2 * D),
            *sum_scratch(D),
            vmem((12, D), f32),
            vmem((1, wide), f32),
            vmem((1, group), jnp.int32),
            vmem((wide, D), bf16),
            vmem((4, 2, D // 16, HALF), f32),
            vmem((3, 2, D // 16, HALF), f32),
            vmem((2, D, HALF), f32),
            vmem((D, D), f32),
            vmem((D, D), bf16),
            vmem((7, 12, D), f32),
            pltpu.SemaphoreType.DMA((SENDS,)),
            pltpu.SemaphoreType.DMA((RECVS,)),
            pltpu.SemaphoreType.DMA((10,)),
        ],
        compiler_params=pltpu.CompilerParams(collective_id=1, has_side_effects=True, vmem_limit_bytes=40 * 1024 * 1024),
    )(x_own, cot, lengths, order, wq, wo, wf, wp, mq, mo, mf, mp, small)


def finish_kernel(
    sums_one, sums_two, q_all, u_fc, mq, mo, mf, mp, wf, wp, out_in, dx_in, small_sum, small_params, small_first, small_second,
    wq, wo,
    out_ref, dx_ref, gq, go, gf, gp, nq, no, nf, np_, rq, ro, rf, rp, small_grad, first_ref, second_ref, small_new, last_bias,
):
    i = pl.program_id(0)
    nt, tn = ((1,), (1,)), ((0,), (0,))

    @pl.when(i == 0)
    def _():
        out_ref[...] = out_in[...]
        dx_ref[...] = dx_in[...]
        g = small_sum[...]
        small_grad[...] = g
        last_bias[...] = g[11:12, :]
        first = beta_one * small_first[...] + (1.0 - beta_one) * g
        second = beta_two * small_second[...] + (1.0 - beta_two) * g * g
        first_ref[...] = first
        second_ref[...] = second
        first_hat = first / (1.0 - beta_one**STEP)
        second_hat = second / (1.0 - beta_two**STEP)
        small_new[...] = small_params[...] - adam_rate * first_hat / (jnp.sqrt(second_hat) + adam_eps)

    def renew(owner, sums, base, w, m, g_out, w_out, m_out, longest, rate):
        count = g_out.shape[0]
        keep_rate, step_rate = 1.0 - rate * muon_decay, rate * 0.2 * math.sqrt(longest)
        spot = pl.ds(pl.multiple_of(base + i * count, 16), count)
        mine = pl.ds(pl.multiple_of(i * count, 16), count)
        held = mine if w.shape[0] > count else pl.ds(0, count)
        low = []
        for k in range(2):
            cols = slice(k * HALF, k * HALF + HALF)
            g = sums[k, spot, :].astype(f32)
            moved = momentum_decay * m[mine, cols] + g
            g_out[:, cols] = g
            m_out[:, cols] = moved
            low.append((g + momentum_decay * moved).astype(bf16))
        q11, q12, q22 = q_all[owner, 0], q_all[owner, 1], q_all[owner, 2]
        w_out[:, :HALF] = keep_rate * w[held, :HALF] - step_rate * (dot(low[0], q11) + dot(low[1], q12, nt))
        w_out[:, HALF:] = keep_rate * w[held, HALF:] - step_rate * (dot(low[0], q12) + dot(low[1], q22))

    renew(0, sums_two, 192, wq, mq, gq, nq, rq, 3 * D, muon_rate)
    renew(1, sums_two, 0, wo, mo, go, no, ro, D, out_rate)
    renew(3, sums_one, D, wp, mp, gp, np_, rp, FF, muon_rate)
    count = gf.shape[0]
    keep_rate, step_rate = 1.0 - muon_rate * muon_decay, muon_rate * 0.2 * math.sqrt(FF)
    spot = pl.ds(pl.multiple_of(i * count, 16), count)
    for k in range(2):
        cols = slice(k * HALF, k * HALF + HALF)
        g = sums_one[k, spot, :].astype(f32)
        gf[:, cols] = g
        rf[:, cols] = momentum_decay * mf[spot, cols] + g
    half_steps = HALF // count

    @pl.when(i < half_steps)
    def _():
        at = pl.ds(pl.multiple_of(i * count, count), count)
        nf[...] = keep_rate * wf[spot, :] - step_rate * (dot(q_all[2, 0, at, :], u_fc[:HALF, :]) + dot(q_all[2, 1, at, :], u_fc[HALF:, :]))

    @pl.when(i >= half_steps)
    def _():
        at = pl.ds(pl.multiple_of((i - half_steps) * count, count), count)
        nf[...] = keep_rate * wf[spot, :] - step_rate * (dot(q_all[2, 1, :, at], u_fc[:HALF, :], tn) + dot(q_all[2, 2, at, :], u_fc[HALF:, :]))


def finish(kept, small, weights):
    steps = 6
    vm = pl.BlockSpec(memory_space=pltpu.VMEM)

    def tiles(a):
        return pl.BlockSpec((a.shape[0] // steps, a.shape[1]), lambda i: (i, 0))

    def whole(shape):
        return pl.BlockSpec(shape, lambda i: (0, 0))

    like = [jax.ShapeDtypeStruct(w.shape, f32) for w in weights]
    flat = jax.ShapeDtypeStruct((12, D), f32)
    last = jax.ShapeDtypeStruct((1, D), f32)
    block_out, dx = kept[10], kept[11]
    own = [jax.ShapeDtypeStruct(block_out.shape, bf16), jax.ShapeDtypeStruct(dx.shape, f32)]
    return pl.pallas_call(
        finish_kernel,
        grid=(steps,),
        out_shape=(*own, *like, *like, *like, flat, flat, flat, flat, last),
        in_specs=[vm] * 16 + [tiles(w) for w in weights[:2]],
        out_specs=(whole(block_out.shape), whole(dx.shape), *([tiles(w) for w in weights] * 3), *([whole((12, D))] * 4), whole((1, D))),
        compiler_params=pltpu.CompilerParams(vmem_limit_bytes=24 * 1024 * 1024),
    )(*kept, *small, *weights[:2])


def shards(block_input, cotangent, lengths, block_order, w_qkv, w_out, w_fc, w_proj, mom_qkv, mom_out, mom_fc, mom_proj, small_params, small_first, small_second):
    cube = w_qkv.shape

    def turned(a):
        return a.transpose(1, 2, 0).reshape(-1, D)

    def back(a):
        return a.reshape(cube[1], cube[2], D).transpose(2, 0, 1)

    weights = (turned(w_qkv), w_out, w_fc, w_proj)
    moms = (turned(mom_qkv), mom_out, mom_fc, mom_proj)
    block_output, input_grad, sums_one, sums_two, small_sum, factors, u_fc, *held = run_block(block_input, cotangent, lengths, block_order, *weights, *moms, small_params)
    kept = [sums_one, sums_two, factors, u_fc, *held, block_output, input_grad, small_sum]
    kept = [pltpu.with_memory_space_constraint(a, pltpu.VMEM) for a in kept]
    weights = [pltpu.with_memory_space_constraint(a, pltpu.HBM) for a in weights]
    block_output, input_grad, gq, go, gf, gp, nq, no, nf, np_, rq, ro, rf, rp, grad_small, first, second, new_small, last = finish(
        kept, (small_params, small_first, small_second), weights
    )
    return (
        block_output, input_grad, back(gq), go, gf, gp, grad_small, back(nq), no, nf, np_, back(rq), ro, rf, rp, first, second, new_small, last.reshape(D),
    )


def solution(mesh):
    rows = P(("rep", "shard"), None)
    mats = (P(None, None, "shard"), P("shard", None), P(None, "shard"), P("shard", None))
    in_specs = (rows, rows, P("rep"), P("rep", None), *mats, *mats, P(), P(), P())
    out_specs = (rows, rows, *mats, P(), *mats, *mats, P(), P(), P(), P())
    return jax.shard_map(shards, mesh=mesh, in_specs=in_specs, out_specs=out_specs, check_vma=False)
```
